32 devices in a mesh: dp: 8 (over y, x, core), seq: 4 (over z).
Axes of the slice: x: 2, y: 2, z: 4, core: 2. Of those that a mesh axis runs over, the one named last changes fastest.
Arguments:
- tokens: bfloat16 [32, 1024, 512], P('dp', 'seq'), may hold values from -6 to 6
- memory: bfloat16 [32, 256, 512], P('dp', 'seq'), may hold values from -6 to 6
- doc_lengths: int32 [32, 32], P('dp'), may hold values from 0 to 1024, as said below
- src_lengths: int32 [32, 32], P('dp'), may hold values from 1 to 225, as said below
- cotangent: bfloat16 [32, 1024, 512], P('dp', 'seq'), may hold values from -6 to 6
- w_qkv: bfloat16 [512, 1536], replicated, may hold values from -0.25 to 0.25
- qv_bias: bfloat16 [1024], replicated, may hold values from -1.75 to 1.75
- self_out: bfloat16 [512, 512], replicated, may hold values from -0.75 to 0.75
- self_out_bias: bfloat16 [512], replicated, may hold values from -1.75 to 1.75
- cross_query: bfloat16 [512, 512], replicated, may hold values from -0.25 to 0.25
- cross_q_bias: bfloat16 [512], replicated, may hold values from -1.75 to 1.75
- cross_kv: bfloat16 [512, 1024], replicated, may hold values from -0.25 to 0.25
- cross_v_bias: bfloat16 [512], replicated, may hold values from -1.75 to 1.75
- cross_out: bfloat16 [512, 512], replicated, may hold values from -0.75 to 0.75
- cross_out_bias: bfloat16 [512], replicated, may hold values from -1.75 to 1.75
- ffn_in: bfloat16 [512, 2048], replicated, may hold values from -0.25 to 0.25
- ffn_in_bias: bfloat16 [2048], replicated, may hold values from -1.75 to 1.75
- ffn_out: bfloat16 [2048, 512], replicated, may hold values from -0.1875 to 0.1875
- ffn_out_bias: bfloat16 [512], replicated, may hold values from -1.75 to 1.75
- norm_gains: bfloat16 [3, 512], replicated, may hold values from 0.5 to 1.5
- norm_biases: bfloat16 [3, 512], replicated, may hold values from -1.75 to 1.75
Outputs:
- output: bfloat16 [32, 1024, 512], P('dp', 'seq')
- d_tokens: float32 [32, 1024, 512], P('dp', 'seq')
- d_memory: float32 [32, 256, 512], P('dp', 'seq')
- d_w_qkv: float32 [512, 1536], replicated
- d_qv_bias: float32 [1024], replicated
- d_self_out: float32 [512, 512], replicated
- d_self_out_bias: float32 [512], replicated
- d_cross_query: float32 [512, 512], replicated
- d_cross_q_bias: float32 [512], replicated
- d_cross_kv: float32 [512, 1024], replicated
- d_cross_v_bias: float32 [512], replicated
- d_cross_out: float32 [512, 512], replicated
- d_cross_out_bias: float32 [512], replicated
- d_ffn_in: float32 [512, 2048], replicated
- d_ffn_in_bias: float32 [2048], replicated
- d_ffn_out: float32 [2048, 512], replicated
- d_ffn_out_bias: float32 [512], replicated
- d_norm_gains: float32 [3, 512], replicated
- d_norm_biases: float32 [3, 512], replicated
The draws below stay inside these ranges and needn't reach their ends.
Inputs may be any that keep to these rules, and one draw needn't show every extreme that they name: `doc_lengths`: the 32 lengths of a row sum to at most 1024; positions after their sum are padding. Document j of a target row belongs with document j of its source row. `src_lengths`: the 32 lengths of a row sum to 256.
All inputs are finite; a program needn't handle non-finite values.
Results may differ from the reference program's by a relative error of at most 0.018.
Values may be sent and summed in bfloat16 or wider, within the bound.
A program may use at most 256 MiB of HBM per device.

```python
import jax
import jax.numpy as jnp
from jax import lax

D = 512
HEADS = 8
HEAD = 64
FF = 2048
BLK = 256
ROWS_DEV = 4
NDOC = 32
ROW_LEN = 1024
SRC_LEN = 256
ROWS = 32


def draw_doc_lengths(key, part):
    key = jax.random.fold_in(key, 17)
    pad_key, cut_key, pick_key = jax.random.split(key, 3)
    padding = jax.random.randint(pad_key, (ROWS,), 0, BLK // 2)
    live_count = ROW_LEN - padding
    raw_draw = jax.random.randint(cut_key, (ROWS, NDOC - 1), 0, 256)
    cut_points = jnp.sort(raw_draw * raw_draw * live_count[:, None] // 65536, axis=1)
    bounds = jnp.concatenate([jnp.zeros((ROWS, 1), jnp.int32), cut_points, live_count[:, None]], axis=1)
    lengths = bounds[:, 1:] - bounds[:, :-1]
    group_count = ROWS // ROWS_DEV
    picks = jax.random.randint(pick_key, (group_count,), 0, ROWS_DEV)
    row_numbers = jnp.arange(ROWS, dtype=jnp.int32)
    chosen = row_numbers % ROWS_DEV == picks[row_numbers // ROWS_DEV]
    single_doc = jnp.zeros((ROWS, NDOC), jnp.int32).at[:, 0].set(ROW_LEN)
    return jnp.where(chosen[:, None], single_doc, lengths).astype(jnp.int32)


def draw_src_lengths(key, part):
    key = jax.random.fold_in(key, 29)
    raw_draw = jax.random.randint(key, (ROWS, NDOC - 1), 0, 256)
    spare_room = SRC_LEN - NDOC
    cut_points = jnp.sort(raw_draw * raw_draw * spare_room // 65536, axis=1)
    bounds = jnp.concatenate([jnp.zeros((ROWS, 1), jnp.int32), cut_points, jnp.full((ROWS, 1), spare_room, jnp.int32)], axis=1)
    lengths = bounds[:, 1:] - bounds[:, :-1] + 1
    longest = jnp.ones((NDOC,), jnp.int32).at[0].set(spare_room + 1)
    lengths = lengths.at[0].set(longest)
    return lengths.astype(jnp.int32)


def steps_of(own_key, extent, cuts, smallest, largest):
    level, own = 1.0, jax.random.fold_in(own_key, 6)
    for position, blocks in cuts:
        heights = jnp.exp(jax.random.uniform(jax.random.fold_in(own, position), (blocks,), jnp.float32, smallest / len(cuts), largest / len(cuts)))
        level = level * jnp.repeat(heights, extent[position] // blocks).reshape([-1 if axis == position else 1 for axis in range(len(extent))])
    return level


def scatter_about(own_key, dims, deviation, most, cuts=(), kind=jnp.bfloat16):
    entries = deviation * jax.random.normal(own_key, dims, jnp.float32)
    if cuts:
        entries = entries * steps_of(own_key, dims, cuts, -0.22, 0.18)
    return jnp.clip(entries, -most, most).astype(kind)


def setup_inputs(seed: int = 0) -> dict:
    seeds = jax.random.split(jax.random.key(seed), 22)
    tokens = scatter_about(seeds[0], (ROWS, ROW_LEN, D), 1.0, 6.0, ((0, 8), (1, 4)))
    memory = scatter_about(seeds[1], (ROWS, SRC_LEN, D), 1.0, 6.0, ((0, 8), (1, 4)))
    doc_lengths = draw_doc_lengths(jax.random.fold_in(seeds[21], 71), 0)
    src_lengths = draw_src_lengths(jax.random.fold_in(seeds[21], 71), 0)
    cotangent = scatter_about(seeds[4], (ROWS, ROW_LEN, D), 1.0, 6.0, ((0, 8), (1, 4)))
    w_qkv = scatter_about(seeds[5], (D, 3 * D), D ** -0.5, 0.25)
    qv_bias = scatter_about(seeds[6], (2 * D,), 0.3, 1.75)
    self_out = scatter_about(seeds[7], (D, D), HEAD ** -0.5, 0.75)
    self_out_bias = scatter_about(seeds[8], (D,), 0.3, 1.75)
    cross_query = scatter_about(seeds[9], (D, D), D ** -0.5, 0.25)
    cross_q_bias = scatter_about(seeds[10], (D,), 0.3, 1.75)
    cross_kv = scatter_about(seeds[11], (D, 2 * D), D ** -0.5, 0.25)
    cross_v_bias = scatter_about(seeds[12], (D,), 0.3, 1.75)
    cross_out = scatter_about(seeds[13], (D, D), HEAD ** -0.5, 0.75)
    cross_out_bias = scatter_about(seeds[14], (D,), 0.3, 1.75)
    ffn_in = scatter_about(seeds[15], (D, FF), D ** -0.5, 0.25)
    ffn_in_bias = scatter_about(seeds[16], (FF,), 0.3, 1.75)
    ffn_out = scatter_about(seeds[17], (FF, D), (FF // 2) ** -0.5, 0.1875)
    ffn_out_bias = scatter_about(seeds[18], (D,), 0.3, 1.75)
    norm_gains = jnp.clip(1.0 + 0.1 * jax.random.normal(seeds[19], (3, D), jnp.float32), 0.5, 1.5).astype(jnp.bfloat16)
    norm_biases = scatter_about(seeds[20], (3, D), 0.3, 1.75)
    return {"tokens": tokens, "memory": memory, "doc_lengths": doc_lengths, "src_lengths": src_lengths, "cotangent": cotangent, "w_qkv": w_qkv, "qv_bias": qv_bias, "self_out": self_out, "self_out_bias": self_out_bias, "cross_query": cross_query, "cross_q_bias": cross_q_bias, "cross_kv": cross_kv, "cross_v_bias": cross_v_bias, "cross_out": cross_out, "cross_out_bias": cross_out_bias, "ffn_in": ffn_in, "ffn_in_bias": ffn_in_bias, "ffn_out": ffn_out, "ffn_out_bias": ffn_out_bias, "norm_gains": norm_gains, "norm_biases": norm_biases}


@jax.custom_vjp
def low(v):
    return lax.optimization_barrier(v.astype(jnp.bfloat16)).astype(jnp.float32)

@jax.custom_vjp
def low_back(v):
    return v

def low_keep(v):
    return (low(v), None)

def low_pass(kept, grad):
    return (grad,)

def back_keep(v):
    return (v, None)

def back_low(kept, grad):
    return (low(grad),)
low.defvjp(low_keep, low_pass)
low_back.defvjp(back_keep, back_low)

def round_both(values):
    return low(low_back(values))

def matmul_high(left, right):
    return jnp.dot(left, right, precision=lax.Precision.HIGHEST)

def layer_norm(values, gain, shift):
    center = values - lax.optimization_barrier(jnp.mean(values, axis=-1, keepdims=True))
    spread = lax.optimization_barrier(jnp.mean(center * center, axis=-1, keepdims=True))
    return center * lax.rsqrt(spread + 1e-05) * gain + shift

def doc_ids(lengths, size):
    ends = jnp.cumsum(lengths)
    places = jnp.arange(size, dtype=jnp.int32)
    return lax.optimization_barrier(jnp.sum((ends[None, :] <= places[:, None]).astype(jnp.int32), axis=1))

def attend(queries, keys, values, query_ids, key_ids, causal):
    query_count = queries.shape[0]
    key_count = keys.shape[0]
    block_len = 512 if query_count % 512 == 0 else query_count
    block_count = query_count // block_len
    score_scale = HEAD ** (-0.5)
    key_heads = keys.reshape(key_count, HEADS, HEAD)
    value_heads = values.reshape(key_count, HEADS, HEAD)
    key_places = jnp.arange(key_count, dtype=jnp.int32)
    query_blocks = queries.reshape(block_count, block_len, HEADS, HEAD)
    id_blocks = query_ids.reshape(block_count, block_len)
    place_blocks = jnp.arange(query_count, dtype=jnp.int32).reshape(block_count, block_len)

    def one_block(operands):
        query_blk, ids_blk, places_blk = operands
        scores = low_back(jnp.einsum('qhd,khd->hqk', query_blk, key_heads, precision=lax.Precision.HIGHEST) * score_scale)
        if causal:
            allowed = (ids_blk[:, None] == key_ids[None, :]) & (key_places[None, :] <= places_blk[:, None])
        else:
            allowed = (ids_blk[:, None] == key_ids[None, :]) | (ids_blk[:, None] == NDOC)
        scores = jnp.where(allowed[None], scores, -1000000000.0)
        probs = jax.nn.softmax(scores, axis=-1)
        mixed = jnp.einsum('hqk,khd->qhd', low(probs), value_heads, precision=lax.Precision.HIGHEST)
        return mixed.reshape(block_len, HEADS * HEAD)
    blocks_out = lax.map(jax.checkpoint(one_block), (query_blocks, id_blocks, place_blocks))
    return blocks_out.reshape(query_count, HEADS * HEAD)

def decoder_layer(inputs_f, memory_f, target_ids, source_ids, params):
    w_qkv, qv_bias, self_out, self_out_bias, cross_query, cross_q_bias, cross_kv, cross_v_bias, cross_out, cross_out_bias, ffn_in, ffn_in_bias, ffn_out, ffn_out_bias, norm_gains, norm_biases = params
    packed = matmul_high(inputs_f, w_qkv)
    queries = round_both(packed[:, :D] + qv_bias[:D])
    keys = round_both(packed[:, D:2 * D])
    values = round_both(packed[:, 2 * D:] + qv_bias[D:])
    context = round_both(attend(queries, keys, values, target_ids, target_ids, True))
    first_sum = inputs_f + low_back(matmul_high(context, self_out) + self_out_bias)
    first_norm = layer_norm(first_sum, norm_gains[0], norm_biases[0])
    cross_queries = round_both(matmul_high(low(first_norm), cross_query) + cross_q_bias)
    memory_pair = matmul_high(memory_f, cross_kv)
    cross_keys = round_both(memory_pair[:, :D])
    cross_values = round_both(memory_pair[:, D:] + cross_v_bias)
    cross_context = round_both(attend(cross_queries, cross_keys, cross_values, target_ids, source_ids, False))
    second_sum = first_norm + low_back(matmul_high(cross_context, cross_out) + cross_out_bias)
    second_norm = layer_norm(second_sum, norm_gains[1], norm_biases[1])
    hidden_pre = low_back(matmul_high(low(second_norm), ffn_in) + ffn_in_bias)
    branch_out = low_back(matmul_high(low(jax.nn.silu(hidden_pre)), ffn_out) + ffn_out_bias)
    return layer_norm(second_norm + branch_out, norm_gains[2], norm_biases[2])

def reference(tokens, memory, doc_lengths, src_lengths, cotangent, w_qkv, qv_bias, self_out, self_out_bias, cross_query, cross_q_bias, cross_kv, cross_v_bias, cross_out, cross_out_bias, ffn_in, ffn_in_bias, ffn_out, ffn_out_bias, norm_gains, norm_biases):
    params = tuple((weight.astype(jnp.float32) for weight in (w_qkv, qv_bias, self_out, self_out_bias, cross_query, cross_q_bias, cross_kv, cross_v_bias, cross_out, cross_out_bias, ffn_in, ffn_in_bias, ffn_out, ffn_out_bias, norm_gains, norm_biases)))

    def one_row(totals, operands):
        row_in, row_memory, row_cot, row_lengths, row_src = operands
        target_ids = doc_ids(row_lengths, ROW_LEN)
        source_ids = doc_ids(row_src, SRC_LEN)

        def forward(inputs_f, memory_f, weights):
            return decoder_layer(inputs_f, memory_f, target_ids, source_ids, weights)
        result, pull = jax.vjp(forward, row_in.astype(jnp.float32), row_memory.astype(jnp.float32), params)
        grad_in, grad_memory, grad_weights = pull(row_cot.astype(jnp.float32))
        totals = jax.tree.map(lambda summed, addend: summed + addend, totals, grad_weights)
        return (totals, (result.astype(jnp.bfloat16), grad_in, grad_memory))
    start_totals = jax.tree.map(jnp.zeros_like, params)
    totals, (output, d_tokens, d_memory) = lax.scan(one_row, start_totals, (tokens, memory, cotangent, doc_lengths, src_lengths))
    d_w_qkv, d_qv_bias, d_self_out, d_self_out_bias, d_cross_query, d_cross_q_bias, d_cross_kv, d_cross_v_bias, d_cross_out, d_cross_out_bias, d_ffn_in, d_ffn_in_bias, d_ffn_out, d_ffn_out_bias, d_norm_gains, d_norm_biases = totals
    return (output, d_tokens, d_memory, d_w_qkv, d_qv_bias, d_self_out, d_self_out_bias, d_cross_query, d_cross_q_bias, d_cross_kv, d_cross_v_bias, d_cross_out, d_cross_out_bias, d_ffn_in, d_ffn_in_bias, d_ffn_out, d_ffn_out_bias, d_norm_gains, d_norm_biases)
```

```python
import functools
import jax
import jax.numpy as jnp
from jax import lax
from jax.experimental import pallas as pl
from jax.experimental.pallas import tpu as pltpu
from jax.sharding import PartitionSpec as P

HEADS = 8
HEAD = 64
NDOC = 32
AUG = HEAD + 16
MASKED = -1e9
LOG2E = 1.4426950408889634
SCALE = HEAD**-0.5
F32 = jnp.float32
BF16 = jnp.bfloat16
TB = 256

V_Q, V_V, V_SO, V_CQ, V_CV, V_CO, V_FI, V_FO, V_G, V_B = 0, 1, 2, 3, 4, 5, 6, 10, 11, 14
VECS = 24


def mm(left, right, lc=1, rc=0):
    return lax.dot_general(
        left, right, (((lc,), (rc,)), ((), ())), preferred_element_type=F32
    )


def row_ids(lengths, row, size):
    rows, docs = lengths.shape
    at_row = lax.broadcasted_iota(jnp.int32, (rows, docs), 0) == row
    own = jnp.sum(jnp.where(at_row, lengths.astype(F32), 0.0), axis=0, keepdims=True)
    own = jnp.broadcast_to(own, (docs, docs))
    down = lax.broadcasted_iota(jnp.int32, (docs, docs), 0)
    over = lax.broadcasted_iota(jnp.int32, (docs, docs), 1)
    ends_col = jnp.sum(jnp.where(over <= down, own, 0.0), axis=1, keepdims=True)
    own_col = jnp.sum(jnp.where(over == down, own, 0.0), axis=1, keepdims=True)
    ends_row = jnp.sum(
        jnp.where(down <= over, jnp.broadcast_to(own_col, (docs, docs)), 0.0),
        axis=0,
        keepdims=True,
    )
    place_row = lax.broadcasted_iota(jnp.int32, (docs, size), 1).astype(F32)
    place_col = lax.broadcasted_iota(jnp.int32, (size, docs), 0).astype(F32)
    ids_row = jnp.sum(jnp.where(ends_col <= place_row, 1.0, 0.0), axis=0, keepdims=True)
    ids_col = jnp.sum(jnp.where(ends_row <= place_col, 1.0, 0.0), axis=1, keepdims=True)
    return ids_row, ids_col


def self_mask(mask_ref, lengths, row, size):
    ids_row, ids_col = row_ids(lengths, row, size)
    for kb in range(size // TB):
        for qb in range(kb, size // TB):
            ks, qs = slice(kb * TB, (kb + 1) * TB), slice(qb * TB, (qb + 1) * TB)
            seen = ids_col[ks] == ids_row[:, qs]
            if kb == qb:
                down = lax.broadcasted_iota(jnp.int32, (TB, TB), 0)
                over = lax.broadcasted_iota(jnp.int32, (TB, TB), 1)
                seen = seen & (down <= over)
            mask_ref[ks, qs] = jnp.where(seen, 0.0, MASKED)


def cross_mask(mask_ref, lengths, src_lengths, row, size, src):
    ids_row, _ = row_ids(lengths, row, size)
    _, src_col = row_ids(src_lengths, row, src)
    for qb in range(size // TB):
        qs = slice(qb * TB, (qb + 1) * TB)
        seen = (src_col == ids_row[:, qs]) | (ids_row[:, qs] == float(NDOC))
        mask_ref[:, qs] = jnp.where(seen, 0.0, MASKED)


def half_of(values, half):
    down = lax.broadcasted_iota(jnp.int32, values.shape, 0)
    keep = (down >= HEAD) if half else (down < HEAD)
    return jnp.where(keep, values, jnp.zeros_like(values))


def normalize(h):
    center = h - jnp.mean(h, axis=-1, keepdims=True)
    spread = jnp.mean(center * center, axis=-1, keepdims=True)
    rstd = lax.rsqrt(spread + 1e-05)
    return center * rstd, rstd


def norm_back(grad, xh, rstd, gain):
    gs = grad * gain
    m1 = jnp.mean(gs, axis=-1, keepdims=True)
    m2 = jnp.mean(gs * xh, axis=-1, keepdims=True)
    dh = (gs - m1 - xh * m2) * rstd
    return (
        dh,
        jnp.sum(grad * xh, axis=0, keepdims=True),
        jnp.sum(grad, axis=0, keepdims=True),
    )


def row_attend(k_ref, qt_ref, vt_ref, mask_ref, ctx_ref, lse_ref, size, key_end):
    @pl.loop(0, HEADS // 2)
    def _(pair):
        lanes = pl.ds(pl.multiple_of(pair * 2 * HEAD, 2 * HEAD), 2 * HEAD)
        for half in range(2):
            head = pair * 2 + half
            for qb in range(size // TB):
                ke, qs = key_end(qb), slice(qb * TB, (qb + 1) * TB)
                s = mm(k_ref[0:ke, lanes], half_of(qt_ref[lanes, qs], half))
                s = s + mask_ref[0:ke, qs]
                m = jnp.max(s, axis=0, keepdims=True)
                p = jnp.exp2(s - m).astype(BF16)
                o = mm(vt_ref[pl.ds(pl.multiple_of(head * AUG, 16), AUG), 0:ke], p)
                total = o[HEAD : HEAD + 1]
                ctx_ref[pl.ds(pl.multiple_of(head * HEAD, HEAD), HEAD), qs] = (
                    o[:HEAD] * (1.0 / total)
                ).astype(BF16)
                lse_ref[head, :, qs] = m + jnp.log2(total)


def forward_kernel(
    row_of, x_ref, mem_ref, tl_ref, sl_ref, vec_ref, wqkv_ref, wso_ref, wcq_ref, wckv_ref, wco_ref,
    q_ref, qt_ref, k_ref, kt_ref, v_ref, ctx_ref, lse_ref, xh1_ref, rs1_ref,
    q2_ref, q2t_ref, k2_ref, k2t_ref, v2_ref, c2_ref, lse2_ref, y2_ref, xh2_ref, rs2_ref,
    mask, mask2, vt, v2t, y1,
):
    size, width = x_ref.shape
    src = mem_ref.shape[0]
    blocks = size // TB
    row = row_of()

    def vec(i):
        return vec_ref[i : i + 1, :]

    for head in range(HEADS):
        vt[head * AUG + HEAD : (head + 1) * AUG, :] = jnp.ones((AUG - HEAD, size), BF16)
        v2t[head * AUG + HEAD : (head + 1) * AUG, :] = jnp.ones((AUG - HEAD, src), BF16)
    self_mask(mask, tl_ref[...], row, size)
    cross_mask(mask2, tl_ref[...], sl_ref[...], row, size, src)

    def put_vt(ref, values, place):
        for head in range(HEADS):
            ref[head * AUG : head * AUG + HEAD, place] = values[head * HEAD : (head + 1) * HEAD]

    for tb in range(blocks):
        ts = slice(tb * TB, (tb + 1) * TB)
        xb = x_ref[ts, :]
        q = ((mm(xb, wqkv_ref[:, :width]) + vec(V_Q)) * (SCALE * LOG2E)).astype(BF16)
        q_ref[ts, :] = q
        qt_ref[:, ts] = q.T
        k = mm(xb, wqkv_ref[:, width : 2 * width]).astype(BF16)
        k_ref[ts, :] = k
        kt_ref[:, ts] = k.T
        v = (mm(xb, wqkv_ref[:, 2 * width :]) + vec(V_V)).astype(BF16)
        v_ref[ts, :] = v
        put_vt(vt, v.T, ts)
    k2 = mm(mem_ref[...], wckv_ref[:, :width]).astype(BF16)
    k2_ref[...] = k2
    k2t_ref[...] = k2.T
    v2 = (mm(mem_ref[...], wckv_ref[:, width:]) + vec(V_CV)).astype(BF16)
    v2_ref[...] = v2
    put_vt(v2t, v2.T, slice(None))

    row_attend(k_ref, qt_ref, vt, mask, ctx_ref, lse_ref, size, lambda qb: (qb + 1) * TB)
    for tb in range(blocks):
        ts = slice(tb * TB, (tb + 1) * TB)
        h1 = x_ref[ts, :].astype(F32) + mm(ctx_ref[:, ts].T, wso_ref[...]) + vec(V_SO)
        xh, rstd = normalize(h1)
        xh1_ref[ts, :] = xh.astype(BF16)
        rs1_ref[ts, :] = rstd
        yb = xh * vec(V_G) + vec(V_B)
        y1[ts, :] = yb
        q2 = ((mm(yb.astype(BF16), wcq_ref[...]) + vec(V_CQ)) * (SCALE * LOG2E)).astype(BF16)
        q2_ref[ts, :] = q2
        q2t_ref[:, ts] = q2.T
    row_attend(k2_ref, q2t_ref, v2t, mask2, c2_ref, lse2_ref, size, lambda qb: src)
    for tb in range(blocks):
        ts = slice(tb * TB, (tb + 1) * TB)
        h2 = y1[ts, :] + mm(c2_ref[:, ts].T, wco_ref[...]) + vec(V_CO)
        xh, rstd = normalize(h2)
        xh2_ref[ts, :] = xh.astype(BF16)
        rs2_ref[ts, :] = rstd
        y2_ref[ts, :] = xh * vec(V_G + 1) + vec(V_B + 1)


def ffn_kernel(
    y2_ref, xh2_ref, rs2_ref, cot_ref, vec_ref, win_ref, wout_ref,
    out_ref, dh2_ref, dwin_ref, dwout_ref, dvec_ref,
    a_s, du_s, slope_s, y2b_s, dz_s,
):
    size, width = y2_ref.shape
    inner = win_ref.shape[1]
    cols = [slice(j, j + width) for j in range(0, inner, width)]

    def vec(i):
        return vec_ref[i : i + 1, :]

    dvec_ref[...] = jnp.zeros_like(dvec_ref)

    @pl.loop(0, size // TB)
    def _(tb):
        ts = pl.ds(pl.multiple_of(tb * TB, TB), TB)
        y2 = y2_ref[ts, :]
        y2b = y2.astype(BF16)
        y2b_s[ts, :] = y2b
        h3 = y2 + vec(V_FO)
        for j, cs in enumerate(cols):
            u = mm(y2b, win_ref[:, cs]) + vec(V_FI + j)
            sg = 0.5 * jnp.tanh(0.5 * u) + 0.5
            act = u * sg
            slope_s[:, cs] = sg + act * (1.0 - sg)
            act = act.astype(BF16)
            a_s[ts, cs] = act
            h3 = h3 + mm(act, wout_ref[cs, :])
        xh, rstd = normalize(h3)
        out_ref[ts, :] = (xh * vec(V_G + 2) + vec(V_B + 2)).astype(BF16)
        grad = cot_ref[ts, :].astype(F32)
        dh3, dg, db = norm_back(grad, xh, rstd, vec(V_G + 2))
        dz = dh3.astype(BF16)
        dz_s[ts, :] = dz
        dvec_ref[V_G + 2 : V_G + 3, :] += dg
        dvec_ref[V_B + 2 : V_B + 3, :] += db
        dvec_ref[V_FO : V_FO + 1, :] += jnp.sum(dz.astype(F32), axis=0, keepdims=True)
        dy2 = dh3
        for j, cs in enumerate(cols):
            du = (mm(dz, wout_ref[cs, :], 1, 1) * slope_s[:, cs]).astype(BF16)
            du_s[ts, cs] = du
            dvec_ref[V_FI + j : V_FI + j + 1, :] += jnp.sum(du.astype(F32), axis=0, keepdims=True)
            dy2 = dy2 + mm(du, win_ref[:, cs], 1, 1)
        xh2 = xh2_ref[ts, :].astype(F32)
        dh2, dg, db = norm_back(dy2, xh2, rs2_ref[ts, :], vec(V_G + 1))
        dh2_ref[ts, :] = dh2
        dvec_ref[V_G + 1 : V_G + 2, :] += dg
        dvec_ref[V_B + 1 : V_B + 2, :] += db

    for j, cs in enumerate(cols):
        dwin_ref[j * width : (j + 1) * width, :] = mm(y2b_s[...], du_s[:, cs], 0, 0).astype(BF16)
        dwout_ref[cs, :] = mm(a_s[:, cs], dz_s[...], 0, 0).astype(BF16)


def row_attend_back(
    k_ref, kt_ref, v_ref, q_ref, qt_ref, dc_ref, dct_ref, ctx_ref, lse_ref, mask_ref,
    delta, dqt, dq_ref, dk_ref, dv_ref, size, keys, query_start,
):
    @pl.loop(0, HEADS // 2)
    def _(pair):
        lanes = pl.ds(pl.multiple_of(pair * 2 * HEAD, 2 * HEAD), 2 * HEAD)
        both = dct_ref[lanes, :].astype(F32) * ctx_ref[lanes, :].astype(F32)
        for half in range(2):
            delta[half] = jnp.sum(both[half * HEAD : (half + 1) * HEAD], axis=0, keepdims=True)
        dqt[...] = jnp.zeros_like(dqt)
        for kb in range(keys // TB):
            ks, qs = slice(kb * TB, (kb + 1) * TB), slice(query_start(kb), size)
            dks, dvs = [], []
            for half in range(2):
                head = pair * 2 + half
                rows = pl.ds(pl.multiple_of(head * HEAD, HEAD), HEAD)
                s = mm(k_ref[ks, lanes], half_of(qt_ref[lanes, qs], half))
                p = jnp.exp2(s + mask_ref[ks, qs] - lse_ref[head, :, qs])
                dp = mm(v_ref[ks, lanes], half_of(dct_ref[lanes, qs], half))
                ds = (p * (dp - delta[half, :, qs])).astype(BF16)
                dvs.append(mm(p.astype(BF16), dc_ref[qs, lanes]))
                dks.append(mm(ds, q_ref[qs, lanes]))
                dqt[half * HEAD : (half + 1) * HEAD, qs] += mm(kt_ref[rows, ks], ds)
            first = lax.broadcasted_iota(jnp.int32, (TB, 2 * HEAD), 1) < HEAD
            dv_ref[ks, lanes] = jnp.where(first, dvs[0], dvs[1]).astype(BF16)
            dk_ref[ks, lanes] = (jnp.where(first, dks[0], dks[1]) * (1.0 / LOG2E)).astype(BF16)
        dq_ref[:, lanes] = (dqt[...] * SCALE).astype(BF16).T


def backward_kernel(
    row_of, dh2_ref, x_ref, mem_ref, tl_ref, sl_ref, vec_ref,
    wqkv_ref, wso_ref, wcq_ref, wckv_ref, wco_ref,
    q_ref, qt_ref, k_ref, kt_ref, v_ref, ctx_ref, lse_ref, xh1_ref, rs1_ref,
    q2_ref, q2t_ref, k2_ref, k2t_ref, v2_ref, c2_ref, lse2_ref,
    dtok_ref, dmem_ref, dw_ref, dvec_ref,
    mask, mask2, delta, dqt, dc, dct, dq, dk, dv, dk2, dv2, dh1, y1b,
):
    size, width = x_ref.shape
    src = mem_ref.shape[0]
    blocks = [slice(t, t + TB) for t in range(0, size, TB)]
    row = row_of()

    def vec(i):
        return vec_ref[i : i + 1, :]

    def total(values):
        return jnp.sum(values.astype(F32), axis=0, keepdims=True)

    dvec_ref[...] = jnp.zeros_like(dvec_ref)
    self_mask(mask, tl_ref[...], row, size)
    cross_mask(mask2, tl_ref[...], sl_ref[...], row, size, src)
    da = dh1
    for ts in blocks:
        da2 = dh2_ref[ts, :].astype(BF16)
        dc[ts, :] = mm(da2, wco_ref[...], 1, 1).astype(BF16)
        dct[:, ts] = mm(wco_ref[...], da2, 1, 1).astype(BF16)
        dvec_ref[V_CO : V_CO + 1, :] += total(da2)
    da2 = dh2_ref[...].astype(BF16)
    dw_ref[0:width, :] = mm(c2_ref[...], da2).astype(BF16)
    row_attend_back(
        k2_ref, k2t_ref, v2_ref, q2_ref, q2t_ref, dc, dct, c2_ref, lse2_ref, mask2,
        delta, dqt, dq, dk2, dv2, size, src, lambda kb: 0,
    )
    dvec_ref[V_CV : V_CV + 1, :] = total(dv2[...])
    dvec_ref[V_CQ : V_CQ + 1, :] = total(dq[...])
    dw_ref[2 * width : 3 * width, :] = mm(mem_ref[...], dk2[...], 0, 0).astype(BF16)
    dw_ref[3 * width : 4 * width, :] = mm(mem_ref[...], dv2[...], 0, 0).astype(BF16)
    dmem_ref[...] = (
        mm(dk2[...], wckv_ref[:, :width], 1, 1) + mm(dv2[...], wckv_ref[:, width:], 1, 1)
    ).astype(BF16)
    for ts in blocks:
        dqb = dq[ts, :]
        dy1 = dh2_ref[ts, :] + mm(dqb, wcq_ref[...], 1, 1)
        xh1 = xh1_ref[ts, :].astype(F32)
        y1b[ts, :] = (xh1 * vec(V_G) + vec(V_B)).astype(BF16)
        dh, dg, db = norm_back(dy1, xh1, rs1_ref[ts, :], vec(V_G))
        dvec_ref[V_G : V_G + 1, :] += dg
        dvec_ref[V_B : V_B + 1, :] += db
        dh1[ts, :] = dh
        da1 = dh.astype(BF16)
        dvec_ref[V_SO : V_SO + 1, :] += total(da1)
    dw_ref[width : 2 * width, :] = mm(y1b[...], dq[...], 0, 0).astype(BF16)
    for ts in blocks:
        da1 = dh1[ts, :].astype(BF16)
        dc[ts, :] = mm(da1, wso_ref[...], 1, 1).astype(BF16)
        dct[:, ts] = mm(wso_ref[...], da1, 1, 1).astype(BF16)
    dw_ref[4 * width : 5 * width, :] = mm(ctx_ref[...], dh1[...].astype(BF16)).astype(BF16)
    row_attend_back(
        k_ref, kt_ref, v_ref, q_ref, qt_ref, dc, dct, ctx_ref, lse_ref, mask,
        delta, dqt, dq, dk, dv, size, size, lambda kb: kb * TB,
    )
    dvec_ref[V_Q : V_Q + 1, :] = total(dq[...])
    dvec_ref[V_V : V_V + 1, :] = total(dv[...])
    for i, part in enumerate((dq, dk, dv)):
        dw_ref[(5 + i) * width : (6 + i) * width, :] = mm(x_ref[...], part[...], 0, 0).astype(BF16)
    for ts in blocks:
        dtok_ref[ts, :] = (
            dh1[ts, :]
            + mm(dq[ts, :], wqkv_ref[:, :width], 1, 1)
            + mm(dk[ts, :], wqkv_ref[:, width : 2 * width], 1, 1)
            + mm(dv[ts, :], wqkv_ref[:, 2 * width :], 1, 1)
        ).astype(BF16)


WHOLE = pl.BlockSpec(memory_space=pltpu.VMEM)


def call(kernel, ins, outs, scratch, name):
    return pl.pallas_call(
        kernel,
        out_shape=[jax.ShapeDtypeStruct(*o) for o in outs],
        in_specs=[WHOLE] * len(ins),
        out_specs=[WHOLE] * len(outs),
        scratch_shapes=[pltpu.VMEM(*s) for s in scratch],
        compiler_params=pltpu.CompilerParams(vmem_limit_bytes=60 * 2**20),
        name=name,
    )(*ins)


def forward(row_of, x, mem, tl, sl, vecs, wqkv, wso, wcq, wckv, wco):
    (t, d), s = x.shape, mem.shape[0]
    tok, feat, row = ((t, d), BF16), ((d, t), BF16), ((HEADS, 1, t), F32)
    col = ((t, 1), F32)
    return call(
        functools.partial(forward_kernel, row_of),
        (x, mem, tl, sl, vecs, wqkv, wso, wcq, wckv, wco),
        [tok, feat, tok, feat, tok, feat, row, tok, col,
         tok, feat, ((s, d), BF16), ((d, s), BF16), ((s, d), BF16), feat, row, ((t, d), F32), tok, col],
        [((t, t), F32), ((s, t), F32), ((HEADS * AUG, t), BF16), ((HEADS * AUG, s), BF16), ((t, d), F32)],
        "forward",
    )


def ffn(y2, xh2, rs2, cot, vecs, win, wout):
    (t, d), f = y2.shape, win.shape[1]
    return call(
        ffn_kernel,
        (y2, xh2, rs2, cot, vecs, win, wout),
        [((t, d), BF16), ((t, d), F32), ((f, d), BF16), ((f, d), BF16), ((VECS, d), F32)],
        [((t, f), BF16), ((t, f), BF16), ((TB, f), F32), ((t, d), BF16), ((t, d), BF16)],
        "ffn",
    )


def backward(row_of, dh2, x, mem, tl, sl, vecs, wqkv, wso, wcq, wckv, wco, *saved):
    (t, d), s = x.shape, mem.shape[0]
    tok = ((t, d), BF16)
    return call(
        functools.partial(backward_kernel, row_of),
        (dh2, x, mem, tl, sl, vecs, wqkv, wso, wcq, wckv, wco) + saved,
        [tok, ((s, d), BF16), ((8 * d, d), BF16), ((VECS, d), F32)],
        [((t, t), F32), ((s, t), F32), ((2, 1, t), F32), ((2 * HEAD, t), F32), tok, ((d, t), BF16),
         tok, tok, tok, ((s, d), BF16), ((s, d), BF16), ((t, d), F32), tok],
        "backward",
    )


def pack_vecs(qv_bias, so, cq, cv, co, fi, fo, gains, shifts):
    d = so.shape[0]
    parts = [qv_bias, so, cq, cv, co, fi, fo, gains.reshape(-1), shifts.reshape(-1)]
    flat = jnp.concatenate([p.astype(F32) for p in parts])
    return jnp.pad(flat, (0, VECS * d - flat.shape[0])).reshape(VECS, d)


def row_layer(row_of, x, mem, tl, sl, cot, w_qkv, qv_bias, self_out, self_out_bias, cross_query, cross_q_bias, cross_kv, cross_v_bias, cross_out, cross_out_bias, ffn_in, ffn_in_bias, ffn_out, ffn_out_bias, norm_gains, norm_biases):
    vecs = pack_vecs(qv_bias, self_out_bias, cross_q_bias, cross_v_bias, cross_out_bias, ffn_in_bias, ffn_out_bias, norm_gains, norm_biases)
    *saved, y2, xh2, rs2 = forward(row_of, x, mem, tl, sl, vecs, w_qkv, self_out, cross_query, cross_kv, cross_out)
    out, dh2, dwin, dwout, dvec_a = ffn(y2, xh2, rs2, cot, vecs, ffn_in, ffn_out)
    dtok, dmem, dw, dvec_b = backward(row_of, dh2, x, mem, tl, sl, vecs, w_qkv, self_out, cross_query, cross_kv, cross_out, *saved)
    return out, dtok, dmem, dwin, dwout, dw, dvec_a + dvec_b


def unpack(dwin, dwout, dw, dvec):
    d = dw.shape[1]
    f = dwout.shape[0]
    w = [dw[i * d:(i + 1) * d].astype(F32) for i in range(8)]
    v = dvec.reshape(-1).astype(F32)
    d_ffn_in = jnp.concatenate([dwin[i * d:(i + 1) * d] for i in range(f // d)], axis=1).astype(F32)
    return (
        jnp.concatenate(w[5:8], axis=1), v[:2 * d], w[4], v[2 * d:3 * d], w[1], v[3 * d:4 * d],
        jnp.concatenate(w[2:4], axis=1), v[4 * d:5 * d], w[0], v[5 * d:6 * d], d_ffn_in, v[6 * d:10 * d],
        dwout.astype(F32), v[10 * d:11 * d], v[11 * d:14 * d].reshape(3, d), v[14 * d:17 * d].reshape(3, d),
    )


def layer_norm(values, gain, shift):
    center = values - jnp.mean(values, axis=-1, keepdims=True)
    spread = jnp.mean(center * center, axis=-1, keepdims=True)
    return center * lax.rsqrt(spread + 1e-05) * gain + shift


def doc_ids(lengths, size):
    ends = jnp.cumsum(lengths, axis=1)
    places = jnp.arange(size, dtype=jnp.int32)
    return jnp.sum((ends[:, None, :] <= places[None, :, None]).astype(jnp.int32), axis=2)


def block_width(key_total):
    return 512 if key_total % 512 == 0 else key_total


def contract_rows(left, right):
    return lax.dot_general(
        left, right, (((0,), (0,)), ((), ())), preferred_element_type=jnp.float32
    )


def contract_cols(left, right):
    return lax.dot_general(
        left, right, (((1,), (1,)), ((), ())), preferred_element_type=jnp.float32
    )


def block_scores(queries, keys, allowed, start_at, width_of, score_scale):
    key_block = lax.dynamic_slice_in_dim(keys, start_at, width_of, 1)
    scores = (
        jnp.einsum("rqhd,rkhd->rhqk", queries, key_block, preferred_element_type=jnp.float32)
        * score_scale
    )
    return jnp.where(allowed(start_at, width_of)[:, None], scores, -1000000000.0)


def attend_forward(queries, keys, values, allowed, skip_after, score_scale):
    row_count, query_count, head_count, head_size = queries.shape
    key_total = keys.shape[1]
    width_of = block_width(key_total)
    block_count = key_total // width_of

    def statistics(carried, block_index):
        start_at = block_index * width_of

        def statistics_work(state):
            running_max, running_sum = state
            scores = block_scores(queries, keys, allowed, start_at, width_of, score_scale)
            new_max = jnp.maximum(running_max, jnp.max(scores, axis=3))
            new_sum = running_sum * jnp.exp(running_max - new_max) + jnp.sum(
                jnp.exp(scores - new_max[..., None]), axis=3
            )
            return (new_max, new_sum)

        return (
            lax.cond(start_at > skip_after, lambda state: state, statistics_work, carried),
            None,
        )

    stat_shape = (row_count, head_count, query_count)
    start_state = (
        jnp.full(stat_shape, -1000000000.0, jnp.float32),
        jnp.zeros(stat_shape, jnp.float32),
    )
    block_numbers = jnp.arange(block_count, dtype=jnp.int32)
    (running_max, running_sum), _ = lax.scan(statistics, start_state, block_numbers)
    log_total = running_max + jnp.log(running_sum)

    def mixing(carried, block_index):
        start_at = block_index * width_of

        def mixing_work(accum):
            scores = block_scores(queries, keys, allowed, start_at, width_of, score_scale)
            probs = jnp.exp(scores - log_total[..., None]).astype(jnp.bfloat16)
            value_block = lax.dynamic_slice_in_dim(values, start_at, width_of, 1)
            return accum + jnp.einsum(
                "rhqk,rkhd->rqhd", probs, value_block, preferred_element_type=jnp.float32
            )

        return (lax.cond(start_at > skip_after, lambda accum: accum, mixing_work, carried), None)

    start_accum = jnp.zeros((row_count, query_count, head_count, head_size), jnp.float32)
    accum, _ = lax.scan(mixing, start_accum, block_numbers)
    return (accum, log_total)


def attend_back(
    queries, keys, values, allowed, skip_after, score_scale, log_total, grad_out, delta
):
    row_count, query_count, head_count, head_size = queries.shape
    key_total = keys.shape[1]
    width_of = block_width(key_total)
    block_count = key_total // width_of

    def step(block_index, state):
        start_at = block_index * width_of

        def step_work(inner):
            scores = block_scores(queries, keys, allowed, start_at, width_of, score_scale)
            probs = jnp.exp(scores - log_total[..., None])
            key_block = lax.dynamic_slice_in_dim(keys, start_at, width_of, 1)
            value_block = lax.dynamic_slice_in_dim(values, start_at, width_of, 1)
            grad_probs = jnp.einsum(
                "rqhd,rkhd->rhqk", grad_out, value_block, preferred_element_type=jnp.float32
            )
            grad_scores = (probs * (grad_probs - delta[..., None])).astype(jnp.bfloat16)
            grad_query = (
                inner[0]
                + jnp.einsum(
                    "rhqk,rkhd->rqhd", grad_scores, key_block, preferred_element_type=jnp.float32
                )
                * score_scale
            )
            key_part = (
                jnp.einsum(
                    "rhqk,rqhd->rkhd", grad_scores, queries, preferred_element_type=jnp.float32
                )
                * score_scale
            )
            value_part = jnp.einsum(
                "rhqk,rqhd->rkhd",
                probs.astype(jnp.bfloat16),
                grad_out,
                preferred_element_type=jnp.float32,
            )
            grad_keys = lax.dynamic_update_slice_in_dim(inner[1], key_part, start_at, 1)
            grad_values = lax.dynamic_update_slice_in_dim(inner[2], value_part, start_at, 1)
            return (grad_query, grad_keys, grad_values)

        return lax.cond(start_at > skip_after, lambda inner: inner, step_work, state)

    start_state = (jnp.zeros((row_count, query_count, head_count, head_size), jnp.float32),)
    start_state = start_state + (
        jnp.zeros((row_count, key_total, head_count, head_size), jnp.float32),
        jnp.zeros((row_count, key_total, head_count, head_size), jnp.float32),
    )
    return lax.fori_loop(0, block_count, step, start_state)


def blocks_on_device(
    tokens,
    memory,
    doc_lengths,
    src_lengths,
    cotangent,
    w_qkv,
    qv_bias,
    self_out,
    self_out_bias,
    cross_query,
    cross_q_bias,
    cross_kv,
    cross_v_bias,
    cross_out,
    cross_out_bias,
    ffn_in,
    ffn_in_bias,
    ffn_out,
    ffn_out_bias,
    norm_gains,
    norm_biases,
):
    row_count, block_len, model_width = tokens.shape
    src_block = memory.shape[1]
    seq_count = lax.axis_size("seq")
    row_length = block_len * seq_count
    src_length = src_block * seq_count
    score_scale = HEAD ** (-0.5)
    first_place = lax.axis_index("seq") * block_len
    last_place = first_place + block_len - 1
    target_ids = doc_ids(doc_lengths, row_length)
    source_ids = doc_ids(src_lengths, src_length)
    own_ids = lax.dynamic_slice_in_dim(target_ids, first_place, block_len, 1)
    own_places = first_place + jnp.arange(block_len, dtype=jnp.int32)

    def self_allowed(start_at, width_of):
        key_ids = lax.dynamic_slice_in_dim(target_ids, start_at, width_of, 1)
        key_places = start_at + jnp.arange(width_of, dtype=jnp.int32)
        return (own_ids[:, :, None] == key_ids[:, None, :]) & (
            key_places[None, None, :] <= own_places[None, :, None]
        )

    def cross_allowed(start_at, width_of):
        return (own_ids[:, :, None] == source_ids[:, None, :]) | (own_ids[:, :, None] == NDOC)

    def split_heads(array_in):
        return array_in.reshape(array_in.shape[0], array_in.shape[1], HEADS, HEAD)

    token_rows = row_count * block_len
    flat_tokens = tokens.reshape(token_rows, model_width)
    flat_memory = memory.reshape(row_count * src_block, model_width)
    pair_bias = qv_bias.astype(jnp.float32)
    gains = norm_gains.astype(jnp.float32)
    shifts = norm_biases.astype(jnp.float32)
    packed = jnp.dot(flat_tokens, w_qkv, preferred_element_type=jnp.float32)
    self_queries = (packed[:, :model_width] + pair_bias[:model_width]).astype(jnp.bfloat16)
    self_keys = (
        packed[:, model_width : 2 * model_width]
        .astype(jnp.bfloat16)
        .reshape(row_count, block_len, model_width)
    )
    self_values = (
        (packed[:, 2 * model_width :] + pair_bias[model_width:])
        .astype(jnp.bfloat16)
        .reshape(row_count, block_len, model_width)
    )
    memory_pair = jnp.dot(flat_memory, cross_kv, preferred_element_type=jnp.float32)
    cross_keys = (
        memory_pair[:, :model_width].astype(jnp.bfloat16).reshape(row_count, src_block, model_width)
    )
    cross_values = (
        (memory_pair[:, model_width:] + cross_v_bias.astype(jnp.float32))
        .astype(jnp.bfloat16)
        .reshape(row_count, src_block, model_width)
    )
    all_keys, all_values, all_ckeys, all_cvalues = (
        lax.all_gather(self_keys, "seq", axis=1, tiled=True),
        lax.all_gather(self_values, "seq", axis=1, tiled=True),
        lax.all_gather(cross_keys, "seq", axis=1, tiled=True),
        lax.all_gather(cross_values, "seq", axis=1, tiled=True),
    )
    query_heads = split_heads(self_queries.reshape(row_count, block_len, model_width))
    self_accum, self_log = attend_forward(
        query_heads,
        split_heads(all_keys),
        split_heads(all_values),
        self_allowed,
        last_place,
        score_scale,
    )
    context_low = self_accum.reshape(token_rows, model_width).astype(jnp.bfloat16)
    inputs_f = flat_tokens.astype(jnp.float32)
    first_sum = (
        inputs_f
        + jnp.dot(context_low, self_out, preferred_element_type=jnp.float32)
        + self_out_bias.astype(jnp.float32)
    )
    first_norm, first_pull = jax.vjp(layer_norm, first_sum, gains[0], shifts[0])
    first_low = first_norm.astype(jnp.bfloat16)
    cross_q_rows = (
        jnp.dot(first_low, cross_query, preferred_element_type=jnp.float32)
        + cross_q_bias.astype(jnp.float32)
    ).astype(jnp.bfloat16)
    cross_heads = split_heads(cross_q_rows.reshape(row_count, block_len, model_width))
    cross_accum, cross_log = attend_forward(
        cross_heads,
        split_heads(all_ckeys),
        split_heads(all_cvalues),
        cross_allowed,
        src_length,
        score_scale,
    )
    cross_low = cross_accum.reshape(token_rows, model_width).astype(jnp.bfloat16)
    second_sum = (
        first_norm
        + jnp.dot(cross_low, cross_out, preferred_element_type=jnp.float32)
        + cross_out_bias.astype(jnp.float32)
    )
    second_norm, second_pull = jax.vjp(layer_norm, second_sum, gains[1], shifts[1])
    second_low = second_norm.astype(jnp.bfloat16)
    hidden_pre = jnp.dot(
        second_low, ffn_in, preferred_element_type=jnp.float32
    ) + ffn_in_bias.astype(jnp.float32)
    hidden_low = jax.nn.silu(hidden_pre).astype(jnp.bfloat16)
    third_sum = (
        second_norm
        + jnp.dot(hidden_low, ffn_out, preferred_element_type=jnp.float32)
        + ffn_out_bias.astype(jnp.float32)
    )
    result, third_pull = jax.vjp(layer_norm, third_sum, gains[2], shifts[2])
    output = result.astype(jnp.bfloat16).reshape(row_count, block_len, model_width)
    grad_third, gain_three, shift_three = third_pull(
        cotangent.reshape(token_rows, model_width).astype(jnp.float32)
    )
    grad_branch = grad_third.astype(jnp.bfloat16)
    d_ffn_out = contract_rows(hidden_low, grad_branch)
    d_ffn_out_bias = jnp.sum(grad_branch.astype(jnp.float32), axis=0)
    grad_hidden = contract_cols(grad_branch, ffn_out)
    sigmoid_pre = jax.nn.sigmoid(hidden_pre)
    grad_pre = (grad_hidden * sigmoid_pre * (1.0 + hidden_pre * (1.0 - sigmoid_pre))).astype(
        jnp.bfloat16
    )
    d_ffn_in = contract_rows(second_low, grad_pre)
    d_ffn_in_bias = jnp.sum(grad_pre.astype(jnp.float32), axis=0)
    grad_second_norm = grad_third + contract_cols(grad_pre, ffn_in)
    back_keys, back_values, back_ckeys, back_cvalues = (
        all_keys,
        all_values,
        all_ckeys,
        all_cvalues,
    )
    grad_second, gain_two, shift_two = second_pull(grad_second_norm)
    grad_cross_branch = grad_second.astype(jnp.bfloat16)
    d_cross_out = contract_rows(cross_low, grad_cross_branch)
    d_cross_out_bias = jnp.sum(grad_cross_branch.astype(jnp.float32), axis=0)
    grad_cross_ctx = contract_cols(grad_cross_branch, cross_out).astype(jnp.bfloat16)
    grad_cross_heads = split_heads(grad_cross_ctx.reshape(row_count, block_len, model_width))
    cross_delta = jnp.swapaxes(
        jnp.sum(grad_cross_heads.astype(jnp.float32) * cross_accum, axis=3), 1, 2
    )
    grad_cq, grad_ck_all, grad_cv_all = attend_back(
        cross_heads,
        split_heads(back_ckeys),
        split_heads(back_cvalues),
        cross_allowed,
        src_length,
        score_scale,
        cross_log,
        grad_cross_heads,
        cross_delta,
    )
    grad_ck_own, grad_cv_own = (
        lax.psum_scatter(
            grad_ck_all.reshape(row_count, src_length, model_width).astype(jnp.bfloat16),
            "seq",
            scatter_dimension=1,
            tiled=True,
        ).astype(jnp.float32),
        lax.psum_scatter(
            grad_cv_all.reshape(row_count, src_length, model_width).astype(jnp.bfloat16),
            "seq",
            scatter_dimension=1,
            tiled=True,
        ).astype(jnp.float32),
    )
    grad_pair = jnp.concatenate(
        [
            grad_ck_own.reshape(row_count * src_block, model_width).astype(jnp.bfloat16),
            grad_cv_own.reshape(row_count * src_block, model_width).astype(jnp.bfloat16),
        ],
        axis=1,
    )
    d_cross_kv = contract_rows(flat_memory, grad_pair)
    d_cross_v_bias = jnp.sum(grad_pair[:, model_width:].astype(jnp.float32), axis=0)
    d_memory = contract_cols(grad_pair, cross_kv).reshape(row_count, src_block, model_width)
    grad_cq_low = grad_cq.reshape(token_rows, model_width).astype(jnp.bfloat16)
    d_cross_query = contract_rows(first_low, grad_cq_low)
    d_cross_q_bias = jnp.sum(grad_cq_low.astype(jnp.float32), axis=0)
    grad_first_norm = grad_second + contract_cols(grad_cq_low, cross_query)
    grad_first, gain_one, shift_one = first_pull(grad_first_norm)
    grad_self_branch = grad_first.astype(jnp.bfloat16)
    d_self_out = contract_rows(context_low, grad_self_branch)
    d_self_out_bias = jnp.sum(grad_self_branch.astype(jnp.float32), axis=0)
    grad_context = contract_cols(grad_self_branch, self_out).astype(jnp.bfloat16)
    grad_context_heads = split_heads(grad_context.reshape(row_count, block_len, model_width))
    self_delta = jnp.swapaxes(
        jnp.sum(grad_context_heads.astype(jnp.float32) * self_accum, axis=3), 1, 2
    )
    grad_q, grad_k_all, grad_v_all = attend_back(
        query_heads,
        split_heads(back_keys),
        split_heads(back_values),
        self_allowed,
        last_place,
        score_scale,
        self_log,
        grad_context_heads,
        self_delta,
    )
    grad_k_own, grad_v_own = (
        lax.psum_scatter(
            grad_k_all.reshape(row_count, row_length, model_width).astype(jnp.bfloat16),
            "seq",
            scatter_dimension=1,
            tiled=True,
        ).astype(jnp.float32),
        lax.psum_scatter(
            grad_v_all.reshape(row_count, row_length, model_width).astype(jnp.bfloat16),
            "seq",
            scatter_dimension=1,
            tiled=True,
        ).astype(jnp.float32),
    )
    grad_k_flat = grad_k_own.reshape(token_rows, model_width)
    grad_v_flat = grad_v_own.reshape(token_rows, model_width)
    grad_q_low = grad_q.reshape(token_rows, model_width).astype(jnp.bfloat16)
    grad_v_low = grad_v_flat.astype(jnp.bfloat16)
    grad_proj = jnp.concatenate([grad_q_low, grad_k_flat.astype(jnp.bfloat16), grad_v_low], axis=1)
    d_w_qkv = contract_rows(flat_tokens, grad_proj)
    d_qv_bias = jnp.concatenate(
        [
            jnp.sum(grad_q_low.astype(jnp.float32), axis=0),
            jnp.sum(grad_v_low.astype(jnp.float32), axis=0),
        ]
    )
    d_tokens = (grad_first + contract_cols(grad_proj, w_qkv)).reshape(
        row_count, block_len, model_width
    )
    d_norm_gains = jnp.stack([gain_one, gain_two, gain_three])
    d_norm_biases = jnp.stack([shift_one, shift_two, shift_three])
    (
        d_w_qkv,
        d_qv_bias,
        d_self_out,
        d_self_out_bias,
        d_cross_query,
        d_cross_q_bias,
        d_cross_kv,
        d_cross_v_bias,
        d_cross_out,
        d_cross_out_bias,
        d_ffn_in,
        d_ffn_in_bias,
        d_ffn_out,
        d_ffn_out_bias,
        d_norm_gains,
        d_norm_biases,
    ) = lax.psum(
        (
            d_w_qkv,
            d_qv_bias,
            d_self_out,
            d_self_out_bias,
            d_cross_query,
            d_cross_q_bias,
            d_cross_kv,
            d_cross_v_bias,
            d_cross_out,
            d_cross_out_bias,
            d_ffn_in,
            d_ffn_in_bias,
            d_ffn_out,
            d_ffn_out_bias,
            d_norm_gains,
            d_norm_biases,
        ),
        ("dp", "seq"),
    )
    return (
        output,
        d_tokens,
        d_memory,
        d_w_qkv,
        d_qv_bias,
        d_self_out,
        d_self_out_bias,
        d_cross_query,
        d_cross_q_bias,
        d_cross_kv,
        d_cross_v_bias,
        d_cross_out,
        d_cross_out_bias,
        d_ffn_in,
        d_ffn_in_bias,
        d_ffn_out,
        d_ffn_out_bias,
        d_norm_gains,
        d_norm_biases,
    )


def rows_on_device(tokens, memory, doc_lengths, src_lengths, cotangent, *params):
    row_count, block_len, width = tokens.shape

    def to_row(blocks):
        return lax.all_to_all(blocks, "seq", split_axis=0, concat_axis=1, tiled=True)[0]

    def to_blocks(row):
        return lax.all_to_all(row[None], "seq", split_axis=1, concat_axis=0, tiled=True)

    out, dtok, dmem, dwin, dwout, dw, dvec = row_layer(
        lambda: lax.axis_index("seq"),
        to_row(tokens),
        to_row(memory),
        doc_lengths,
        src_lengths,
        to_row(cotangent),
        *params,
    )
    packed = jnp.concatenate([dwin, dwout, dw, dvec.astype(BF16)], axis=0)
    packed = lax.psum(packed, ("dp", "seq"))
    f = dwout.shape[0]
    grads = unpack(packed[:f], packed[f : 2 * f], packed[2 * f : 2 * f + dw.shape[0]], packed[2 * f + dw.shape[0] :])
    return (to_blocks(out), to_blocks(dtok).astype(F32), to_blocks(dmem).astype(F32)) + grads


def on_device(tokens, *rest):
    if tokens.shape[0] == lax.axis_size("seq"):
        return rows_on_device(tokens, *rest)
    return blocks_on_device(tokens, *rest)


def solution(mesh):
    in_specs = (
        P("dp", "seq", None),
        P("dp", "seq", None),
        P("dp", None),
        P("dp", None),
        P("dp", "seq", None),
        P(),
        P(),
        P(),
        P(),
        P(),
        P(),
        P(),
        P(),
        P(),
        P(),
        P(),
        P(),
        P(),
        P(),
        P(),
        P(),
    )
    out_specs = (
        P("dp", "seq", None),
        P("dp", "seq", None),
        P("dp", "seq", None),
        P(),
        P(),
        P(),
        P(),
        P(),
        P(),
        P(),
        P(),
        P(),
        P(),
        P(),
        P(),
        P(),
        P(),
        P(),
        P(),
    )
    return jax.shard_map(
        on_device, mesh=mesh, in_specs=in_specs, out_specs=out_specs, check_vma=False
    )
```

```python
import functools
import jax
import jax.numpy as jnp
from jax import lax
from jax.experimental import pallas as pl
from jax.experimental.pallas import tpu as pltpu
from jax.sharding import PartitionSpec as P

HEADS = 8
HEAD = 64
NDOC = 32
AUG = HEAD + 16
MASKED = -1e9
LOG2E = 1.4426950408889634
SCALE = HEAD**-0.5
F32 = jnp.float32
BF16 = jnp.bfloat16
TB = 256

V_Q, V_V, V_SO, V_CQ, V_CV, V_CO, V_FI, V_FO, V_G, V_B = 0, 1, 2, 3, 4, 5, 6, 10, 11, 14
VECS = 24


def mm(left, right, lc=1, rc=0):
    return lax.dot_general(
        left, right, (((lc,), (rc,)), ((), ())), preferred_element_type=F32
    )


def row_ids(lengths, row, size):
    rows, docs = lengths.shape
    at_row = lax.broadcasted_iota(jnp.int32, (rows, docs), 0) == row
    own = jnp.sum(jnp.where(at_row, lengths.astype(F32), 0.0), axis=0, keepdims=True)
    own = jnp.broadcast_to(own, (docs, docs))
    down = lax.broadcasted_iota(jnp.int32, (docs, docs), 0)
    over = lax.broadcasted_iota(jnp.int32, (docs, docs), 1)
    ends_col = jnp.sum(jnp.where(over <= down, own, 0.0), axis=1, keepdims=True)
    own_col = jnp.sum(jnp.where(over == down, own, 0.0), axis=1, keepdims=True)
    ends_row = jnp.sum(
        jnp.where(down <= over, jnp.broadcast_to(own_col, (docs, docs)), 0.0),
        axis=0,
        keepdims=True,
    )
    place_row = lax.broadcasted_iota(jnp.int32, (docs, size), 1).astype(F32)
    place_col = lax.broadcasted_iota(jnp.int32, (size, docs), 0).astype(F32)
    ids_row = jnp.sum(jnp.where(ends_col <= place_row, 1.0, 0.0), axis=0, keepdims=True)
    ids_col = jnp.sum(jnp.where(ends_row <= place_col, 1.0, 0.0), axis=1, keepdims=True)
    return ids_row, ids_col


def self_mask(mask_ref, lengths, row, size):
    ids_row, ids_col = row_ids(lengths, row, size)
    for kb in range(size // TB):
        for qb in range(kb, size // TB):
            ks, qs = slice(kb * TB, (kb + 1) * TB), slice(qb * TB, (qb + 1) * TB)
            seen = ids_col[ks] == ids_row[:, qs]
            if kb == qb:
                down = lax.broadcasted_iota(jnp.int32, (TB, TB), 0)
                over = lax.broadcasted_iota(jnp.int32, (TB, TB), 1)
                seen = seen & (down <= over)
            mask_ref[ks, qs] = jnp.where(seen, 0.0, MASKED)


def cross_mask(mask_ref, lengths, src_lengths, row, size, src):
    ids_row, _ = row_ids(lengths, row, size)
    _, src_col = row_ids(src_lengths, row, src)
    for qb in range(size // TB):
        qs = slice(qb * TB, (qb + 1) * TB)
        seen = (src_col == ids_row[:, qs]) | (ids_row[:, qs] == float(NDOC))
        mask_ref[:, qs] = jnp.where(seen, 0.0, MASKED)


def half_of(values, half):
    down = lax.broadcasted_iota(jnp.int32, values.shape, 0)
    keep = (down >= HEAD) if half else (down < HEAD)
    return jnp.where(keep, values, jnp.zeros_like(values))


def normalize(h):
    center = h - jnp.mean(h, axis=-1, keepdims=True)
    spread = jnp.mean(center * center, axis=-1, keepdims=True)
    rstd = lax.rsqrt(spread + 1e-05)
    return center * rstd, rstd


def norm_back(grad, xh, rstd, gain):
    gs = grad * gain
    m1 = jnp.mean(gs, axis=-1, keepdims=True)
    m2 = jnp.mean(gs * xh, axis=-1, keepdims=True)
    dh = (gs - m1 - xh * m2) * rstd
    return (
        dh,
        jnp.sum(grad * xh, axis=0, keepdims=True),
        jnp.sum(grad, axis=0, keepdims=True),
    )


def row_attend(k_ref, qt_ref, vt_ref, mask_ref, ctx_ref, lse_ref, size, key_end):
    @pl.loop(0, HEADS // 2)
    def _(pair):
        lanes = pl.ds(pl.multiple_of(pair * 2 * HEAD, 2 * HEAD), 2 * HEAD)
        for half in range(2):
            head = pair * 2 + half
            for qb in range(size // TB):
                ke, qs = key_end(qb), slice(qb * TB, (qb + 1) * TB)
                s = mm(k_ref[0:ke, lanes], half_of(qt_ref[lanes, qs], half))
                s = s + mask_ref[0:ke, qs]
                m = jnp.max(s, axis=0, keepdims=True)
                p = jnp.exp2(s - m).astype(BF16)
                o = mm(vt_ref[pl.ds(pl.multiple_of(head * AUG, 16), AUG), 0:ke], p)
                total = o[HEAD : HEAD + 1]
                ctx_ref[pl.ds(pl.multiple_of(head * HEAD, HEAD), HEAD), qs] = (
                    o[:HEAD] * (1.0 / total)
                ).astype(BF16)
                lse_ref[head, :, qs] = m + jnp.log2(total)


class Mover:
    def __init__(self, sems):
        self.sems, self.used, self.pending = sems, 0, {}

    def start(self, name, src, dst):
        copy = pltpu.make_async_copy(src, dst, self.sems.at[self.used])
        self.used += 1
        copy.start()
        self.pending[name] = copy

    def wait(self, *names):
        for name in names:
            self.pending.pop(name).wait()

    def finish(self):
        self.wait(*list(self.pending))


def meet(peers):
    barrier = pltpu.get_barrier_semaphore()
    for peer in peers:
        pl.semaphore_signal(barrier, inc=1, device_id=peer, device_id_type=pl.DeviceIdType.MESH)
    pl.semaphore_wait(barrier, len(peers))


def remote(src, dst, sends, recvs, index, peer):
    return pltpu.make_async_remote_copy(
        src_ref=src, dst_ref=dst, send_sem=sends.at[index], recv_sem=recvs.at[index],
        device_id=peer, device_id_type=pl.DeviceIdType.MESH,
    )


FWD_OUTS = 22


def forward_kernel(
    tok_ref, src_ref, cot_ref, tl_ref, sl_ref, vec_ref, wqkv_h, wso_h, wcq_h, wckv_h, wco_h,
    *rest,
):
    outs, rest = rest[:FWD_OUTS], rest[FWD_OUTS:]
    cot_out = outs[0]
    kept, rest = rest[: FWD_OUTS - 1], rest[FWD_OUTS - 1 :]
    (wqkv_ref, wso_ref, wcq_ref, wckv_ref, wco_ref, mask, mask2, vt, v2t, y1,
     sems, sends, recvs) = rest
    (x_ref, mem_ref, q_ref, qt_ref, k_ref, kt_ref, v_ref, ctx_ref, lse_ref, xh1_ref, rs1_ref,
     q2_ref, q2t_ref, k2_ref, k2t_ref, v2_ref, c2_ref, lse2_ref, y2_ref, xh2_ref, rs2_ref) = kept
    size, width = x_ref.shape
    src = mem_ref.shape[0]
    seq = tok_ref.shape[0]
    blocks = size // TB
    row = lax.axis_index("seq")
    mover = Mover(sems)
    mover.start("wqkv", wqkv_h, wqkv_ref)
    mover.start("wckv", wckv_h, wckv_ref)
    mover.start("wso", wso_h, wso_ref)
    mover.start("wcq", wcq_h, wcq_ref)
    mover.start("wco", wco_h, wco_ref)

    def place(block, length):
        return pl.ds(pl.multiple_of(block * length, length), length)

    peers = [{"seq": lax.rem(row + d, seq)} for d in range(1, seq)]
    meet(peers)

    def exchange(source, target, length, kind):
        copies = []
        for d in range(1, seq):
            to = lax.rem(row + d, seq)
            copy = remote(source.at[to], target.at[place(row, length)], sends, recvs, kind * seq + d, {"seq": to})
            copy.start()
            copies.append(copy)
        mover.start((kind, "own"), source.at[row], target.at[place(row, length)])
        return copies

    tok_copies = exchange(tok_ref, x_ref, TB, 0)
    mem_copies = exchange(src_ref, mem_ref, src // seq, 1)

    def vec(i):
        return vec_ref[i : i + 1, :]

    for head in range(HEADS):
        vt[head * AUG + HEAD : (head + 1) * AUG, :] = jnp.ones((AUG - HEAD, size), BF16)
        v2t[head * AUG + HEAD : (head + 1) * AUG, :] = jnp.ones((AUG - HEAD, src), BF16)
    self_mask(mask, tl_ref[...], row, size)
    cross_mask(mask2, tl_ref[...], sl_ref[...], row, size, src)

    def put_vt(ref, values, place):
        for head in range(HEADS):
            ref[head * AUG : head * AUG + HEAD, place] = values[head * HEAD : (head + 1) * HEAD]

    mover.wait("wqkv", (0, "own"))
    for d in range(seq):
        if d:
            tok_copies[d - 1].wait_recv()
        ts = place(lax.rem(row + seq - d, seq), TB)
        xb = x_ref[ts, :]
        q = ((mm(xb, wqkv_ref[:, :width]) + vec(V_Q)) * (SCALE * LOG2E)).astype(BF16)
        q_ref[ts, :] = q
        qt_ref[:, ts] = q.T
        k = mm(xb, wqkv_ref[:, width : 2 * width]).astype(BF16)
        k_ref[ts, :] = k
        kt_ref[:, ts] = k.T
        v = (mm(xb, wqkv_ref[:, 2 * width :]) + vec(V_V)).astype(BF16)
        v_ref[ts, :] = v
        put_vt(vt, v.T, ts)
    mover.wait("wckv", (1, "own"))
    for copy in mem_copies:
        copy.wait_recv()
    cot_copies = exchange(cot_ref, cot_out, TB, 2)
    for i in (0, 1, 2, 3, 4, 5, 6):
        mover.start(i, kept[i], outs[1 + i])
    k2 = mm(mem_ref[...], wckv_ref[:, :width]).astype(BF16)
    k2_ref[...] = k2
    k2t_ref[...] = k2.T
    v2 = (mm(mem_ref[...], wckv_ref[:, width:]) + vec(V_CV)).astype(BF16)
    v2_ref[...] = v2
    put_vt(v2t, v2.T, slice(None))
    for i in (13, 14, 15):
        mover.start(i, kept[i], outs[1 + i])

    row_attend(k_ref, qt_ref, vt, mask, ctx_ref, lse_ref, size, lambda qb: (qb + 1) * TB)
    for i in (7, 8):
        mover.start(i, kept[i], outs[1 + i])
    mover.wait("wso", "wcq")
    for tb in range(blocks):
        ts = slice(tb * TB, (tb + 1) * TB)
        h1 = x_ref[ts, :].astype(F32) + mm(ctx_ref[:, ts].T, wso_ref[...]) + vec(V_SO)
        xh, rstd = normalize(h1)
        xh1_ref[ts, :] = xh.astype(BF16)
        rs1_ref[ts, :] = rstd
        yb = xh * vec(V_G) + vec(V_B)
        y1[ts, :] = yb
        q2 = ((mm(yb.astype(BF16), wcq_ref[...]) + vec(V_CQ)) * (SCALE * LOG2E)).astype(BF16)
        q2_ref[ts, :] = q2
        q2t_ref[:, ts] = q2.T
    for i in (9, 10, 11, 12):
        mover.start(i, kept[i], outs[1 + i])
    row_attend(k2_ref, q2t_ref, v2t, mask2, c2_ref, lse2_ref, size, lambda qb: src)
    for i in (16, 17):
        mover.start(i, kept[i], outs[1 + i])
    mover.wait("wco")
    for tb in range(blocks):
        ts = slice(tb * TB, (tb + 1) * TB)
        h2 = y1[ts, :] + mm(c2_ref[:, ts].T, wco_ref[...]) + vec(V_CO)
        xh, rstd = normalize(h2)
        xh2_ref[ts, :] = xh.astype(BF16)
        rs2_ref[ts, :] = rstd
        y2_ref[ts, :] = xh * vec(V_G + 1) + vec(V_B + 1)
        for i in (18, 19, 20):
            mover.start((i, tb), kept[i].at[ts], outs[1 + i].at[ts])
    for copy in cot_copies:
        copy.wait_recv()
    for copy in tok_copies + mem_copies + cot_copies:
        copy.wait_send()
    mover.finish()


def ffn_kernel(
    y2_ref, xh2_ref, rs2_ref, cot_ref, vec_ref, win_ref, wout_ref,
    out_ref, dh2_ref, dwin_ref, dwout_ref, dvec_ref,
    a_s, du_s, slope_s, y2b_s, dz_s,
):
    size, width = y2_ref.shape
    inner = win_ref.shape[1]
    cols = [slice(j, j + width) for j in range(0, inner, width)]

    def vec(i):
        return vec_ref[i : i + 1, :]

    dvec_ref[...] = jnp.zeros_like(dvec_ref)

    @pl.loop(0, size // TB)
    def _(tb):
        ts = pl.ds(pl.multiple_of(tb * TB, TB), TB)
        y2 = y2_ref[ts, :]
        y2b = y2.astype(BF16)
        y2b_s[ts, :] = y2b
        h3 = y2 + vec(V_FO)
        for j, cs in enumerate(cols):
            u = mm(y2b, win_ref[:, cs]) + vec(V_FI + j)
            sg = 0.5 * jnp.tanh(0.5 * u) + 0.5
            act = u * sg
            slope_s[:, cs] = sg + act * (1.0 - sg)
            act = act.astype(BF16)
            a_s[ts, cs] = act
            h3 = h3 + mm(act, wout_ref[cs, :])
        xh, rstd = normalize(h3)
        out_ref[ts, :] = (xh * vec(V_G + 2) + vec(V_B + 2)).astype(BF16)
        grad = cot_ref[ts, :].astype(F32)
        dh3, dg, db = norm_back(grad, xh, rstd, vec(V_G + 2))
        dz = dh3.astype(BF16)
        dz_s[ts, :] = dz
        dvec_ref[V_G + 2 : V_G + 3, :] += dg
        dvec_ref[V_B + 2 : V_B + 3, :] += db
        dvec_ref[V_FO : V_FO + 1, :] += jnp.sum(dz.astype(F32), axis=0, keepdims=True)
        dy2 = dh3
        for j, cs in enumerate(cols):
            du = (mm(dz, wout_ref[cs, :], 1, 1) * slope_s[:, cs]).astype(BF16)
            du_s[ts, cs] = du
            dvec_ref[V_FI + j : V_FI + j + 1, :] += jnp.sum(du.astype(F32), axis=0, keepdims=True)
            dy2 = dy2 + mm(du, win_ref[:, cs], 1, 1)
        xh2 = xh2_ref[ts, :].astype(F32)
        dh2, dg, db = norm_back(dy2, xh2, rs2_ref[ts, :], vec(V_G + 1))
        dh2_ref[ts, :] = dh2
        dvec_ref[V_G + 1 : V_G + 2, :] += dg
        dvec_ref[V_B + 1 : V_B + 2, :] += db

    for j, cs in enumerate(cols):
        dwin_ref[j * width : (j + 1) * width, :] = mm(y2b_s[...], du_s[:, cs], 0, 0).astype(BF16)
        dwout_ref[cs, :] = mm(a_s[:, cs], dz_s[...], 0, 0).astype(BF16)


def row_attend_back(
    k_ref, kt_ref, v_ref, q_ref, qt_ref, dc_ref, dct_ref, ctx_ref, lse_ref, mask_ref,
    delta, dqt, dq_ref, dk_ref, dv_ref, size, keys, query_start,
):
    @pl.loop(0, HEADS // 2)
    def _(pair):
        lanes = pl.ds(pl.multiple_of(pair * 2 * HEAD, 2 * HEAD), 2 * HEAD)
        both = dct_ref[lanes, :].astype(F32) * ctx_ref[lanes, :].astype(F32)
        for half in range(2):
            delta[half] = jnp.sum(both[half * HEAD : (half + 1) * HEAD], axis=0, keepdims=True)
        dqt[...] = jnp.zeros_like(dqt)
        for kb in range(keys // TB):
            ks, qs = slice(kb * TB, (kb + 1) * TB), slice(query_start(kb), size)
            dks, dvs = [], []
            for half in range(2):
                head = pair * 2 + half
                rows = pl.ds(pl.multiple_of(head * HEAD, HEAD), HEAD)
                s = mm(k_ref[ks, lanes], half_of(qt_ref[lanes, qs], half))
                p = jnp.exp2(s + mask_ref[ks, qs] - lse_ref[head, :, qs])
                dp = mm(v_ref[ks, lanes], half_of(dct_ref[lanes, qs], half))
                ds = (p * (dp - delta[half, :, qs])).astype(BF16)
                dvs.append(mm(p.astype(BF16), dc_ref[qs, lanes]))
                dks.append(mm(ds, q_ref[qs, lanes]))
                dqt[half * HEAD : (half + 1) * HEAD, qs] += mm(kt_ref[rows, ks], ds)
            first = lax.broadcasted_iota(jnp.int32, (TB, 2 * HEAD), 1) < HEAD
            dv_ref[ks, lanes] = jnp.where(first, dvs[0], dvs[1]).astype(BF16)
            dk_ref[ks, lanes] = (jnp.where(first, dks[0], dks[1]) * (1.0 / LOG2E)).astype(BF16)
        dq_ref[:, lanes] = (dqt[...] * SCALE).astype(BF16).T


def backward_kernel(
    row_of, dh2_ref, x_ref, mem_ref, tl_ref, sl_ref, vec_ref,
    wqkv_ref, wso_ref, wcq_ref, wckv_ref, wco_ref,
    q_ref, qt_ref, k_ref, kt_ref, v_ref, ctx_ref, lse_ref, xh1_ref, rs1_ref,
    q2_ref, q2t_ref, k2_ref, k2t_ref, v2_ref, c2_ref, lse2_ref,
    dtok_ref, dmem_ref, dw_ref, dvec_ref,
    mask, mask2, delta, dqt, dc, dct, dq, dk, dv, dk2, dv2, dh1, y1b,
):
    size, width = x_ref.shape
    src = mem_ref.shape[0]
    blocks = [slice(t, t + TB) for t in range(0, size, TB)]
    row = row_of()

    def vec(i):
        return vec_ref[i : i + 1, :]

    def total(values):
        return jnp.sum(values.astype(F32), axis=0, keepdims=True)

    dvec_ref[...] = jnp.zeros_like(dvec_ref)
    self_mask(mask, tl_ref[...], row, size)
    cross_mask(mask2, tl_ref[...], sl_ref[...], row, size, src)
    da = dh1
    for ts in blocks:
        da2 = dh2_ref[ts, :].astype(BF16)
        dc[ts, :] = mm(da2, wco_ref[...], 1, 1).astype(BF16)
        dct[:, ts] = mm(wco_ref[...], da2, 1, 1).astype(BF16)
        dvec_ref[V_CO : V_CO + 1, :] += total(da2)
    da2 = dh2_ref[...].astype(BF16)
    dw_ref[0:width, :] = mm(c2_ref[...], da2).astype(BF16)
    row_attend_back(
        k2_ref, k2t_ref, v2_ref, q2_ref, q2t_ref, dc, dct, c2_ref, lse2_ref, mask2,
        delta, dqt, dq, dk2, dv2, size, src, lambda kb: 0,
    )
    dvec_ref[V_CV : V_CV + 1, :] = total(dv2[...])
    dvec_ref[V_CQ : V_CQ + 1, :] = total(dq[...])
    dw_ref[2 * width : 3 * width, :] = mm(mem_ref[...], dk2[...], 0, 0).astype(BF16)
    dw_ref[3 * width : 4 * width, :] = mm(mem_ref[...], dv2[...], 0, 0).astype(BF16)
    dmem_ref[...] = (
        mm(dk2[...], wckv_ref[:, :width], 1, 1) + mm(dv2[...], wckv_ref[:, width:], 1, 1)
    ).astype(BF16)
    for ts in blocks:
        dqb = dq[ts, :]
        dy1 = dh2_ref[ts, :] + mm(dqb, wcq_ref[...], 1, 1)
        xh1 = xh1_ref[ts, :].astype(F32)
        y1b[ts, :] = (xh1 * vec(V_G) + vec(V_B)).astype(BF16)
        dh, dg, db = norm_back(dy1, xh1, rs1_ref[ts, :], vec(V_G))
        dvec_ref[V_G : V_G + 1, :] += dg
        dvec_ref[V_B : V_B + 1, :] += db
        dh1[ts, :] = dh
        da1 = dh.astype(BF16)
        dvec_ref[V_SO : V_SO + 1, :] += total(da1)
    dw_ref[width : 2 * width, :] = mm(y1b[...], dq[...], 0, 0).astype(BF16)
    for ts in blocks:
        da1 = dh1[ts, :].astype(BF16)
        dc[ts, :] = mm(da1, wso_ref[...], 1, 1).astype(BF16)
        dct[:, ts] = mm(wso_ref[...], da1, 1, 1).astype(BF16)
    dw_ref[4 * width : 5 * width, :] = mm(ctx_ref[...], dh1[...].astype(BF16)).astype(BF16)
    row_attend_back(
        k_ref, kt_ref, v_ref, q_ref, qt_ref, dc, dct, ctx_ref, lse_ref, mask,
        delta, dqt, dq, dk, dv, size, size, lambda kb: kb * TB,
    )
    dvec_ref[V_Q : V_Q + 1, :] = total(dq[...])
    dvec_ref[V_V : V_V + 1, :] = total(dv[...])
    for i, part in enumerate((dq, dk, dv)):
        dw_ref[(5 + i) * width : (6 + i) * width, :] = mm(x_ref[...], part[...], 0, 0).astype(BF16)
    for ts in blocks:
        dtok_ref[ts, :] = (
            dh1[ts, :]
            + mm(dq[ts, :], wqkv_ref[:, :width], 1, 1)
            + mm(dk[ts, :], wqkv_ref[:, width : 2 * width], 1, 1)
            + mm(dv[ts, :], wqkv_ref[:, 2 * width :], 1, 1)
        ).astype(BF16)


WHOLE = pl.BlockSpec(memory_space=pltpu.VMEM)


def call(kernel, ins, outs, scratch, name):
    return pl.pallas_call(
        kernel,
        out_shape=[jax.ShapeDtypeStruct(*o) for o in outs],
        in_specs=[WHOLE] * len(ins),
        out_specs=[WHOLE] * len(outs),
        scratch_shapes=[pltpu.VMEM(*s) for s in scratch],
        compiler_params=pltpu.CompilerParams(vmem_limit_bytes=60 * 2**20),
        name=name,
    )(*ins)


ANY = pl.BlockSpec(memory_space=pl.ANY)


def forward(tokens, memory, cot, tl, sl, vecs, wqkv, wso, wcq, wckv, wco):
    seq, block, d = tokens.shape
    t, s = seq * block, seq * memory.shape[1]
    tok, feat, row = ((t, d), BF16), ((d, t), BF16), ((HEADS, 1, t), F32)
    col, mem = ((t, 1), F32), ((s, d), BF16)
    kept = [tok, mem, tok, feat, tok, feat, tok, feat, row, tok, col,
            tok, feat, mem, ((d, s), BF16), mem, feat, row, ((t, d), F32), tok, col]
    weights = (wqkv, wso, wcq, wckv, wco)
    scratch = kept + [(w.shape, w.dtype) for w in weights]
    scratch += [((t, t), F32), ((s, t), F32), ((HEADS * AUG, t), BF16), ((HEADS * AUG, s), BF16), ((t, d), F32)]
    return pl.pallas_call(
        forward_kernel,
        out_shape=[jax.ShapeDtypeStruct(*o) for o in [tok] + kept],
        in_specs=[ANY] * 3 + [WHOLE] * 3 + [ANY] * 5,
        out_specs=[ANY] * FWD_OUTS,
        scratch_shapes=[pltpu.VMEM(*x) for x in scratch]
        + [pltpu.SemaphoreType.DMA((40,)), pltpu.SemaphoreType.DMA((3 * seq,)), pltpu.SemaphoreType.DMA((3 * seq,))],
        compiler_params=pltpu.CompilerParams(vmem_limit_bytes=60 * 2**20, collective_id=0, has_side_effects=True),
        name="forward",
    )(tokens, memory, cot, tl, sl, vecs, *weights)


def ffn(y2, xh2, rs2, cot, vecs, win, wout):
    (t, d), f = y2.shape, win.shape[1]
    return call(
        ffn_kernel,
        (y2, xh2, rs2, cot, vecs, win, wout),
        [((t, d), BF16), ((t, d), F32), ((f, d), BF16), ((f, d), BF16), ((VECS, d), F32)],
        [((t, f), BF16), ((t, f), BF16), ((TB, f), F32), ((t, d), BF16), ((t, d), BF16)],
        "ffn",
    )


def backward(row_of, dh2, x, mem, tl, sl, vecs, wqkv, wso, wcq, wckv, wco, *saved):
    (t, d), s = x.shape, mem.shape[0]
    tok = ((t, d), BF16)
    return call(
        functools.partial(backward_kernel, row_of),
        (dh2, x, mem, tl, sl, vecs, wqkv, wso, wcq, wckv, wco) + saved,
        [tok, ((s, d), BF16), ((8 * d, d), BF16), ((VECS, d), F32)],
        [((t, t), F32), ((s, t), F32), ((2, 1, t), F32), ((2 * HEAD, t), F32), tok, ((d, t), BF16),
         tok, tok, tok, ((s, d), BF16), ((s, d), BF16), ((t, d), F32), tok],
        "backward",
    )


def pack_vecs(qv_bias, so, cq, cv, co, fi, fo, gains, shifts):
    d = so.shape[0]
    parts = [qv_bias, so, cq, cv, co, fi, fo, gains.reshape(-1), shifts.reshape(-1)]
    flat = jnp.concatenate([p.astype(F32) for p in parts])
    return jnp.pad(flat, (0, VECS * d - flat.shape[0])).reshape(VECS, d)


def row_layer(tokens, memory, tl, sl, cotangent, w_qkv, qv_bias, self_out, self_out_bias, cross_query, cross_q_bias, cross_kv, cross_v_bias, cross_out, cross_out_bias, ffn_in, ffn_in_bias, ffn_out, ffn_out_bias, norm_gains, norm_biases):
    vecs = pack_vecs(qv_bias, self_out_bias, cross_q_bias, cross_v_bias, cross_out_bias, ffn_in_bias, ffn_out_bias, norm_gains, norm_biases)
    cot, x, mem, *saved, y2, xh2, rs2 = forward(tokens, memory, cotangent, tl, sl, vecs, w_qkv, self_out, cross_query, cross_kv, cross_out)
    out, dh2, dwin, dwout, dvec_a = ffn(y2, xh2, rs2, cot, vecs, ffn_in, ffn_out)
    dtok, dmem, dw, dvec_b = backward(lambda: lax.axis_index("seq"), dh2, x, mem, tl, sl, vecs, w_qkv, self_out, cross_query, cross_kv, cross_out, *saved)
    return out, dtok, dmem, dwin, dwout, dw, dvec_a + dvec_b


def unpack(dwin, dwout, dw, dvec):
    d = dw.shape[1]
    f = dwout.shape[0]
    w = [dw[i * d:(i + 1) * d].astype(F32) for i in range(8)]
    v = dvec.reshape(-1).astype(F32)
    d_ffn_in = jnp.concatenate([dwin[i * d:(i + 1) * d] for i in range(f // d)], axis=1).astype(F32)
    return (
        jnp.concatenate(w[5:8], axis=1), v[:2 * d], w[4], v[2 * d:3 * d], w[1], v[3 * d:4 * d],
        jnp.concatenate(w[2:4], axis=1), v[4 * d:5 * d], w[0], v[5 * d:6 * d], d_ffn_in, v[6 * d:10 * d],
        dwout.astype(F32), v[10 * d:11 * d], v[11 * d:14 * d].reshape(3, d), v[14 * d:17 * d].reshape(3, d),
    )


def layer_norm(values, gain, shift):
    center = values - jnp.mean(values, axis=-1, keepdims=True)
    spread = jnp.mean(center * center, axis=-1, keepdims=True)
    return center * lax.rsqrt(spread + 1e-05) * gain + shift


def doc_ids(lengths, size):
    ends = jnp.cumsum(lengths, axis=1)
    places = jnp.arange(size, dtype=jnp.int32)
    return jnp.sum((ends[:, None, :] <= places[None, :, None]).astype(jnp.int32), axis=2)


def block_width(key_total):
    return 512 if key_total % 512 == 0 else key_total


def contract_rows(left, right):
    return lax.dot_general(
        left, right, (((0,), (0,)), ((), ())), preferred_element_type=jnp.float32
    )


def contract_cols(left, right):
    return lax.dot_general(
        left, right, (((1,), (1,)), ((), ())), preferred_element_type=jnp.float32
    )


def block_scores(queries, keys, allowed, start_at, width_of, score_scale):
    key_block = lax.dynamic_slice_in_dim(keys, start_at, width_of, 1)
    scores = (
        jnp.einsum("rqhd,rkhd->rhqk", queries, key_block, preferred_element_type=jnp.float32)
        * score_scale
    )
    return jnp.where(allowed(start_at, width_of)[:, None], scores, -1000000000.0)


def attend_forward(queries, keys, values, allowed, skip_after, score_scale):
    row_count, query_count, head_count, head_size = queries.shape
    key_total = keys.shape[1]
    width_of = block_width(key_total)
    block_count = key_total // width_of

    def statistics(carried, block_index):
        start_at = block_index * width_of

        def statistics_work(state):
            running_max, running_sum = state
            scores = block_scores(queries, keys, allowed, start_at, width_of, score_scale)
            new_max = jnp.maximum(running_max, jnp.max(scores, axis=3))
            new_sum = running_sum * jnp.exp(running_max - new_max) + jnp.sum(
                jnp.exp(scores - new_max[..., None]), axis=3
            )
            return (new_max, new_sum)

        return (
            lax.cond(start_at > skip_after, lambda state: state, statistics_work, carried),
            None,
        )

    stat_shape = (row_count, head_count, query_count)
    start_state = (
        jnp.full(stat_shape, -1000000000.0, jnp.float32),
        jnp.zeros(stat_shape, jnp.float32),
    )
    block_numbers = jnp.arange(block_count, dtype=jnp.int32)
    (running_max, running_sum), _ = lax.scan(statistics, start_state, block_numbers)
    log_total = running_max + jnp.log(running_sum)

    def mixing(carried, block_index):
        start_at = block_index * width_of

        def mixing_work(accum):
            scores = block_scores(queries, keys, allowed, start_at, width_of, score_scale)
            probs = jnp.exp(scores - log_total[..., None]).astype(jnp.bfloat16)
            value_block = lax.dynamic_slice_in_dim(values, start_at, width_of, 1)
            return accum + jnp.einsum(
                "rhqk,rkhd->rqhd", probs, value_block, preferred_element_type=jnp.float32
            )

        return (lax.cond(start_at > skip_after, lambda accum: accum, mixing_work, carried), None)

    start_accum = jnp.zeros((row_count, query_count, head_count, head_size), jnp.float32)
    accum, _ = lax.scan(mixing, start_accum, block_numbers)
    return (accum, log_total)


def attend_back(
    queries, keys, values, allowed, skip_after, score_scale, log_total, grad_out, delta
):
    row_count, query_count, head_count, head_size = queries.shape
    key_total = keys.shape[1]
    width_of = block_width(key_total)
    block_count = key_total // width_of

    def step(block_index, state):
        start_at = block_index * width_of

        def step_work(inner):
            scores = block_scores(queries, keys, allowed, start_at, width_of, score_scale)
            probs = jnp.exp(scores - log_total[..., None])
            key_block = lax.dynamic_slice_in_dim(keys, start_at, width_of, 1)
            value_block = lax.dynamic_slice_in_dim(values, start_at, width_of, 1)
            grad_probs = jnp.einsum(
                "rqhd,rkhd->rhqk", grad_out, value_block, preferred_element_type=jnp.float32
            )
            grad_scores = (probs * (grad_probs - delta[..., None])).astype(jnp.bfloat16)
            grad_query = (
                inner[0]
                + jnp.einsum(
                    "rhqk,rkhd->rqhd", grad_scores, key_block, preferred_element_type=jnp.float32
                )
                * score_scale
            )
            key_part = (
                jnp.einsum(
                    "rhqk,rqhd->rkhd", grad_scores, queries, preferred_element_type=jnp.float32
                )
                * score_scale
            )
            value_part = jnp.einsum(
                "rhqk,rqhd->rkhd",
                probs.astype(jnp.bfloat16),
                grad_out,
                preferred_element_type=jnp.float32,
            )
            grad_keys = lax.dynamic_update_slice_in_dim(inner[1], key_part, start_at, 1)
            grad_values = lax.dynamic_update_slice_in_dim(inner[2], value_part, start_at, 1)
            return (grad_query, grad_keys, grad_values)

        return lax.cond(start_at > skip_after, lambda inner: inner, step_work, state)

    start_state = (jnp.zeros((row_count, query_count, head_count, head_size), jnp.float32),)
    start_state = start_state + (
        jnp.zeros((row_count, key_total, head_count, head_size), jnp.float32),
        jnp.zeros((row_count, key_total, head_count, head_size), jnp.float32),
    )
    return lax.fori_loop(0, block_count, step, start_state)


def blocks_on_device(
    tokens,
    memory,
    doc_lengths,
    src_lengths,
    cotangent,
    w_qkv,
    qv_bias,
    self_out,
    self_out_bias,
    cross_query,
    cross_q_bias,
    cross_kv,
    cross_v_bias,
    cross_out,
    cross_out_bias,
    ffn_in,
    ffn_in_bias,
    ffn_out,
    ffn_out_bias,
    norm_gains,
    norm_biases,
):
    row_count, block_len, model_width = tokens.shape
    src_block = memory.shape[1]
    seq_count = lax.axis_size("seq")
    row_length = block_len * seq_count
    src_length = src_block * seq_count
    score_scale = HEAD ** (-0.5)
    first_place = lax.axis_index("seq") * block_len
    last_place = first_place + block_len - 1
    target_ids = doc_ids(doc_lengths, row_length)
    source_ids = doc_ids(src_lengths, src_length)
    own_ids = lax.dynamic_slice_in_dim(target_ids, first_place, block_len, 1)
    own_places = first_place + jnp.arange(block_len, dtype=jnp.int32)

    def self_allowed(start_at, width_of):
        key_ids = lax.dynamic_slice_in_dim(target_ids, start_at, width_of, 1)
        key_places = start_at + jnp.arange(width_of, dtype=jnp.int32)
        return (own_ids[:, :, None] == key_ids[:, None, :]) & (
            key_places[None, None, :] <= own_places[None, :, None]
        )

    def cross_allowed(start_at, width_of):
        return (own_ids[:, :, None] == source_ids[:, None, :]) | (own_ids[:, :, None] == NDOC)

    def split_heads(array_in):
        return array_in.reshape(array_in.shape[0], array_in.shape[1], HEADS, HEAD)

    token_rows = row_count * block_len
    flat_tokens = tokens.reshape(token_rows, model_width)
    flat_memory = memory.reshape(row_count * src_block, model_width)
    pair_bias = qv_bias.astype(jnp.float32)
    gains = norm_gains.astype(jnp.float32)
    shifts = norm_biases.astype(jnp.float32)
    packed = jnp.dot(flat_tokens, w_qkv, preferred_element_type=jnp.float32)
    self_queries = (packed[:, :model_width] + pair_bias[:model_width]).astype(jnp.bfloat16)
    self_keys = (
        packed[:, model_width : 2 * model_width]
        .astype(jnp.bfloat16)
        .reshape(row_count, block_len, model_width)
    )
    self_values = (
        (packed[:, 2 * model_width :] + pair_bias[model_width:])
        .astype(jnp.bfloat16)
        .reshape(row_count, block_len, model_width)
    )
    memory_pair = jnp.dot(flat_memory, cross_kv, preferred_element_type=jnp.float32)
    cross_keys = (
        memory_pair[:, :model_width].astype(jnp.bfloat16).reshape(row_count, src_block, model_width)
    )
    cross_values = (
        (memory_pair[:, model_width:] + cross_v_bias.astype(jnp.float32))
        .astype(jnp.bfloat16)
        .reshape(row_count, src_block, model_width)
    )
    all_keys, all_values, all_ckeys, all_cvalues = (
        lax.all_gather(self_keys, "seq", axis=1, tiled=True),
        lax.all_gather(self_values, "seq", axis=1, tiled=True),
        lax.all_gather(cross_keys, "seq", axis=1, tiled=True),
        lax.all_gather(cross_values, "seq", axis=1, tiled=True),
    )
    query_heads = split_heads(self_queries.reshape(row_count, block_len, model_width))
    self_accum, self_log = attend_forward(
        query_heads,
        split_heads(all_keys),
        split_heads(all_values),
        self_allowed,
        last_place,
        score_scale,
    )
    context_low = self_accum.reshape(token_rows, model_width).astype(jnp.bfloat16)
    inputs_f = flat_tokens.astype(jnp.float32)
    first_sum = (
        inputs_f
        + jnp.dot(context_low, self_out, preferred_element_type=jnp.float32)
        + self_out_bias.astype(jnp.float32)
    )
    first_norm, first_pull = jax.vjp(layer_norm, first_sum, gains[0], shifts[0])
    first_low = first_norm.astype(jnp.bfloat16)
    cross_q_rows = (
        jnp.dot(first_low, cross_query, preferred_element_type=jnp.float32)
        + cross_q_bias.astype(jnp.float32)
    ).astype(jnp.bfloat16)
    cross_heads = split_heads(cross_q_rows.reshape(row_count, block_len, model_width))
    cross_accum, cross_log = attend_forward(
        cross_heads,
        split_heads(all_ckeys),
        split_heads(all_cvalues),
        cross_allowed,
        src_length,
        score_scale,
    )
    cross_low = cross_accum.reshape(token_rows, model_width).astype(jnp.bfloat16)
    second_sum = (
        first_norm
        + jnp.dot(cross_low, cross_out, preferred_element_type=jnp.float32)
        + cross_out_bias.astype(jnp.float32)
    )
    second_norm, second_pull = jax.vjp(layer_norm, second_sum, gains[1], shifts[1])
    second_low = second_norm.astype(jnp.bfloat16)
    hidden_pre = jnp.dot(
        second_low, ffn_in, preferred_element_type=jnp.float32
    ) + ffn_in_bias.astype(jnp.float32)
    hidden_low = jax.nn.silu(hidden_pre).astype(jnp.bfloat16)
    third_sum = (
        second_norm
        + jnp.dot(hidden_low, ffn_out, preferred_element_type=jnp.float32)
        + ffn_out_bias.astype(jnp.float32)
    )
    result, third_pull = jax.vjp(layer_norm, third_sum, gains[2], shifts[2])
    output = result.astype(jnp.bfloat16).reshape(row_count, block_len, model_width)
    grad_third, gain_three, shift_three = third_pull(
        cotangent.reshape(token_rows, model_width).astype(jnp.float32)
    )
    grad_branch = grad_third.astype(jnp.bfloat16)
    d_ffn_out = contract_rows(hidden_low, grad_branch)
    d_ffn_out_bias = jnp.sum(grad_branch.astype(jnp.float32), axis=0)
    grad_hidden = contract_cols(grad_branch, ffn_out)
    sigmoid_pre = jax.nn.sigmoid(hidden_pre)
    grad_pre = (grad_hidden * sigmoid_pre * (1.0 + hidden_pre * (1.0 - sigmoid_pre))).astype(
        jnp.bfloat16
    )
    d_ffn_in = contract_rows(second_low, grad_pre)
    d_ffn_in_bias = jnp.sum(grad_pre.astype(jnp.float32), axis=0)
    grad_second_norm = grad_third + contract_cols(grad_pre, ffn_in)
    back_keys, back_values, back_ckeys, back_cvalues = (
        all_keys,
        all_values,
        all_ckeys,
        all_cvalues,
    )
    grad_second, gain_two, shift_two = second_pull(grad_second_norm)
    grad_cross_branch = grad_second.astype(jnp.bfloat16)
    d_cross_out = contract_rows(cross_low, grad_cross_branch)
    d_cross_out_bias = jnp.sum(grad_cross_branch.astype(jnp.float32), axis=0)
    grad_cross_ctx = contract_cols(grad_cross_branch, cross_out).astype(jnp.bfloat16)
    grad_cross_heads = split_heads(grad_cross_ctx.reshape(row_count, block_len, model_width))
    cross_delta = jnp.swapaxes(
        jnp.sum(grad_cross_heads.astype(jnp.float32) * cross_accum, axis=3), 1, 2
    )
    grad_cq, grad_ck_all, grad_cv_all = attend_back(
        cross_heads,
        split_heads(back_ckeys),
        split_heads(back_cvalues),
        cross_allowed,
        src_length,
        score_scale,
        cross_log,
        grad_cross_heads,
        cross_delta,
    )
    grad_ck_own, grad_cv_own = (
        lax.psum_scatter(
            grad_ck_all.reshape(row_count, src_length, model_width).astype(jnp.bfloat16),
            "seq",
            scatter_dimension=1,
            tiled=True,
        ).astype(jnp.float32),
        lax.psum_scatter(
            grad_cv_all.reshape(row_count, src_length, model_width).astype(jnp.bfloat16),
            "seq",
            scatter_dimension=1,
            tiled=True,
        ).astype(jnp.float32),
    )
    grad_pair = jnp.concatenate(
        [
            grad_ck_own.reshape(row_count * src_block, model_width).astype(jnp.bfloat16),
            grad_cv_own.reshape(row_count * src_block, model_width).astype(jnp.bfloat16),
        ],
        axis=1,
    )
    d_cross_kv = contract_rows(flat_memory, grad_pair)
    d_cross_v_bias = jnp.sum(grad_pair[:, model_width:].astype(jnp.float32), axis=0)
    d_memory = contract_cols(grad_pair, cross_kv).reshape(row_count, src_block, model_width)
    grad_cq_low = grad_cq.reshape(token_rows, model_width).astype(jnp.bfloat16)
    d_cross_query = contract_rows(first_low, grad_cq_low)
    d_cross_q_bias = jnp.sum(grad_cq_low.astype(jnp.float32), axis=0)
    grad_first_norm = grad_second + contract_cols(grad_cq_low, cross_query)
    grad_first, gain_one, shift_one = first_pull(grad_first_norm)
    grad_self_branch = grad_first.astype(jnp.bfloat16)
    d_self_out = contract_rows(context_low, grad_self_branch)
    d_self_out_bias = jnp.sum(grad_self_branch.astype(jnp.float32), axis=0)
    grad_context = contract_cols(grad_self_branch, self_out).astype(jnp.bfloat16)
    grad_context_heads = split_heads(grad_context.reshape(row_count, block_len, model_width))
    self_delta = jnp.swapaxes(
        jnp.sum(grad_context_heads.astype(jnp.float32) * self_accum, axis=3), 1, 2
    )
    grad_q, grad_k_all, grad_v_all = attend_back(
        query_heads,
        split_heads(back_keys),
        split_heads(back_values),
        self_allowed,
        last_place,
        score_scale,
        self_log,
        grad_context_heads,
        self_delta,
    )
    grad_k_own, grad_v_own = (
        lax.psum_scatter(
            grad_k_all.reshape(row_count, row_length, model_width).astype(jnp.bfloat16),
            "seq",
            scatter_dimension=1,
            tiled=True,
        ).astype(jnp.float32),
        lax.psum_scatter(
            grad_v_all.reshape(row_count, row_length, model_width).astype(jnp.bfloat16),
            "seq",
            scatter_dimension=1,
            tiled=True,
        ).astype(jnp.float32),
    )
    grad_k_flat = grad_k_own.reshape(token_rows, model_width)
    grad_v_flat = grad_v_own.reshape(token_rows, model_width)
    grad_q_low = grad_q.reshape(token_rows, model_width).astype(jnp.bfloat16)
    grad_v_low = grad_v_flat.astype(jnp.bfloat16)
    grad_proj = jnp.concatenate([grad_q_low, grad_k_flat.astype(jnp.bfloat16), grad_v_low], axis=1)
    d_w_qkv = contract_rows(flat_tokens, grad_proj)
    d_qv_bias = jnp.concatenate(
        [
            jnp.sum(grad_q_low.astype(jnp.float32), axis=0),
            jnp.sum(grad_v_low.astype(jnp.float32), axis=0),
        ]
    )
    d_tokens = (grad_first + contract_cols(grad_proj, w_qkv)).reshape(
        row_count, block_len, model_width
    )
    d_norm_gains = jnp.stack([gain_one, gain_two, gain_three])
    d_norm_biases = jnp.stack([shift_one, shift_two, shift_three])
    (
        d_w_qkv,
        d_qv_bias,
        d_self_out,
        d_self_out_bias,
        d_cross_query,
        d_cross_q_bias,
        d_cross_kv,
        d_cross_v_bias,
        d_cross_out,
        d_cross_out_bias,
        d_ffn_in,
        d_ffn_in_bias,
        d_ffn_out,
        d_ffn_out_bias,
        d_norm_gains,
        d_norm_biases,
    ) = lax.psum(
        (
            d_w_qkv,
            d_qv_bias,
            d_self_out,
            d_self_out_bias,
            d_cross_query,
            d_cross_q_bias,
            d_cross_kv,
            d_cross_v_bias,
            d_cross_out,
            d_cross_out_bias,
            d_ffn_in,
            d_ffn_in_bias,
            d_ffn_out,
            d_ffn_out_bias,
            d_norm_gains,
            d_norm_biases,
        ),
        ("dp", "seq"),
    )
    return (
        output,
        d_tokens,
        d_memory,
        d_w_qkv,
        d_qv_bias,
        d_self_out,
        d_self_out_bias,
        d_cross_query,
        d_cross_q_bias,
        d_cross_kv,
        d_cross_v_bias,
        d_cross_out,
        d_cross_out_bias,
        d_ffn_in,
        d_ffn_in_bias,
        d_ffn_out,
        d_ffn_out_bias,
        d_norm_gains,
        d_norm_biases,
    )


def rows_on_device(tokens, memory, doc_lengths, src_lengths, cotangent, *params):
    row_count, block_len, width = tokens.shape

    def to_blocks(row):
        return lax.all_to_all(row[None], "seq", split_axis=1, concat_axis=0, tiled=True)

    out, dtok, dmem, dwin, dwout, dw, dvec = row_layer(tokens, memory, doc_lengths, src_lengths, cotangent, *params)
    packed = jnp.concatenate([dwin, dwout, dw, dvec.astype(BF16)], axis=0)
    packed = lax.psum(packed, ("dp", "seq"))
    f = dwout.shape[0]
    grads = unpack(packed[:f], packed[f : 2 * f], packed[2 * f : 2 * f + dw.shape[0]], packed[2 * f + dw.shape[0] :])
    return (to_blocks(out), to_blocks(dtok).astype(F32), to_blocks(dmem).astype(F32)) + grads


def on_device(tokens, *rest):
    if tokens.shape[0] == lax.axis_size("seq"):
        return rows_on_device(tokens, *rest)
    return blocks_on_device(tokens, *rest)


def solution(mesh):
    in_specs = (
        P("dp", "seq", None),
        P("dp", "seq", None),
        P("dp", None),
        P("dp", None),
        P("dp", "seq", None),
        P(),
        P(),
        P(),
        P(),
        P(),
        P(),
        P(),
        P(),
        P(),
        P(),
        P(),
        P(),
        P(),
        P(),
        P(),
        P(),
    )
    out_specs = (
        P("dp", "seq", None),
        P("dp", "seq", None),
        P("dp", "seq", None),
        P(),
        P(),
        P(),
        P(),
        P(),
        P(),
        P(),
        P(),
        P(),
        P(),
        P(),
        P(),
        P(),
        P(),
        P(),
        P(),
    )
    return jax.shard_map(
        on_device, mesh=mesh, in_specs=in_specs, out_specs=out_specs, check_vma=False
    )
```

```python
import functools
import jax
import jax.numpy as jnp
from jax import lax
from jax.experimental import pallas as pl
from jax.experimental.pallas import tpu as pltpu
from jax.sharding import PartitionSpec as P

HEADS = 8
HEAD = 64
NDOC = 32
AUG = HEAD + 16
MASKED = -1e9
LOG2E = 1.4426950408889634
SCALE = HEAD**-0.5
F32 = jnp.float32
BF16 = jnp.bfloat16
TB = 256

V_Q, V_V, V_SO, V_CQ, V_CV, V_CO, V_FI, V_FO, V_G, V_B = 0, 1, 2, 3, 4, 5, 6, 10, 11, 14
VECS = 24
G_IN, G_OUT, G_CO, G_CQ, G_CK, G_SO, G_QKV = 0, 4, 8, 9, 10, 12, 13
STREAMS = ((G_OUT, 4), (G_IN, 4), (G_CO, 5), (G_QKV, 3))
STEPS = 8
COPIES = (1, 2, 2, 6, 6, 2, 2, 1)
OWN = sum(COPIES)


def vec_of(ref, start, length):
    return ref[start : start + length].astype(F32).reshape(1, length)


def mm(left, right, lc=1, rc=0):
    return lax.dot_general(
        left, right, (((lc,), (rc,)), ((), ())), preferred_element_type=F32
    )


def row_ids(lengths, row, size):
    rows, docs = lengths.shape
    at_row = lax.broadcasted_iota(jnp.int32, (rows, docs), 0) == row
    own = jnp.sum(jnp.where(at_row, lengths.astype(F32), 0.0), axis=0, keepdims=True)
    own = jnp.broadcast_to(own, (docs, docs))
    down = lax.broadcasted_iota(jnp.int32, (docs, docs), 0)
    over = lax.broadcasted_iota(jnp.int32, (docs, docs), 1)
    ends_col = jnp.sum(jnp.where(over <= down, own, 0.0), axis=1, keepdims=True)
    own_col = jnp.sum(jnp.where(over == down, own, 0.0), axis=1, keepdims=True)
    ends_row = jnp.sum(
        jnp.where(down <= over, jnp.broadcast_to(own_col, (docs, docs)), 0.0),
        axis=0,
        keepdims=True,
    )
    place_row = lax.broadcasted_iota(jnp.int32, (docs, size), 1).astype(F32)
    place_col = lax.broadcasted_iota(jnp.int32, (size, docs), 0).astype(F32)
    ids_row = jnp.sum(jnp.where(ends_col <= place_row, 1.0, 0.0), axis=0, keepdims=True)
    ids_col = jnp.sum(jnp.where(ends_row <= place_col, 1.0, 0.0), axis=1, keepdims=True)
    return ids_row, ids_col


def self_mask(mask_ref, lengths, row, size):
    ids_row, ids_col = row_ids(lengths, row, size)
    for kb in range(size // TB):
        for qb in range(kb, size // TB):
            ks, qs = slice(kb * TB, (kb + 1) * TB), slice(qb * TB, (qb + 1) * TB)
            seen = ids_col[ks] == ids_row[:, qs]
            if kb == qb:
                down = lax.broadcasted_iota(jnp.int32, (TB, TB), 0)
                over = lax.broadcasted_iota(jnp.int32, (TB, TB), 1)
                seen = seen & (down <= over)
            mask_ref[ks, qs] = jnp.where(seen, 0.0, MASKED)


def cross_mask(mask_ref, lengths, src_lengths, row, size, src):
    ids_row, _ = row_ids(lengths, row, size)
    _, src_col = row_ids(src_lengths, row, src)
    for qb in range(size // TB):
        qs = slice(qb * TB, (qb + 1) * TB)
        seen = (src_col == ids_row[:, qs]) | (ids_row[:, qs] == float(NDOC))
        mask_ref[:, qs] = jnp.where(seen, 0.0, MASKED)


def half_of(values, half):
    down = lax.broadcasted_iota(jnp.int32, values.shape, 0)
    keep = (down >= HEAD) if half else (down < HEAD)
    return jnp.where(keep, values, jnp.zeros_like(values))


def normalize(h):
    center = h - jnp.mean(h, axis=-1, keepdims=True)
    spread = jnp.mean(center * center, axis=-1, keepdims=True)
    rstd = lax.rsqrt(spread + 1e-05)
    return center * rstd, rstd


def norm_back(grad, xh, rstd, gain):
    gs = grad * gain
    m1 = jnp.mean(gs, axis=-1, keepdims=True)
    m2 = jnp.mean(gs * xh, axis=-1, keepdims=True)
    dh = (gs - m1 - xh * m2) * rstd
    return (
        dh,
        jnp.sum(grad * xh, axis=0, keepdims=True),
        jnp.sum(grad, axis=0, keepdims=True),
    )


def row_attend(k_ref, qt_ref, vt_ref, mask_ref, ctx_ref, lse_ref, size, key_end):
    @pl.loop(0, HEADS // 2)
    def _(pair):
        lanes = pl.ds(pl.multiple_of(pair * 2 * HEAD, 2 * HEAD), 2 * HEAD)
        for half in range(2):
            head = pair * 2 + half
            for qb in range(size // TB):
                ke, qs = key_end(qb), slice(qb * TB, (qb + 1) * TB)
                s = mm(k_ref[0:ke, lanes], half_of(qt_ref[lanes, qs], half))
                s = s + mask_ref[0:ke, qs]
                m = jnp.max(s, axis=0, keepdims=True)
                p = jnp.exp2(s - m).astype(BF16)
                o = mm(vt_ref[pl.ds(pl.multiple_of(head * AUG, 16), AUG), 0:ke], p)
                total = o[HEAD : HEAD + 1]
                ctx_ref[pl.ds(pl.multiple_of(head * HEAD, HEAD), HEAD), qs] = (
                    o[:HEAD] * (1.0 / total)
                ).astype(BF16)
                lse_ref[head, :, qs] = m + jnp.log2(total)


class Mover:
    def __init__(self, sems):
        self.sems, self.used, self.pending = sems, 0, {}

    def start(self, name, src, dst):
        copy = pltpu.make_async_copy(src, dst, self.sems.at[self.used])
        self.used += 1
        copy.start()
        self.pending[name] = copy

    def wait(self, *names):
        for name in names:
            self.pending.pop(name).wait()

    def finish(self):
        self.wait(*list(self.pending))


def meet(peers):
    barrier = pltpu.get_barrier_semaphore()
    for peer in peers:
        pl.semaphore_signal(barrier, inc=1, device_id=peer, device_id_type=pl.DeviceIdType.MESH)
    pl.semaphore_wait(barrier, len(peers))


def remote(src, dst, sends, recvs, index, peer):
    return pltpu.make_async_remote_copy(
        src_ref=src, dst_ref=dst, send_sem=sends.at[index], recv_sem=recvs.at[index],
        device_id=peer, device_id_type=pl.DeviceIdType.MESH,
    )


FWD_OUTS = 22


def forward_kernel(
    tok_ref, src_ref, cot_ref, tl_ref, sl_ref, bqv, bso, bcq, bcv, bco, gains, shifts,
    wqkv_h, wso_h, wcq_h, wckv_h, wco_h, *rest,
):
    outs, rest = rest[:FWD_OUTS], rest[FWD_OUTS:]
    cot_out = outs[0]
    kept, rest = rest[: FWD_OUTS - 1], rest[FWD_OUTS - 1 :]
    (wqkv_ref, wso_ref, wcq_ref, wckv_ref, wco_ref, mask, mask2, vt, v2t, y1,
     sems, sends, recvs) = rest
    (x_ref, mem_ref, q_ref, qt_ref, k_ref, kt_ref, v_ref, ctx_ref, lse_ref, xh1_ref, rs1_ref,
     q2_ref, q2t_ref, k2_ref, k2t_ref, v2_ref, c2_ref, lse2_ref, y2_ref, xh2_ref, rs2_ref) = kept
    size, width = x_ref.shape
    src = mem_ref.shape[0]
    seq = tok_ref.shape[0]
    blocks = size // TB
    row = lax.axis_index("seq")
    mover = Mover(sems)
    mover.start("wqkv", wqkv_h, wqkv_ref)
    mover.start("wckv", wckv_h, wckv_ref)
    mover.start("wso", wso_h, wso_ref)
    mover.start("wcq", wcq_h, wcq_ref)
    mover.start("wco", wco_h, wco_ref)

    def place(block, length):
        return pl.ds(pl.multiple_of(block * length, length), length)

    peers = [{"seq": lax.rem(row + d, seq)} for d in range(1, seq)]
    meet(peers)

    def exchange(source, target, length, kind):
        copies = []
        for d in range(1, seq):
            to = lax.rem(row + d, seq)
            copy = remote(source.at[to], target.at[place(row, length)], sends, recvs, kind * seq + d, {"seq": to})
            copy.start()
            copies.append(copy)
        mover.start((kind, "own"), source.at[row], target.at[place(row, length)])
        return copies

    tok_copies = exchange(tok_ref, x_ref, TB, 0)
    mem_copies = exchange(src_ref, mem_ref, src // seq, 1)

    for head in range(HEADS):
        vt[head * AUG + HEAD : (head + 1) * AUG, :] = jnp.ones((AUG - HEAD, size), BF16)
        v2t[head * AUG + HEAD : (head + 1) * AUG, :] = jnp.ones((AUG - HEAD, src), BF16)
    self_mask(mask, tl_ref[...], row, size)
    cross_mask(mask2, tl_ref[...], sl_ref[...], row, size, src)

    def put_vt(ref, values, place):
        for head in range(HEADS):
            ref[head * AUG : head * AUG + HEAD, place] = values[head * HEAD : (head + 1) * HEAD]

    mover.wait("wqkv", (0, "own"))
    for d in range(seq):
        if d:
            tok_copies[d - 1].wait_recv()
        ts = place(lax.rem(row + seq - d, seq), TB)
        xb = x_ref[ts, :]
        q = ((mm(xb, wqkv_ref[:, :width]) + vec_of(bqv, 0, width)) * (SCALE * LOG2E)).astype(BF16)
        q_ref[ts, :] = q
        qt_ref[:, ts] = q.T
        k = mm(xb, wqkv_ref[:, width : 2 * width]).astype(BF16)
        k_ref[ts, :] = k
        kt_ref[:, ts] = k.T
        v = (mm(xb, wqkv_ref[:, 2 * width :]) + vec_of(bqv, width, width)).astype(BF16)
        v_ref[ts, :] = v
        put_vt(vt, v.T, ts)
    mover.wait("wckv", (1, "own"))
    for copy in mem_copies:
        copy.wait_recv()
    cot_copies = exchange(cot_ref, cot_out, TB, 2)
    for i in (0, 1, 2, 3, 4, 5, 6):
        mover.start(i, kept[i], outs[1 + i])
    k2 = mm(mem_ref[...], wckv_ref[:, :width]).astype(BF16)
    k2_ref[...] = k2
    k2t_ref[...] = k2.T
    v2 = (mm(mem_ref[...], wckv_ref[:, width:]) + vec_of(bcv, 0, width)).astype(BF16)
    v2_ref[...] = v2
    put_vt(v2t, v2.T, slice(None))
    for i in (13, 14, 15):
        mover.start(i, kept[i], outs[1 + i])

    row_attend(k_ref, qt_ref, vt, mask, ctx_ref, lse_ref, size, lambda qb: (qb + 1) * TB)
    for i in (7, 8):
        mover.start(i, kept[i], outs[1 + i])
    mover.wait("wso", "wcq")
    for tb in range(blocks):
        ts = slice(tb * TB, (tb + 1) * TB)
        h1 = x_ref[ts, :].astype(F32) + mm(ctx_ref[:, ts].T, wso_ref[...]) + vec_of(bso, 0, width)
        xh, rstd = normalize(h1)
        xh1_ref[ts, :] = xh.astype(BF16)
        rs1_ref[ts, :] = rstd
        yb = xh * gains[0:1, :].astype(F32) + shifts[0:1, :].astype(F32)
        y1[ts, :] = yb
        q2 = ((mm(yb.astype(BF16), wcq_ref[...]) + vec_of(bcq, 0, width)) * (SCALE * LOG2E)).astype(BF16)
        q2_ref[ts, :] = q2
        q2t_ref[:, ts] = q2.T
    for i in (9, 10, 11, 12):
        mover.start(i, kept[i], outs[1 + i])
    row_attend(k2_ref, q2t_ref, v2t, mask2, c2_ref, lse2_ref, size, lambda qb: src)
    for i in (16, 17):
        mover.start(i, kept[i], outs[1 + i])
    mover.wait("wco")
    for tb in range(blocks):
        ts = slice(tb * TB, (tb + 1) * TB)
        h2 = y1[ts, :] + mm(c2_ref[:, ts].T, wco_ref[...]) + vec_of(bco, 0, width)
        xh, rstd = normalize(h2)
        xh2_ref[ts, :] = xh.astype(BF16)
        rs2_ref[ts, :] = rstd
        y2_ref[ts, :] = xh * gains[1:2, :].astype(F32) + shifts[1:2, :].astype(F32)
        for i in (18, 19, 20):
            mover.start((i, tb), kept[i].at[ts], outs[1 + i].at[ts])
    for copy in cot_copies:
        copy.wait_recv()
    for copy in tok_copies + mem_copies + cot_copies:
        copy.wait_send()
    mover.finish()


def put_halves(ref, rows, values):
    half = values.shape[1] // 2
    ref[0, rows, :] = values[:, :half].astype(BF16)
    ref[1, rows, :] = values[:, half:].astype(BF16)


def ffn_kernel(
    y2_h, xh2_h, rs2_h, cot_h, bfi, bfo, gains, shifts, win_h, wout_h,
    out_h, dh2_h, dw_h, dvec_ref,
    y2_ref, xh2_ref, rs2_ref, cot_ref, win_ref, wout_ref, out_ref, dh2_ref, dw_ref,
    a_s, du_s, slope_s, y2b_s, dz_s, sems,
):
    size, width = y2_ref.shape
    inner = win_ref.shape[1]
    cols = [slice(j, j + width) for j in range(0, inner, width)]
    mover = Mover(sems)
    for name, src, dst in (
        ("y2", y2_h, y2_ref), ("win", win_h, win_ref), ("wout", wout_h, wout_ref),
        ("cot", cot_h, cot_ref), ("xh2", xh2_h, xh2_ref), ("rs2", rs2_h, rs2_ref),
    ):
        mover.start(name, src, dst)
    gain2, shift2, gain1 = gains[2:3, :].astype(F32), shifts[2:3, :].astype(F32), gains[1:2, :].astype(F32)
    dvec_ref[...] = jnp.zeros_like(dvec_ref)
    mover.wait("y2", "win", "wout", "cot", "xh2", "rs2")

    @pl.loop(0, size // TB)
    def _(tb):
        ts = pl.ds(pl.multiple_of(tb * TB, TB), TB)
        y2 = y2_ref[ts, :]
        y2b = y2.astype(BF16)
        y2b_s[ts, :] = y2b
        h3 = y2 + vec_of(bfo, 0, width)
        for j, cs in enumerate(cols):
            u = mm(y2b, win_ref[:, cs]) + vec_of(bfi, j * width, width)
            sg = 0.5 * jnp.tanh(0.5 * u) + 0.5
            act = u * sg
            slope_s[:, cs] = sg + act * (1.0 - sg)
            act = act.astype(BF16)
            a_s[ts, cs] = act
            h3 = h3 + mm(act, wout_ref[cs, :])
        xh, rstd = normalize(h3)
        out_ref[ts, :] = (xh * gain2 + shift2).astype(BF16)
        grad = cot_ref[ts, :].astype(F32)
        dh3, dg, db = norm_back(grad, xh, rstd, gain2)
        dz = dh3.astype(BF16)
        dz_s[ts, :] = dz
        dvec_ref[V_G + 2 : V_G + 3, :] += dg
        dvec_ref[V_B + 2 : V_B + 3, :] += db
        dvec_ref[V_FO : V_FO + 1, :] += jnp.sum(dz.astype(F32), axis=0, keepdims=True)
        dy2 = dh3
        for j, cs in enumerate(cols):
            du = (mm(dz, wout_ref[cs, :], 1, 1) * slope_s[:, cs]).astype(BF16)
            du_s[ts, cs] = du
            dvec_ref[V_FI + j : V_FI + j + 1, :] += jnp.sum(du.astype(F32), axis=0, keepdims=True)
            dy2 = dy2 + mm(du, win_ref[:, cs], 1, 1)
        xh2 = xh2_ref[ts, :].astype(F32)
        dh2, dg, db = norm_back(dy2, xh2, rs2_ref[ts, :], gain1)
        dh2_ref[ts, :] = dh2
        dvec_ref[V_G + 1 : V_G + 2, :] += dg
        dvec_ref[V_B + 1 : V_B + 2, :] += db

    mover.start("out", out_ref, out_h)
    mover.start("dh2", dh2_ref, dh2_h)
    for j, cs in enumerate(cols):
        rows = slice((G_OUT + j) * width, (G_OUT + j + 1) * width)
        put_halves(dw_ref, rows, mm(a_s[:, cs], dz_s[...], 0, 0))
        mover.start(rows.start, dw_ref.at[:, rows], dw_h.at[:, rows])
    for j, cs in enumerate(cols):
        rows = slice((G_IN + j) * width, (G_IN + j + 1) * width)
        put_halves(dw_ref, rows, mm(y2b_s[...], du_s[:, cs], 0, 0))
        mover.start(rows.start, dw_ref.at[:, rows], dw_h.at[:, rows])
    mover.finish()


def row_attend_back(
    k_ref, kt_ref, v_ref, q_ref, qt_ref, dc_ref, dct_ref, ctx_ref, lse_ref, mask_ref,
    delta, dqt, dq_ref, dk_ref, dv_ref, size, keys, query_start, after,
):
    @pl.loop(0, HEADS // 2)
    def _(pair):
        lanes = pl.ds(pl.multiple_of(pair * 2 * HEAD, 2 * HEAD), 2 * HEAD)
        both = dct_ref[lanes, :].astype(F32) * ctx_ref[lanes, :].astype(F32)
        for half in range(2):
            delta[half] = jnp.sum(both[half * HEAD : (half + 1) * HEAD], axis=0, keepdims=True)
        dqt[...] = jnp.zeros_like(dqt)
        for kb in range(keys // TB):
            ks, qs = slice(kb * TB, (kb + 1) * TB), slice(query_start(kb), size)
            dks, dvs = [], []
            for half in range(2):
                head = pair * 2 + half
                rows = pl.ds(pl.multiple_of(head * HEAD, HEAD), HEAD)
                s = mm(k_ref[ks, lanes], half_of(qt_ref[lanes, qs], half))
                p = jnp.exp2(s + mask_ref[ks, qs] - lse_ref[head, :, qs])
                dp = mm(v_ref[ks, lanes], half_of(dct_ref[lanes, qs], half))
                ds = (p * (dp - delta[half, :, qs])).astype(BF16)
                dvs.append(mm(p.astype(BF16), dc_ref[qs, lanes]))
                dks.append(mm(ds, q_ref[qs, lanes]))
                dqt[half * HEAD : (half + 1) * HEAD, qs] += mm(kt_ref[rows, ks], ds)
            first = lax.broadcasted_iota(jnp.int32, (TB, 2 * HEAD), 1) < HEAD
            dv_ref[ks, lanes] = jnp.where(first, dvs[0], dvs[1]).astype(BF16)
            dk_ref[ks, lanes] = (jnp.where(first, dks[0], dks[1]) * (1.0 / LOG2E)).astype(BF16)
        dq_ref[:, lanes] = (dqt[...] * SCALE).astype(BF16).T
        for place, act in enumerate(after):
            pl.when(pair == place)(act)


class Stream:
    def __init__(self, grads, sums, source, base, rows, slots, sems):
        dp, self.seq = lax.axis_index("dp"), lax.axis_size("seq")
        self.z = lax.axis_index("seq")
        self.core, x, y = lax.rem(dp, 2), lax.rem(dp // 2, 2), dp // 4
        self.near = {"dp": dp + 1 - 2 * self.core}
        by_x, by_y = {"dp": dp + 2 - 4 * x}, {"dp": dp + 4 - 8 * y}
        self.grads, self.sums, self.source, self.base, self.rows = grads, sums, source, base, rows
        self.slots, self.sems = slots, sems
        half, quarter, eighth = rows // 2, rows // 4, rows // 8
        self.unit = rows // (8 * self.seq)
        self.plan = []
        for part, (one, two, b1, b2) in enumerate(((x, y, by_x, by_y), (y, x, by_y, by_x))):
            start = part * half
            keep1, give1 = start + one * quarter, start + (1 - one) * quarter
            keep2, give2 = keep1 + two * eighth, keep1 + (1 - two) * eighth
            self.plan.append((b1, keep1, give1, b2, keep2, give2))

    def at(self, start, length):
        return pl.ds(pl.multiple_of(self.base + start, 16), length)

    def view(self, start, length):
        return self.grads.at[self.core, self.at(start, length)]

    def summed(self, start, length):
        return self.sums.at[self.core, self.at(start, length)]

    def own_copies(self):
        moves = [keep2 + self.z * self.unit for _, _, _, _, keep2, _ in self.plan]
        return [
            pltpu.make_async_copy(self.view(at, self.unit), self.summed(at, self.unit), self.sems[0].at[OWN + i])
            for i, at in enumerate(moves)
        ]

    def copies(self, step):
        rows, (s0, s1, s2, s3), seq = self.rows, self.slots, self.seq
        first = sum(COPIES[:step])
        sends, recvs = self.sems
        moves = []
        if step == 0:
            src = self.source.at[1 - self.core, self.at(0, rows)]
            moves.append((src, s0, self.near))
        if step == 7:
            moves.append((self.summed(0, rows), self.summed(0, rows), self.near))
        for part, (b1, keep1, give1, b2, keep2, give2) in enumerate(self.plan):
            if step == 1:
                moves.append((self.view(give1, rows // 4), s1.at[part], b1))
            if step == 2:
                moves.append((self.view(give2, rows // 8), s2.at[part], b2))
            if step == 5:
                moves.append((self.summed(keep2, rows // 8), self.summed(keep2, rows // 8), b2))
            if step == 6:
                moves.append((self.summed(keep1, rows // 4), self.summed(keep1, rows // 4), b1))
            for d in range(1, seq):
                to = lax.rem(self.z + d, seq)
                if step == 3:
                    moves.append((self.view(keep2 + to * self.unit, self.unit), s3.at[part, d - 1], {"seq": to}))
                if step == 4:
                    own = keep2 + self.z * self.unit
                    moves.append((self.view(own, self.unit), self.summed(own, self.unit), {"seq": to}))
        return [remote(*move[:2], sends, recvs, first + i, move[2]) for i, move in enumerate(moves)]

    def add(self, start, slots, length):
        unit = self.unit

        @pl.loop(0, length // unit)
        def _(i):
            place = pl.ds(pl.multiple_of(self.base + start + i * unit, 16), unit)
            total = self.grads[self.core, place, :].astype(F32)
            for slot in slots:
                total = total + slot[pl.ds(pl.multiple_of(i * unit, 16), unit), :].astype(F32)
            self.grads[self.core, place, :] = total.astype(BF16)

    def tick(self, step):
        if step:
            for copy in self.copies(step - 1):
                copy.wait()
        if step == 5:
            for copy in self.own_copies():
                copy.wait()
        s0, s1, s2, s3 = self.slots
        if step == 1:
            self.add(0, [s0], self.rows)
        for part, (_, keep1, _, _, keep2, _) in enumerate(self.plan):
            if step == 2:
                self.add(keep1, [s1.at[part]], self.rows // 4)
            if step == 3:
                self.add(keep2, [s2.at[part]], self.rows // 8)
            if step == 4:
                self.add(keep2 + self.z * self.unit, [s3.at[part, d] for d in range(self.seq - 1)], self.unit)
        if step < STEPS:
            for copy in self.copies(step):
                copy.start()
        if step == 4:
            for copy in self.own_copies():
                copy.start()


class VectorSum:
    def __init__(self, held, sems):
        dp, self.seq, self.z = lax.axis_index("dp"), lax.axis_size("seq"), lax.axis_index("seq")
        core, x, y = lax.rem(dp, 2), lax.rem(dp // 2, 2), dp // 4
        self.partners = [{"dp": dp + 1 - 2 * core}, {"dp": dp + 2 - 4 * x}, {"dp": dp + 4 - 8 * y}]
        self.held, self.sems = held, sems

    def copies(self, step):
        sends, recvs = self.sems
        if step < 3:
            return [remote(self.held.at[2 * step], self.held.at[2 * step + 1], sends, recvs, step, self.partners[step])]
        own = self.held.at[6 + self.z]
        return [remote(own, own, sends, recvs, 2 + d, {"seq": lax.rem(self.z + d, self.seq)}) for d in range(1, self.seq)]

    def tick(self, step):
        if step:
            for copy in self.copies(step - 1):
                copy.wait()
            if step < 4:
                to = 2 * step if step < 3 else 6 + self.z
                self.held[to] = self.held[2 * step - 2] + self.held[2 * step - 1]
        if step < 4:
            for copy in self.copies(step):
                copy.start()

    def total(self):
        values = self.held[6]
        for i in range(1, self.seq):
            values = values + self.held[6 + i]
        return values


BACK_INS = ("dh2", "co", "c2", "k2", "q2t", "v2", "q2", "k2t", "lse2", "mem", "ckv", "cq", "xh1", "rs1", "so",
            "ctx", "k", "qt", "v", "q", "kt", "lse", "x", "qkv")


def backward_kernel(tl_ref, sl_ref, gains, shifts, dvec_in, out_row_h, dwf_h, *rest):
    n = len(BACK_INS)
    hbm, rest = dict(zip(BACK_INS, rest[:n])), rest[n:]
    (out_h, dtok_h, dmem_h, grads_h, dvec_ref), rest = rest[:5], rest[5:]
    vmem, rest = dict(zip(BACK_INS, rest[:n])), rest[n:]
    (mask, mask2, delta, dqt, dc, dct, dq, dk, dv, dk2, dv2, dh1, y1b, dtok, dmem, grads, held), rest = rest[:17], rest[17:]
    slots, rest = [rest[4 * i : 4 * i + 4] for i in range(len(STREAMS))], rest[4 * len(STREAMS) :]
    sems, sends, recvs, xsends, xrecvs = rest
    x_ref, mem_ref, dh2_ref = vmem["x"], vmem["mem"], vmem["dh2"]
    c2_ref, ctx_ref = vmem["c2"], vmem["ctx"]
    size, width = x_ref.shape
    src = mem_ref.shape[0]
    seq = lax.axis_size("seq")
    row, dp = lax.axis_index("seq"), lax.axis_index("dp")
    blocks = [slice(t, t + TB) for t in range(0, size, TB)]
    mover = Mover(sems)
    for name in BACK_INS[:3]:
        mover.start(name, hbm[name], vmem[name])
    split = [(base * width, rows * width) for base, rows in STREAMS]
    streams = [
        Stream(grads, grads_h, dwf_h if i < 2 else grads, base, rows, slots[i], (sends.at[i], recvs.at[i]))
        for i, (base, rows) in enumerate(split)
    ]
    w_out, w_in, w_cross, w_qkv = (s.tick for s in streams)
    vectors = VectorSum(held, (sends.at[len(STREAMS)], recvs.at[len(STREAMS)]))
    core, x, y = streams[0].core, lax.rem(dp // 2, 2), dp // 4
    meet(
        [{"dp": dp + 1 - 2 * core}, {"dp": dp + 2 - 4 * x}, {"dp": dp + 4 - 8 * y}]
        + [{"seq": lax.rem(row + d, seq)} for d in range(1, seq)]
    )

    def exchange(source, target, kind):
        length = source.shape[0] // seq
        copies = []
        for d in range(1, seq):
            to = lax.rem(row + d, seq)
            rows = pl.ds(pl.multiple_of(to * length, 16), length)
            copies.append(remote(source.at[rows], target.at[row], xsends, xrecvs, kind * seq + d, {"seq": to}))
        for copy in copies:
            copy.start()
        mover.start((kind, "own"), source.at[pl.ds(pl.multiple_of(row * length, 16), length)], target.at[row])
        return copies

    w_out(0)
    w_in(0)
    mover.start("grads", dwf_h.at[core], grads.at[core, 0 : dwf_h.shape[1]])
    for name in BACK_INS[3:]:
        mover.start(name, hbm[name], vmem[name])
    gain0, shift0 = gains[0:1, :].astype(F32), shifts[0:1, :].astype(F32)

    def total(values):
        return jnp.sum(values.astype(F32), axis=0, keepdims=True)

    def gather(i, values):
        put_halves(grads, slice(i * width, (i + 1) * width), values)

    dvec_ref[...] = dvec_in[...]
    cross_mask(mask2, tl_ref[...], sl_ref[...], row, size, src)
    mover.wait("dh2", "co", "c2")
    for ts in blocks:
        da2 = dh2_ref[ts, :].astype(BF16)
        dc[ts, :] = mm(da2, vmem["co"][...], 1, 1).astype(BF16)
        dct[:, ts] = mm(vmem["co"][...], da2, 1, 1).astype(BF16)
        dvec_ref[V_CO : V_CO + 1, :] += total(da2)
    mover.wait("grads")
    w_out(1)
    gather(G_CO, mm(c2_ref[...], dh2_ref[...].astype(BF16)))
    w_in(1)
    mover.wait(*BACK_INS[3:9])
    row_attend_back(
        vmem["k2"], vmem["k2t"], vmem["v2"], vmem["q2"], vmem["q2t"], dc, dct, c2_ref, vmem["lse2"], mask2,
        delta, dqt, dq, dk2, dv2, size, src, lambda kb: 0,
        cross_ticks(w_out, w_in, w_cross, w_qkv),
    )
    out_copies = exchange(out_row_h, out_h, 0)
    dvec_ref[V_CV : V_CV + 1, :] = total(dv2[...])
    dvec_ref[V_CQ : V_CQ + 1, :] = total(dq[...])
    mover.wait("mem", "ckv", "cq", "xh1", "rs1", "so")
    gather(G_CK, mm(mem_ref[...], dk2[...], 0, 0))
    gather(G_CK + 1, mm(mem_ref[...], dv2[...], 0, 0))
    w_ckv = vmem["ckv"]
    dmem[...] = (
        mm(dk2[...], w_ckv[:, :width], 1, 1) + mm(dv2[...], w_ckv[:, width:], 1, 1)
    ).astype(BF16)
    for ts in blocks:
        dqb = dq[ts, :]
        dy1 = dh2_ref[ts, :] + mm(dqb, vmem["cq"][...], 1, 1)
        xh1 = vmem["xh1"][ts, :].astype(F32)
        y1b[ts, :] = (xh1 * gain0 + shift0).astype(BF16)
        dh, dg, db = norm_back(dy1, xh1, vmem["rs1"][ts, :], gain0)
        dvec_ref[V_G : V_G + 1, :] += dg
        dvec_ref[V_B : V_B + 1, :] += db
        dh1[ts, :] = dh
        dvec_ref[V_SO : V_SO + 1, :] += total(dh.astype(BF16))
    w_out(3)
    gather(G_CQ, mm(y1b[...], dq[...], 0, 0))
    self_mask(mask, tl_ref[...], row, size)
    for ts in blocks:
        da1 = dh1[ts, :].astype(BF16)
        dc[ts, :] = mm(da1, vmem["so"][...], 1, 1).astype(BF16)
        dct[:, ts] = mm(vmem["so"][...], da1, 1, 1).astype(BF16)
    w_in(3)
    mover.wait("ctx")
    gather(G_SO, mm(ctx_ref[...], dh1[...].astype(BF16)))
    w_cross(0)
    w_out(4)
    mover.wait("k", "qt", "v", "q", "kt", "lse")
    row_attend_back(
        vmem["k"], vmem["kt"], vmem["v"], vmem["q"], vmem["qt"], dc, dct, ctx_ref, vmem["lse"], mask,
        delta, dqt, dq, dk, dv, size, size, lambda kb: kb * TB,
        self_ticks(w_out, w_in, w_cross, w_qkv),
    )
    dvec_ref[V_Q : V_Q + 1, :] = total(dq[...])
    dvec_ref[V_V : V_V + 1, :] = total(dv[...])
    held[0] = dvec_ref[...]
    mover.wait("x", "qkv")
    for i, part in enumerate((dq, dk, dv)):
        gather(G_QKV + i, mm(x_ref[...], part[...], 0, 0))
    w_qkv(0)
    vectors.tick(0)
    wqkv_ref = vmem["qkv"]
    for ts in blocks:
        dtok[ts, :] = (
            dh1[ts, :]
            + mm(dq[ts, :], wqkv_ref[:, :width], 1, 1)
            + mm(dk[ts, :], wqkv_ref[:, width : 2 * width], 1, 1)
            + mm(dv[ts, :], wqkv_ref[:, 2 * width :], 1, 1)
        ).astype(BF16)
    w_qkv(1)
    vectors.tick(1)
    tok_copies = exchange(dtok, dtok_h, 1)
    mem_copies = exchange(dmem, dmem_h, 2)

    last_ticks(w_out, w_in, w_cross, w_qkv, vectors.tick)
    dvec_ref[...] = vectors.total()
    for copy in out_copies + tok_copies + mem_copies:
        copy.wait()
    mover.finish()


def cross_ticks(w_out, w_in, w_cross, w_qkv):
    def late():
        w_out(2)

    def last():
        w_in(2)

    return [lambda: None, lambda: None, late, last]


def self_ticks(w_out, w_in, w_cross, w_qkv):
    def first():
        w_in(4)
        w_cross(1)

    def second():
        w_out(5)

    def third():
        w_in(5)
        w_cross(2)
        w_out(6)

    def fourth():
        w_in(6)
        w_cross(3)
        w_out(7)

    return [first, second, third, fourth]


def last_ticks(w_out, w_in, w_cross, w_qkv, vectors):
    w_in(7)
    w_cross(4)
    w_out(8)
    w_qkv(2)
    vectors(2)
    w_cross(5)
    w_in(8)
    w_qkv(3)
    vectors(3)
    w_cross(6)
    w_qkv(4)
    vectors(4)
    w_cross(7)
    w_qkv(5)
    w_cross(8)
    w_qkv(6)
    w_qkv(7)
    w_qkv(8)


def unpack_kernel(grads_h, dvec_ref, dtok_h, dmem_h, *rest):
    outs, rest = rest[:18], rest[18:]
    mats, vecs = outs[:9], outs[9:]
    grads, dtok, dmem, rest = rest[0], rest[1], rest[2], rest[3:]
    wide, sems = rest[:9], rest[9]
    mover = Mover(sems)
    width = 2 * grads.shape[2]
    half = width // 2
    plan = ((0, G_QKV, 1, 3), (1, G_SO, 1, 1), (2, G_CQ, 1, 1), (3, G_CK, 1, 2), (4, G_CO, 1, 1), (5, G_IN, 1, 4), (6, G_OUT, 4, 1))
    for i, base, units, blocks in plan:
        rows = slice(base * width, (base + units * blocks) * width)
        mover.start(i, grads_h.at[:, rows], grads.at[:, rows])
    mover.start("tok", dtok_h, dtok)
    mover.start("mem", dmem_h, dmem)
    for i, base, units, blocks in plan:
        mover.wait(i)
        for b in range(blocks):
            for u in range(units):
                rows = slice((base + b + u) * width, (base + b + u + 1) * width)
                for c in range(2):
                    wide[i][u * width : (u + 1) * width, b * width + c * half : b * width + (c + 1) * half] = grads[c, rows, :].astype(F32)
        mover.start((i, "out"), wide[i], mats[i])
    for i, name, source in ((7, "tok", dtok), (8, "mem", dmem)):
        mover.wait(name)
        wide[i][...] = source[...].astype(F32)
        mover.start((i, "out"), wide[i], mats[i])
    place = 0
    for ref in vecs:
        if len(ref.shape) == 2:
            ref[...] = dvec_ref[place : place + ref.shape[0], :]
            place += ref.shape[0]
        else:
            for j in range(ref.shape[0] // width):
                ref[j * width : (j + 1) * width] = dvec_ref[place, :]
                place += 1
    mover.finish()


WHOLE = pl.BlockSpec(memory_space=pltpu.VMEM)


def call(kernel, ins, outs, scratch, name):
    return pl.pallas_call(
        kernel,
        out_shape=[jax.ShapeDtypeStruct(*o) for o in outs],
        in_specs=[WHOLE] * len(ins),
        out_specs=[WHOLE] * len(outs),
        scratch_shapes=[pltpu.VMEM(*s) for s in scratch],
        compiler_params=pltpu.CompilerParams(vmem_limit_bytes=60 * 2**20),
        name=name,
    )(*ins)


ANY = pl.BlockSpec(memory_space=pl.ANY)


def forward(tokens, memory, cot, tl, sl, small, wqkv, wso, wcq, wckv, wco):
    seq, block, d = tokens.shape
    t, s = seq * block, seq * memory.shape[1]
    tok, feat, row = ((t, d), BF16), ((d, t), BF16), ((HEADS, 1, t), F32)
    col, mem = ((t, 1), F32), ((s, d), BF16)
    kept = [tok, mem, tok, feat, tok, feat, tok, feat, row, tok, col,
            tok, feat, mem, ((d, s), BF16), mem, feat, row, ((t, d), F32), tok, col]
    weights = (wqkv, wso, wcq, wckv, wco)
    scratch = kept + [(w.shape, w.dtype) for w in weights]
    scratch += [((t, t), F32), ((s, t), F32), ((HEADS * AUG, t), BF16), ((HEADS * AUG, s), BF16), ((t, d), F32)]
    return pl.pallas_call(
        forward_kernel,
        out_shape=[jax.ShapeDtypeStruct(*o) for o in [tok] + kept],
        in_specs=[ANY] * 3 + [WHOLE] * (2 + len(small)) + [ANY] * 5,
        out_specs=[ANY] * FWD_OUTS,
        scratch_shapes=[pltpu.VMEM(*x) for x in scratch]
        + [pltpu.SemaphoreType.DMA((40,)), pltpu.SemaphoreType.DMA((3 * seq,)), pltpu.SemaphoreType.DMA((3 * seq,))],
        compiler_params=pltpu.CompilerParams(vmem_limit_bytes=60 * 2**20, collective_id=0, has_side_effects=True),
        name="forward",
    )(tokens, memory, cot, tl, sl, *small, *weights)


def ffn(y2, xh2, rs2, cot, small, win, wout):
    (t, d), f = y2.shape, win.shape[1]
    tok, wide = ((t, d), BF16), ((t, d), F32)
    dw = ((2, 2 * f, d // 2), BF16)
    return pl.pallas_call(
        ffn_kernel,
        out_shape=[jax.ShapeDtypeStruct(*o) for o in (tok, wide, dw, ((VECS, d), F32))],
        in_specs=[ANY] * 4 + [WHOLE] * len(small) + [ANY] * 2,
        out_specs=[ANY] * 3 + [WHOLE],
        scratch_shapes=[
            pltpu.VMEM(*x)
            for x in (wide, tok, ((t, 1), F32), tok, (win.shape, BF16), (wout.shape, BF16), tok, wide, dw,
                      ((t, f), BF16), ((t, f), BF16), ((TB, f), F32), tok, tok)
        ] + [pltpu.SemaphoreType.DMA((24,))],
        compiler_params=pltpu.CompilerParams(vmem_limit_bytes=60 * 2**20),
        name="ffn",
    )(y2, xh2, rs2, cot, *small, win, wout)


def backward(tl, sl, gains, shifts, dvec, out_row, dwf, ins):
    t, d = ins["x"].shape
    s = ins["mem"].shape[0]
    seq = lax.axis_size("seq")
    tok, mem = ((t, d), BF16), ((s, d), BF16)
    total = sum(rows for _, rows in STREAMS) * d
    grads = ((2, total, d // 2), BF16)
    scratch = [(ins[name].shape, ins[name].dtype) for name in BACK_INS]
    scratch += [((t, t), F32), ((s, t), F32), ((2, 1, t), F32), ((2 * HEAD, t), F32), tok, ((d, t), BF16),
                tok, tok, tok, mem, mem, ((t, d), F32), tok, tok, mem, grads, ((6 + seq, VECS, d), F32)]
    for _, rows in STREAMS:
        r, c = rows * d, d // 2
        scratch += [((r, c), BF16), ((2, r // 4, c), BF16), ((2, r // 8, c), BF16), ((2, seq - 1, r // (8 * seq), c), BF16)]
    steps = pltpu.SemaphoreType.DMA((len(STREAMS) + 1, OWN + 2))
    return pl.pallas_call(
        backward_kernel,
        out_shape=[
            jax.ShapeDtypeStruct((seq, t // seq, d), BF16),
            jax.ShapeDtypeStruct((seq, t // seq, d), BF16),
            jax.ShapeDtypeStruct((seq, s // seq, d), BF16),
            jax.ShapeDtypeStruct(*grads),
            jax.ShapeDtypeStruct((VECS, d), F32),
        ],
        in_specs=[WHOLE] * 5 + [ANY] * (2 + len(BACK_INS)),
        out_specs=[ANY] * 4 + [WHOLE],
        scratch_shapes=[pltpu.VMEM(*x) for x in scratch]
        + [pltpu.SemaphoreType.DMA((40,)), steps, steps, pltpu.SemaphoreType.DMA((3 * seq,)), pltpu.SemaphoreType.DMA((3 * seq,))],
        compiler_params=pltpu.CompilerParams(vmem_limit_bytes=62 * 2**20, collective_id=1, has_side_effects=True),
        name="backward",
    )(tl, sl, gains, shifts, dvec, out_row, dwf, *[ins[name] for name in BACK_INS])


def unpack(grads, dvec, dtok, dmem, d, f):
    mats = [(d, 3 * d), (d, d), (d, d), (d, 2 * d), (d, d), (d, f), (f, d), dtok.shape, dmem.shape]
    vecs = [(2 * d,), (d,), (d,), (d,), (d,), (f,), (d,), (3, d), (3, d)]
    outs = pl.pallas_call(
        unpack_kernel,
        out_shape=[jax.ShapeDtypeStruct(o, F32) for o in mats + vecs],
        in_specs=[ANY, WHOLE, ANY, ANY],
        out_specs=[ANY] * 9 + [WHOLE] * 9,
        scratch_shapes=[pltpu.VMEM(x.shape, x.dtype) for x in (grads, dtok, dmem)]
        + [pltpu.VMEM(m, F32) for m in mats] + [pltpu.SemaphoreType.DMA((24,))],
        compiler_params=pltpu.CompilerParams(vmem_limit_bytes=60 * 2**20),
        name="unpack",
    )(grads, dvec, dtok, dmem)
    d_qkv, d_so, d_cq, d_ckv, d_co, d_fi, d_fo, d_tok, d_mem = outs[:9]
    v_qv, v_so, v_cq, v_cv, v_co, v_fi, v_fo, d_gains, d_shifts = outs[9:]
    return (d_tok, d_mem, d_qkv, v_qv, d_so, v_so, d_cq, v_cq, d_ckv, v_cv, d_co, v_co, d_fi, v_fi, d_fo, v_fo, d_gains, d_shifts)


def layer_norm(values, gain, shift):
    center = values - jnp.mean(values, axis=-1, keepdims=True)
    spread = jnp.mean(center * center, axis=-1, keepdims=True)
    return center * lax.rsqrt(spread + 1e-05) * gain + shift


def doc_ids(lengths, size):
    ends = jnp.cumsum(lengths, axis=1)
    places = jnp.arange(size, dtype=jnp.int32)
    return jnp.sum((ends[:, None, :] <= places[None, :, None]).astype(jnp.int32), axis=2)


def block_width(key_total):
    return 512 if key_total % 512 == 0 else key_total


def contract_rows(left, right):
    return lax.dot_general(
        left, right, (((0,), (0,)), ((), ())), preferred_element_type=jnp.float32
    )


def contract_cols(left, right):
    return lax.dot_general(
        left, right, (((1,), (1,)), ((), ())), preferred_element_type=jnp.float32
    )


def block_scores(queries, keys, allowed, start_at, width_of, score_scale):
    key_block = lax.dynamic_slice_in_dim(keys, start_at, width_of, 1)
    scores = (
        jnp.einsum("rqhd,rkhd->rhqk", queries, key_block, preferred_element_type=jnp.float32)
        * score_scale
    )
    return jnp.where(allowed(start_at, width_of)[:, None], scores, -1000000000.0)


def attend_forward(queries, keys, values, allowed, skip_after, score_scale):
    row_count, query_count, head_count, head_size = queries.shape
    key_total = keys.shape[1]
    width_of = block_width(key_total)
    block_count = key_total // width_of

    def statistics(carried, block_index):
        start_at = block_index * width_of

        def statistics_work(state):
            running_max, running_sum = state
            scores = block_scores(queries, keys, allowed, start_at, width_of, score_scale)
            new_max = jnp.maximum(running_max, jnp.max(scores, axis=3))
            new_sum = running_sum * jnp.exp(running_max - new_max) + jnp.sum(
                jnp.exp(scores - new_max[..., None]), axis=3
            )
            return (new_max, new_sum)

        return (
            lax.cond(start_at > skip_after, lambda state: state, statistics_work, carried),
            None,
        )

    stat_shape = (row_count, head_count, query_count)
    start_state = (
        jnp.full(stat_shape, -1000000000.0, jnp.float32),
        jnp.zeros(stat_shape, jnp.float32),
    )
    block_numbers = jnp.arange(block_count, dtype=jnp.int32)
    (running_max, running_sum), _ = lax.scan(statistics, start_state, block_numbers)
    log_total = running_max + jnp.log(running_sum)

    def mixing(carried, block_index):
        start_at = block_index * width_of

        def mixing_work(accum):
            scores = block_scores(queries, keys, allowed, start_at, width_of, score_scale)
            probs = jnp.exp(scores - log_total[..., None]).astype(jnp.bfloat16)
            value_block = lax.dynamic_slice_in_dim(values, start_at, width_of, 1)
            return accum + jnp.einsum(
                "rhqk,rkhd->rqhd", probs, value_block, preferred_element_type=jnp.float32
            )

        return (lax.cond(start_at > skip_after, lambda accum: accum, mixing_work, carried), None)

    start_accum = jnp.zeros((row_count, query_count, head_count, head_size), jnp.float32)
    accum, _ = lax.scan(mixing, start_accum, block_numbers)
    return (accum, log_total)


def attend_back(
    queries, keys, values, allowed, skip_after, score_scale, log_total, grad_out, delta
):
    row_count, query_count, head_count, head_size = queries.shape
    key_total = keys.shape[1]
    width_of = block_width(key_total)
    block_count = key_total // width_of

    def step(block_index, state):
        start_at = block_index * width_of

        def step_work(inner):
            scores = block_scores(queries, keys, allowed, start_at, width_of, score_scale)
            probs = jnp.exp(scores - log_total[..., None])
            key_block = lax.dynamic_slice_in_dim(keys, start_at, width_of, 1)
            value_block = lax.dynamic_slice_in_dim(values, start_at, width_of, 1)
            grad_probs = jnp.einsum(
                "rqhd,rkhd->rhqk", grad_out, value_block, preferred_element_type=jnp.float32
            )
            grad_scores = (probs * (grad_probs - delta[..., None])).astype(jnp.bfloat16)
            grad_query = (
                inner[0]
                + jnp.einsum(
                    "rhqk,rkhd->rqhd", grad_scores, key_block, preferred_element_type=jnp.float32
                )
                * score_scale
            )
            key_part = (
                jnp.einsum(
                    "rhqk,rqhd->rkhd", grad_scores, queries, preferred_element_type=jnp.float32
                )
                * score_scale
            )
            value_part = jnp.einsum(
                "rhqk,rqhd->rkhd",
                probs.astype(jnp.bfloat16),
                grad_out,
                preferred_element_type=jnp.float32,
            )
            grad_keys = lax.dynamic_update_slice_in_dim(inner[1], key_part, start_at, 1)
            grad_values = lax.dynamic_update_slice_in_dim(inner[2], value_part, start_at, 1)
            return (grad_query, grad_keys, grad_values)

        return lax.cond(start_at > skip_after, lambda inner: inner, step_work, state)

    start_state = (jnp.zeros((row_count, query_count, head_count, head_size), jnp.float32),)
    start_state = start_state + (
        jnp.zeros((row_count, key_total, head_count, head_size), jnp.float32),
        jnp.zeros((row_count, key_total, head_count, head_size), jnp.float32),
    )
    return lax.fori_loop(0, block_count, step, start_state)


def blocks_on_device(
    tokens,
    memory,
    doc_lengths,
    src_lengths,
    cotangent,
    w_qkv,
    qv_bias,
    self_out,
    self_out_bias,
    cross_query,
    cross_q_bias,
    cross_kv,
    cross_v_bias,
    cross_out,
    cross_out_bias,
    ffn_in,
    ffn_in_bias,
    ffn_out,
    ffn_out_bias,
    norm_gains,
    norm_biases,
):
    row_count, block_len, model_width = tokens.shape
    src_block = memory.shape[1]
    seq_count = lax.axis_size("seq")
    row_length = block_len * seq_count
    src_length = src_block * seq_count
    score_scale = HEAD ** (-0.5)
    first_place = lax.axis_index("seq") * block_len
    last_place = first_place + block_len - 1
    target_ids = doc_ids(doc_lengths, row_length)
    source_ids = doc_ids(src_lengths, src_length)
    own_ids = lax.dynamic_slice_in_dim(target_ids, first_place, block_len, 1)
    own_places = first_place + jnp.arange(block_len, dtype=jnp.int32)

    def self_allowed(start_at, width_of):
        key_ids = lax.dynamic_slice_in_dim(target_ids, start_at, width_of, 1)
        key_places = start_at + jnp.arange(width_of, dtype=jnp.int32)
        return (own_ids[:, :, None] == key_ids[:, None, :]) & (
            key_places[None, None, :] <= own_places[None, :, None]
        )

    def cross_allowed(start_at, width_of):
        return (own_ids[:, :, None] == source_ids[:, None, :]) | (own_ids[:, :, None] == NDOC)

    def split_heads(array_in):
        return array_in.reshape(array_in.shape[0], array_in.shape[1], HEADS, HEAD)

    token_rows = row_count * block_len
    flat_tokens = tokens.reshape(token_rows, model_width)
    flat_memory = memory.reshape(row_count * src_block, model_width)
    pair_bias = qv_bias.astype(jnp.float32)
    gains = norm_gains.astype(jnp.float32)
    shifts = norm_biases.astype(jnp.float32)
    packed = jnp.dot(flat_tokens, w_qkv, preferred_element_type=jnp.float32)
    self_queries = (packed[:, :model_width] + pair_bias[:model_width]).astype(jnp.bfloat16)
    self_keys = (
        packed[:, model_width : 2 * model_width]
        .astype(jnp.bfloat16)
        .reshape(row_count, block_len, model_width)
    )
    self_values = (
        (packed[:, 2 * model_width :] + pair_bias[model_width:])
        .astype(jnp.bfloat16)
        .reshape(row_count, block_len, model_width)
    )
    memory_pair = jnp.dot(flat_memory, cross_kv, preferred_element_type=jnp.float32)
    cross_keys = (
        memory_pair[:, :model_width].astype(jnp.bfloat16).reshape(row_count, src_block, model_width)
    )
    cross_values = (
        (memory_pair[:, model_width:] + cross_v_bias.astype(jnp.float32))
        .astype(jnp.bfloat16)
        .reshape(row_count, src_block, model_width)
    )
    all_keys, all_values, all_ckeys, all_cvalues = (
        lax.all_gather(self_keys, "seq", axis=1, tiled=True),
        lax.all_gather(self_values, "seq", axis=1, tiled=True),
        lax.all_gather(cross_keys, "seq", axis=1, tiled=True),
        lax.all_gather(cross_values, "seq", axis=1, tiled=True),
    )
    query_heads = split_heads(self_queries.reshape(row_count, block_len, model_width))
    self_accum, self_log = attend_forward(
        query_heads,
        split_heads(all_keys),
        split_heads(all_values),
        self_allowed,
        last_place,
        score_scale,
    )
    context_low = self_accum.reshape(token_rows, model_width).astype(jnp.bfloat16)
    inputs_f = flat_tokens.astype(jnp.float32)
    first_sum = (
        inputs_f
        + jnp.dot(context_low, self_out, preferred_element_type=jnp.float32)
        + self_out_bias.astype(jnp.float32)
    )
    first_norm, first_pull = jax.vjp(layer_norm, first_sum, gains[0], shifts[0])
    first_low = first_norm.astype(jnp.bfloat16)
    cross_q_rows = (
        jnp.dot(first_low, cross_query, preferred_element_type=jnp.float32)
        + cross_q_bias.astype(jnp.float32)
    ).astype(jnp.bfloat16)
    cross_heads = split_heads(cross_q_rows.reshape(row_count, block_len, model_width))
    cross_accum, cross_log = attend_forward(
        cross_heads,
        split_heads(all_ckeys),
        split_heads(all_cvalues),
        cross_allowed,
        src_length,
        score_scale,
    )
    cross_low = cross_accum.reshape(token_rows, model_width).astype(jnp.bfloat16)
    second_sum = (
        first_norm
        + jnp.dot(cross_low, cross_out, preferred_element_type=jnp.float32)
        + cross_out_bias.astype(jnp.float32)
    )
    second_norm, second_pull = jax.vjp(layer_norm, second_sum, gains[1], shifts[1])
    second_low = second_norm.astype(jnp.bfloat16)
    hidden_pre = jnp.dot(
        second_low, ffn_in, preferred_element_type=jnp.float32
    ) + ffn_in_bias.astype(jnp.float32)
    hidden_low = jax.nn.silu(hidden_pre).astype(jnp.bfloat16)
    third_sum = (
        second_norm
        + jnp.dot(hidden_low, ffn_out, preferred_element_type=jnp.float32)
        + ffn_out_bias.astype(jnp.float32)
    )
    result, third_pull = jax.vjp(layer_norm, third_sum, gains[2], shifts[2])
    output = result.astype(jnp.bfloat16).reshape(row_count, block_len, model_width)
    grad_third, gain_three, shift_three = third_pull(
        cotangent.reshape(token_rows, model_width).astype(jnp.float32)
    )
    grad_branch = grad_third.astype(jnp.bfloat16)
    d_ffn_out = contract_rows(hidden_low, grad_branch)
    d_ffn_out_bias = jnp.sum(grad_branch.astype(jnp.float32), axis=0)
    grad_hidden = contract_cols(grad_branch, ffn_out)
    sigmoid_pre = jax.nn.sigmoid(hidden_pre)
    grad_pre = (grad_hidden * sigmoid_pre * (1.0 + hidden_pre * (1.0 - sigmoid_pre))).astype(
        jnp.bfloat16
    )
    d_ffn_in = contract_rows(second_low, grad_pre)
    d_ffn_in_bias = jnp.sum(grad_pre.astype(jnp.float32), axis=0)
    grad_second_norm = grad_third + contract_cols(grad_pre, ffn_in)
    back_keys, back_values, back_ckeys, back_cvalues = (
        all_keys,
        all_values,
        all_ckeys,
        all_cvalues,
    )
    grad_second, gain_two, shift_two = second_pull(grad_second_norm)
    grad_cross_branch = grad_second.astype(jnp.bfloat16)
    d_cross_out = contract_rows(cross_low, grad_cross_branch)
    d_cross_out_bias = jnp.sum(grad_cross_branch.astype(jnp.float32), axis=0)
    grad_cross_ctx = contract_cols(grad_cross_branch, cross_out).astype(jnp.bfloat16)
    grad_cross_heads = split_heads(grad_cross_ctx.reshape(row_count, block_len, model_width))
    cross_delta = jnp.swapaxes(
        jnp.sum(grad_cross_heads.astype(jnp.float32) * cross_accum, axis=3), 1, 2
    )
    grad_cq, grad_ck_all, grad_cv_all = attend_back(
        cross_heads,
        split_heads(back_ckeys),
        split_heads(back_cvalues),
        cross_allowed,
        src_length,
        score_scale,
        cross_log,
        grad_cross_heads,
        cross_delta,
    )
    grad_ck_own, grad_cv_own = (
        lax.psum_scatter(
            grad_ck_all.reshape(row_count, src_length, model_width).astype(jnp.bfloat16),
            "seq",
            scatter_dimension=1,
            tiled=True,
        ).astype(jnp.float32),
        lax.psum_scatter(
            grad_cv_all.reshape(row_count, src_length, model_width).astype(jnp.bfloat16),
            "seq",
            scatter_dimension=1,
            tiled=True,
        ).astype(jnp.float32),
    )
    grad_pair = jnp.concatenate(
        [
            grad_ck_own.reshape(row_count * src_block, model_width).astype(jnp.bfloat16),
            grad_cv_own.reshape(row_count * src_block, model_width).astype(jnp.bfloat16),
        ],
        axis=1,
    )
    d_cross_kv = contract_rows(flat_memory, grad_pair)
    d_cross_v_bias = jnp.sum(grad_pair[:, model_width:].astype(jnp.float32), axis=0)
    d_memory = contract_cols(grad_pair, cross_kv).reshape(row_count, src_block, model_width)
    grad_cq_low = grad_cq.reshape(token_rows, model_width).astype(jnp.bfloat16)
    d_cross_query = contract_rows(first_low, grad_cq_low)
    d_cross_q_bias = jnp.sum(grad_cq_low.astype(jnp.float32), axis=0)
    grad_first_norm = grad_second + contract_cols(grad_cq_low, cross_query)
    grad_first, gain_one, shift_one = first_pull(grad_first_norm)
    grad_self_branch = grad_first.astype(jnp.bfloat16)
    d_self_out = contract_rows(context_low, grad_self_branch)
    d_self_out_bias = jnp.sum(grad_self_branch.astype(jnp.float32), axis=0)
    grad_context = contract_cols(grad_self_branch, self_out).astype(jnp.bfloat16)
    grad_context_heads = split_heads(grad_context.reshape(row_count, block_len, model_width))
    self_delta = jnp.swapaxes(
        jnp.sum(grad_context_heads.astype(jnp.float32) * self_accum, axis=3), 1, 2
    )
    grad_q, grad_k_all, grad_v_all = attend_back(
        query_heads,
        split_heads(back_keys),
        split_heads(back_values),
        self_allowed,
        last_place,
        score_scale,
        self_log,
        grad_context_heads,
        self_delta,
    )
    grad_k_own, grad_v_own = (
        lax.psum_scatter(
            grad_k_all.reshape(row_count, row_length, model_width).astype(jnp.bfloat16),
            "seq",
            scatter_dimension=1,
            tiled=True,
        ).astype(jnp.float32),
        lax.psum_scatter(
            grad_v_all.reshape(row_count, row_length, model_width).astype(jnp.bfloat16),
            "seq",
            scatter_dimension=1,
            tiled=True,
        ).astype(jnp.float32),
    )
    grad_k_flat = grad_k_own.reshape(token_rows, model_width)
    grad_v_flat = grad_v_own.reshape(token_rows, model_width)
    grad_q_low = grad_q.reshape(token_rows, model_width).astype(jnp.bfloat16)
    grad_v_low = grad_v_flat.astype(jnp.bfloat16)
    grad_proj = jnp.concatenate([grad_q_low, grad_k_flat.astype(jnp.bfloat16), grad_v_low], axis=1)
    d_w_qkv = contract_rows(flat_tokens, grad_proj)
    d_qv_bias = jnp.concatenate(
        [
            jnp.sum(grad_q_low.astype(jnp.float32), axis=0),
            jnp.sum(grad_v_low.astype(jnp.float32), axis=0),
        ]
    )
    d_tokens = (grad_first + contract_cols(grad_proj, w_qkv)).reshape(
        row_count, block_len, model_width
    )
    d_norm_gains = jnp.stack([gain_one, gain_two, gain_three])
    d_norm_biases = jnp.stack([shift_one, shift_two, shift_three])
    (
        d_w_qkv,
        d_qv_bias,
        d_self_out,
        d_self_out_bias,
        d_cross_query,
        d_cross_q_bias,
        d_cross_kv,
        d_cross_v_bias,
        d_cross_out,
        d_cross_out_bias,
        d_ffn_in,
        d_ffn_in_bias,
        d_ffn_out,
        d_ffn_out_bias,
        d_norm_gains,
        d_norm_biases,
    ) = lax.psum(
        (
            d_w_qkv,
            d_qv_bias,
            d_self_out,
            d_self_out_bias,
            d_cross_query,
            d_cross_q_bias,
            d_cross_kv,
            d_cross_v_bias,
            d_cross_out,
            d_cross_out_bias,
            d_ffn_in,
            d_ffn_in_bias,
            d_ffn_out,
            d_ffn_out_bias,
            d_norm_gains,
            d_norm_biases,
        ),
        ("dp", "seq"),
    )
    return (
        output,
        d_tokens,
        d_memory,
        d_w_qkv,
        d_qv_bias,
        d_self_out,
        d_self_out_bias,
        d_cross_query,
        d_cross_q_bias,
        d_cross_kv,
        d_cross_v_bias,
        d_cross_out,
        d_cross_out_bias,
        d_ffn_in,
        d_ffn_in_bias,
        d_ffn_out,
        d_ffn_out_bias,
        d_norm_gains,
        d_norm_biases,
    )


def rows_on_device(
    tokens, memory, tl, sl, cotangent, w_qkv, qv_bias, self_out, self_out_bias, cross_query, cross_q_bias,
    cross_kv, cross_v_bias, cross_out, cross_out_bias, ffn_in, ffn_in_bias, ffn_out, ffn_out_bias, gains, shifts,
):
    small = (qv_bias, self_out_bias, cross_q_bias, cross_v_bias, cross_out_bias, gains, shifts)
    cot, *saved = forward(tokens, memory, cotangent, tl, sl, small, w_qkv, self_out, cross_query, cross_kv, cross_out)
    names = ("x", "mem", "q", "qt", "k", "kt", "v", "ctx", "lse", "xh1", "rs1",
             "q2", "q2t", "k2", "k2t", "v2", "c2", "lse2", "y2", "xh2", "rs2")
    ins = dict(zip(names, saved))
    ins |= {"qkv": w_qkv, "so": self_out, "cq": cross_query, "ckv": cross_kv, "co": cross_out}
    out_row, ins["dh2"], dwf, dvec = ffn(
        ins["y2"], ins["xh2"], ins["rs2"], cot, (ffn_in_bias, ffn_out_bias, gains, shifts), ffn_in, ffn_out
    )
    out, dtok, dmem, grads, dvec = backward(tl, sl, gains, shifts, dvec, out_row, dwf, ins)
    return (out,) + unpack(grads, dvec, dtok, dmem, ffn_in.shape[0], ffn_in.shape[1])


def on_device(tokens, *rest):
    if tokens.shape[0] == lax.axis_size("seq") and lax.axis_size("dp") == 8:
        return rows_on_device(tokens, *rest)
    return blocks_on_device(tokens, *rest)


def solution(mesh):
    in_specs = (
        P("dp", "seq", None),
        P("dp", "seq", None),
        P("dp", None),
        P("dp", None),
        P("dp", "seq", None),
        P(),
        P(),
        P(),
        P(),
        P(),
        P(),
        P(),
        P(),
        P(),
        P(),
        P(),
        P(),
        P(),
        P(),
        P(),
        P(),
    )
    out_specs = (
        P("dp", "seq", None),
        P("dp", "seq", None),
        P("dp", "seq", None),
        P(),
        P(),
        P(),
        P(),
        P(),
        P(),
        P(),
        P(),
        P(),
        P(),
        P(),
        P(),
        P(),
        P(),
        P(),
        P(),
    )
    return jax.shard_map(
        on_device, mesh=mesh, in_specs=in_specs, out_specs=out_specs, check_vma=False
    )
```

```python
import functools
import jax
import jax.numpy as jnp
from jax import lax
from jax.experimental import pallas as pl
from jax.experimental.pallas import tpu as pltpu
from jax.sharding import PartitionSpec as P

HEADS = 8
HEAD = 64
NDOC = 32
AUG = HEAD + 16
MASKED = -1e9
LOG2E = 1.4426950408889634
SCALE = HEAD**-0.5
F32 = jnp.float32
BF16 = jnp.bfloat16
TB = 256

V_Q, V_V, V_SO, V_CQ, V_CV, V_CO, V_FI, V_FO, V_G, V_B = 0, 1, 2, 3, 4, 5, 6, 10, 11, 14
VECS = 24
G_IN, G_OUT, G_CO, G_CK, G_CQ, G_SO, G_QKV = 0, 4, 8, 9, 11, 12, 13
STREAMS = ((G_OUT, 20, 4), (G_IN, 16, 4), (G_CO, 20, 3), (G_CQ, 23, 2), (G_QKV, 16, 2), (G_QKV + 2, 18, 1))
UNITS, ALL_UNITS = 16, 25
PIECES = 8
STEPS = 8
COPIES = (1, 2, 2, 6, 6, 2, 2, 1)
OWN = sum(COPIES)


def vec_of(ref, start, length):
    return ref[start : start + length].astype(F32).reshape(1, length)


def mm(left, right, lc=1, rc=0):
    return lax.dot_general(
        left, right, (((lc,), (rc,)), ((), ())), preferred_element_type=F32
    )


def row_ids(lengths, row, size):
    rows, docs = lengths.shape
    at_row = lax.broadcasted_iota(jnp.int32, (rows, docs), 0) == row
    own = jnp.sum(jnp.where(at_row, lengths.astype(F32), 0.0), axis=0, keepdims=True)
    own = jnp.broadcast_to(own, (docs, docs))
    down = lax.broadcasted_iota(jnp.int32, (docs, docs), 0)
    over = lax.broadcasted_iota(jnp.int32, (docs, docs), 1)
    ends_col = jnp.sum(jnp.where(over <= down, own, 0.0), axis=1, keepdims=True)
    own_col = jnp.sum(jnp.where(over == down, own, 0.0), axis=1, keepdims=True)
    ends_row = jnp.sum(
        jnp.where(down <= over, jnp.broadcast_to(own_col, (docs, docs)), 0.0),
        axis=0,
        keepdims=True,
    )
    place_row = lax.broadcasted_iota(jnp.int32, (docs, size), 1).astype(F32)
    place_col = lax.broadcasted_iota(jnp.int32, (size, docs), 0).astype(F32)
    ids_row = jnp.sum(jnp.where(ends_col <= place_row, 1.0, 0.0), axis=0, keepdims=True)
    ids_col = jnp.sum(jnp.where(ends_row <= place_col, 1.0, 0.0), axis=1, keepdims=True)
    return ids_row, ids_col


def self_mask(mask_ref, lengths, row, size):
    ids_row, ids_col = row_ids(lengths, row, size)
    for kb in range(size // TB):
        for qb in range(kb, size // TB):
            ks, qs = slice(kb * TB, (kb + 1) * TB), slice(qb * TB, (qb + 1) * TB)
            seen = ids_col[ks] == ids_row[:, qs]
            if kb == qb:
                down = lax.broadcasted_iota(jnp.int32, (TB, TB), 0)
                over = lax.broadcasted_iota(jnp.int32, (TB, TB), 1)
                seen = seen & (down <= over)
            mask_ref[ks, qs] = jnp.where(seen, 0.0, MASKED)


def cross_mask(mask_ref, lengths, src_lengths, row, size, src):
    ids_row, _ = row_ids(lengths, row, size)
    _, src_col = row_ids(src_lengths, row, src)
    for qb in range(size // TB):
        qs = slice(qb * TB, (qb + 1) * TB)
        seen = (src_col == ids_row[:, qs]) | (ids_row[:, qs] == float(NDOC))
        mask_ref[:, qs] = jnp.where(seen, 0.0, MASKED)


def half_of(values, half):
    down = lax.broadcasted_iota(jnp.int32, values.shape, 0)
    keep = (down >= HEAD) if half else (down < HEAD)
    return jnp.where(keep, values, jnp.zeros_like(values))


def normalize(h):
    center = h - jnp.mean(h, axis=-1, keepdims=True)
    spread = jnp.mean(center * center, axis=-1, keepdims=True)
    rstd = lax.rsqrt(spread + 1e-05)
    return center * rstd, rstd


def norm_back(grad, xh, rstd, gain):
    gs = grad * gain
    m1 = jnp.mean(gs, axis=-1, keepdims=True)
    m2 = jnp.mean(gs * xh, axis=-1, keepdims=True)
    dh = (gs - m1 - xh * m2) * rstd
    return (
        dh,
        jnp.sum(grad * xh, axis=0, keepdims=True),
        jnp.sum(grad, axis=0, keepdims=True),
    )


def row_attend(k_ref, qt_ref, vt_ref, mask_ref, ctx_ref, lse_ref, size, key_end):
    @pl.loop(0, HEADS // 2)
    def _(pair):
        lanes = pl.ds(pl.multiple_of(pair * 2 * HEAD, 2 * HEAD), 2 * HEAD)
        for half in range(2):
            head = pair * 2 + half
            for qb in range(size // TB):
                ke, qs = key_end(qb), slice(qb * TB, (qb + 1) * TB)
                s = mm(k_ref[0:ke, lanes], half_of(qt_ref[lanes, qs], half))
                s = s + mask_ref[0:ke, qs]
                m = jnp.max(s, axis=0, keepdims=True)
                p = jnp.exp2(s - m).astype(BF16)
                o = mm(vt_ref[pl.ds(pl.multiple_of(head * AUG, 16), AUG), 0:ke], p)
                total = o[HEAD : HEAD + 1]
                ctx_ref[pl.ds(pl.multiple_of(head * HEAD, HEAD), HEAD), qs] = (
                    o[:HEAD] * (1.0 / total)
                ).astype(BF16)
                lse_ref[head, :, qs] = m + jnp.log2(total)


class Mover:
    def __init__(self, sems):
        self.sems, self.used, self.pending = sems, 0, {}

    def start(self, name, src, dst):
        copy = pltpu.make_async_copy(src, dst, self.sems.at[self.used])
        self.used += 1
        copy.start()
        self.pending[name] = copy

    def wait(self, *names):
        for name in names:
            self.pending.pop(name).wait()

    def finish(self):
        self.wait(*list(self.pending))


def meet(peers):
    barrier = pltpu.get_barrier_semaphore()
    for peer in peers:
        pl.semaphore_signal(barrier, inc=1, device_id=peer, device_id_type=pl.DeviceIdType.MESH)
    pl.semaphore_wait(barrier, len(peers))


def remote(src, dst, sends, recvs, index, peer):
    return pltpu.make_async_remote_copy(
        src_ref=src, dst_ref=dst, send_sem=sends.at[index], recv_sem=recvs.at[index],
        device_id=peer, device_id_type=pl.DeviceIdType.MESH,
    )


FWD_OUTS = 22


def forward_kernel(
    tok_ref, src_ref, cot_ref, tl_ref, sl_ref, bqv, bso, bcq, bcv, bco, gains, shifts,
    wqkv_h, wso_h, wcq_h, wckv_h, wco_h, *rest,
):
    outs, rest = rest[:FWD_OUTS], rest[FWD_OUTS:]
    cot_out = outs[0]
    kept, rest = rest[: FWD_OUTS - 1], rest[FWD_OUTS - 1 :]
    (wqkv_ref, wso_ref, wcq_ref, wckv_ref, wco_ref, mask, mask2, vt, v2t, y1,
     sems, sends, recvs) = rest
    (x_ref, mem_ref, q_ref, qt_ref, k_ref, kt_ref, v_ref, ctx_ref, lse_ref, xh1_ref, rs1_ref,
     q2_ref, q2t_ref, k2_ref, k2t_ref, v2_ref, c2_ref, lse2_ref, y2_ref, xh2_ref, rs2_ref) = kept
    size, width = x_ref.shape
    src = mem_ref.shape[0]
    seq = tok_ref.shape[0]
    blocks = size // TB
    row = lax.axis_index("seq")
    mover = Mover(sems)
    mover.start("wqkv", wqkv_h, wqkv_ref)
    mover.start("wckv", wckv_h, wckv_ref)
    mover.start("wso", wso_h, wso_ref)
    mover.start("wcq", wcq_h, wcq_ref)
    mover.start("wco", wco_h, wco_ref)

    def place(block, length):
        return pl.ds(pl.multiple_of(block * length, length), length)

    peers = [{"seq": lax.rem(row + d, seq)} for d in range(1, seq)]
    meet(peers)

    def exchange(source, target, length, kind):
        copies = []
        for d in range(1, seq):
            to = lax.rem(row + d, seq)
            copy = remote(source.at[to], target.at[place(row, length)], sends, recvs, kind * seq + d, {"seq": to})
            copy.start()
            copies.append(copy)
        mover.start((kind, "own"), source.at[row], target.at[place(row, length)])
        return copies

    tok_copies = exchange(tok_ref, x_ref, TB, 0)
    mem_copies = exchange(src_ref, mem_ref, src // seq, 1)

    for head in range(HEADS):
        vt[head * AUG + HEAD : (head + 1) * AUG, :] = jnp.ones((AUG - HEAD, size), BF16)
        v2t[head * AUG + HEAD : (head + 1) * AUG, :] = jnp.ones((AUG - HEAD, src), BF16)
    self_mask(mask, tl_ref[...], row, size)
    cross_mask(mask2, tl_ref[...], sl_ref[...], row, size, src)

    def put_vt(ref, values, place):
        for head in range(HEADS):
            ref[head * AUG : head * AUG + HEAD, place] = values[head * HEAD : (head + 1) * HEAD]

    mover.wait("wqkv", (0, "own"))
    for d in range(seq):
        if d:
            tok_copies[d - 1].wait_recv()
        ts = place(lax.rem(row + seq - d, seq), TB)
        xb = x_ref[ts, :]
        q = ((mm(xb, wqkv_ref[:, :width]) + vec_of(bqv, 0, width)) * (SCALE * LOG2E)).astype(BF16)
        q_ref[ts, :] = q
        qt_ref[:, ts] = q.T
        k = mm(xb, wqkv_ref[:, width : 2 * width]).astype(BF16)
        k_ref[ts, :] = k
        kt_ref[:, ts] = k.T
        v = (mm(xb, wqkv_ref[:, 2 * width :]) + vec_of(bqv, width, width)).astype(BF16)
        v_ref[ts, :] = v
        put_vt(vt, v.T, ts)
    mover.wait("wckv", (1, "own"))
    for copy in mem_copies:
        copy.wait_recv()
    cot_copies = exchange(cot_ref, cot_out, TB, 2)
    for i in (0, 1, 2, 3, 4, 5, 6):
        mover.start(i, kept[i], outs[1 + i])
    k2 = mm(mem_ref[...], wckv_ref[:, :width]).astype(BF16)
    k2_ref[...] = k2
    k2t_ref[...] = k2.T
    v2 = (mm(mem_ref[...], wckv_ref[:, width:]) + vec_of(bcv, 0, width)).astype(BF16)
    v2_ref[...] = v2
    put_vt(v2t, v2.T, slice(None))
    for i in (13, 14, 15):
        mover.start(i, kept[i], outs[1 + i])

    row_attend(k_ref, qt_ref, vt, mask, ctx_ref, lse_ref, size, lambda qb: (qb + 1) * TB)
    for i in (7, 8):
        mover.start(i, kept[i], outs[1 + i])
    mover.wait("wso", "wcq")
    for tb in range(blocks):
        ts = slice(tb * TB, (tb + 1) * TB)
        h1 = x_ref[ts, :].astype(F32) + mm(ctx_ref[:, ts].T, wso_ref[...]) + vec_of(bso, 0, width)
        xh, rstd = normalize(h1)
        xh1_ref[ts, :] = xh.astype(BF16)
        rs1_ref[ts, :] = rstd
        yb = xh * gains[0:1, :].astype(F32) + shifts[0:1, :].astype(F32)
        y1[ts, :] = yb
        q2 = ((mm(yb.astype(BF16), wcq_ref[...]) + vec_of(bcq, 0, width)) * (SCALE * LOG2E)).astype(BF16)
        q2_ref[ts, :] = q2
        q2t_ref[:, ts] = q2.T
    for i in (9, 10, 11, 12):
        mover.start(i, kept[i], outs[1 + i])
    row_attend(k2_ref, q2t_ref, v2t, mask2, c2_ref, lse2_ref, size, lambda qb: src)
    for i in (16, 17):
        mover.start(i, kept[i], outs[1 + i])
    mover.wait("wco")
    for tb in range(blocks):
        ts = slice(tb * TB, (tb + 1) * TB)
        h2 = y1[ts, :] + mm(c2_ref[:, ts].T, wco_ref[...]) + vec_of(bco, 0, width)
        xh, rstd = normalize(h2)
        xh2_ref[ts, :] = xh.astype(BF16)
        rs2_ref[ts, :] = rstd
        y2_ref[ts, :] = xh * gains[1:2, :].astype(F32) + shifts[1:2, :].astype(F32)
        for i in (18, 19, 20):
            mover.start((i, tb), kept[i].at[ts], outs[1 + i].at[ts])
    for copy in cot_copies:
        copy.wait_recv()
    for copy in tok_copies + mem_copies + cot_copies:
        copy.wait_send()
    mover.finish()


def row_attend_back(
    k_ref, kt_ref, v_ref, q_ref, qt_ref, dc_ref, dct_ref, ctx_ref, lse_ref, mask_ref,
    delta, dqt, dq_ref, dk_ref, dv_ref, size, keys, query_start, after,
):
    for pair in range(HEADS // 2):
        lanes = slice(pair * 2 * HEAD, (pair + 1) * 2 * HEAD)
        both = dct_ref[lanes, :].astype(F32) * ctx_ref[lanes, :].astype(F32)
        for half in range(2):
            delta[half] = jnp.sum(both[half * HEAD : (half + 1) * HEAD], axis=0, keepdims=True)
        dqt[...] = jnp.zeros_like(dqt)
        for kb in range(keys // TB):
            ks, qs = slice(kb * TB, (kb + 1) * TB), slice(query_start(kb), size)
            dks, dvs = [], []
            for half in range(2):
                head = pair * 2 + half
                rows = slice(head * HEAD, (head + 1) * HEAD)
                s = mm(k_ref[ks, lanes], half_of(qt_ref[lanes, qs], half))
                p = jnp.exp2(s + mask_ref[ks, qs] - lse_ref[head, :, qs])
                dp = mm(v_ref[ks, lanes], half_of(dct_ref[lanes, qs], half))
                ds = (p * (dp - delta[half, :, qs])).astype(BF16)
                dvs.append(mm(p.astype(BF16), dc_ref[qs, lanes]))
                dks.append(mm(ds, q_ref[qs, lanes]))
                dqt[half * HEAD : (half + 1) * HEAD, qs] += mm(kt_ref[rows, ks], ds)
            first = lax.broadcasted_iota(jnp.int32, (TB, 2 * HEAD), 1) < HEAD
            dv_ref[ks, lanes] = jnp.where(first, dvs[0], dvs[1]).astype(BF16)
            dk_ref[ks, lanes] = (jnp.where(first, dks[0], dks[1]) * (1.0 / LOG2E)).astype(BF16)
            after(pair, kb)
        dq_ref[:, lanes] = (dqt[...] * SCALE).astype(BF16).T


class Stream:
    def __init__(self, grads, sums, base, give, rows, slots, sems):
        dp, self.seq = lax.axis_index("dp"), lax.axis_size("seq")
        self.z = lax.axis_index("seq")
        self.core, x, y = lax.rem(dp, 2), lax.rem(dp // 2, 2), dp // 4
        self.near = {"dp": dp + 1 - 2 * self.core}
        by_x, by_y = {"dp": dp + 2 - 4 * x}, {"dp": dp + 4 - 8 * y}
        self.grads, self.sums, self.base, self.give, self.rows = grads, sums, base, give, rows
        self.slots, self.sems = slots, sems
        half, quarter, eighth = rows // 2, rows // 4, rows // 8
        self.unit = rows // (8 * self.seq)
        self.plan = []
        for part, (one, two, b1, b2) in enumerate(((x, y, by_x, by_y), (y, x, by_y, by_x))):
            start = part * half
            keep1, give1 = start + one * quarter, start + (1 - one) * quarter
            keep2, give2 = keep1 + two * eighth, keep1 + (1 - two) * eighth
            self.plan.append((b1, keep1, give1, b2, keep2, give2))

    def at(self, start, length):
        return pl.ds(pl.multiple_of(self.base + start, 16), length)

    def view(self, start, length):
        return self.grads.at[self.at(start, length)]

    def summed(self, start, length):
        return self.sums.at[self.core, self.at(start, length)]

    def own_copies(self):
        moves = [keep2 + self.z * self.unit for _, _, _, _, keep2, _ in self.plan]
        return [
            pltpu.make_async_copy(self.view(at, self.unit), self.summed(at, self.unit), self.sems[0].at[OWN + i])
            for i, at in enumerate(moves)
        ]

    def copies(self, step):
        rows, (s0, s1, s2, s3), seq = self.rows, self.slots, self.seq
        first = sum(COPIES[:step])
        sends, recvs = self.sems
        moves = []
        if step == 0:
            moves.append((self.grads.at[self.give : self.give + rows], s0, self.near))
        if step == 7:
            moves.append((self.summed(0, rows), self.summed(0, rows), self.near))
        for part, (b1, keep1, give1, b2, keep2, give2) in enumerate(self.plan):
            if step == 1:
                moves.append((self.view(give1, rows // 4), s1.at[part], b1))
            if step == 2:
                moves.append((self.view(give2, rows // 8), s2.at[part], b2))
            if step == 5:
                moves.append((self.summed(keep2, rows // 8), self.summed(keep2, rows // 8), b2))
            if step == 6:
                moves.append((self.summed(keep1, rows // 4), self.summed(keep1, rows // 4), b1))
            for d in range(1, seq):
                to = lax.rem(self.z + d, seq)
                if step == 3:
                    moves.append((self.view(keep2 + to * self.unit, self.unit), s3.at[part, d - 1], {"seq": to}))
                if step == 4:
                    own = keep2 + self.z * self.unit
                    moves.append((self.view(own, self.unit), self.summed(own, self.unit), {"seq": to}))
        return [remote(*move[:2], sends, recvs, first + i, move[2]) for i, move in enumerate(moves)]

    def add(self, start, slots, length):
        chunk = min(length, self.rows // 8)

        def at(i):
            place = pl.ds(pl.multiple_of(self.base + start + i * chunk, 16), chunk)
            total = self.grads[place, :].astype(F32)
            for slot in slots:
                total = total + slot[pl.ds(pl.multiple_of(i * chunk, 16), chunk), :].astype(F32)
            self.grads[place, :] = total.astype(BF16)

        if length == chunk:
            at(0)
        else:
            pl.loop(0, length // chunk)(at)

    def tick(self, step):
        if step:
            for copy in self.copies(step - 1):
                copy.wait()
        if step == 5:
            for copy in self.own_copies():
                copy.wait()
        s0, s1, s2, s3 = self.slots
        if step == 1:
            self.add(0, [s0], self.rows)
        for part, (_, keep1, _, _, keep2, _) in enumerate(self.plan):
            if step == 2:
                self.add(keep1, [s1.at[part]], self.rows // 4)
            if step == 3:
                self.add(keep2, [s2.at[part]], self.rows // 8)
            if step == 4:
                self.add(keep2 + self.z * self.unit, [s3.at[part, d] for d in range(self.seq - 1)], self.unit)
        if step < STEPS:
            for copy in self.copies(step):
                copy.start()
        if step == 4 and step < STEPS:
            for copy in self.own_copies():
                copy.start()


class VectorSum:
    def __init__(self, held, sems):
        dp, self.seq, self.z = lax.axis_index("dp"), lax.axis_size("seq"), lax.axis_index("seq")
        core, x, y = lax.rem(dp, 2), lax.rem(dp // 2, 2), dp // 4
        self.partners = [{"dp": dp + 1 - 2 * core}, {"dp": dp + 2 - 4 * x}, {"dp": dp + 4 - 8 * y}]
        self.held, self.sems = held, sems

    def copies(self, step):
        sends, recvs = self.sems
        if step < 3:
            return [remote(self.held.at[2 * step], self.held.at[2 * step + 1], sends, recvs, step, self.partners[step])]
        own = self.held.at[6 + self.z]
        return [remote(own, own, sends, recvs, 2 + d, {"seq": lax.rem(self.z + d, self.seq)}) for d in range(1, self.seq)]

    def tick(self, step):
        if step:
            for copy in self.copies(step - 1):
                copy.wait()
            if step < 4:
                to = 2 * step if step < 3 else 6 + self.z
                self.held[to] = self.held[2 * step - 2] + self.held[2 * step - 1]
        if step < 4:
            for copy in self.copies(step):
                copy.start()

    def total(self):
        values = self.held[6]
        for i in range(1, self.seq):
            values = values + self.held[6 + i]
        return values


INS = ("y2", "win", "cot", "wout", "xh2", "rs2", "co", "c2", "k2", "q2t", "v2", "k2t", "lse2", "mem", "ckv",
       "rs1", "kt", "k", "v", "q", "x", "q2", "xh1", "cq", "so", "qkv", "qt", "ctx", "lse")
HELD = INS[:17]
POOL = 14


def main_kernel(plan, tl_ref, sl_ref, bfi, bfo, gains, shifts, *rest):
    n = len(INS)
    hbm, rest = dict(zip(INS, rest[:n])), rest[n:]
    (out_h, dtok_h, dmem_h, sums_h, dvec_ref), rest = rest[:5], rest[5:]
    vmem, rest = dict(zip(HELD, rest[: len(HELD)])), rest[len(HELD) :]
    pool, rest = rest[:POOL], rest[POOL:]
    (out_row, dh1, mask, mask2, delta, dqt, dct, dk2, dv2, dmem, grads, held), rest = rest[:12], rest[12:]
    slots, rest = [rest[4 * i : 4 * i + 4] for i in range(len(STREAMS))], rest[4 * len(STREAMS) :]
    sems, sends, recvs, xsends, xrecvs = rest
    size, width = vmem["y2"].shape
    inner = vmem["win"].shape[1]
    src = vmem["mem"].shape[0]
    acts, dus, slopes, (y2b, dz_s) = pool[0:4], pool[4:8], pool[8:12], pool[12:14]
    vmem |= dict(zip(("k", "v", "q", "x"), pool[0:4]))
    dq, dk, dv, dc = pool[4:8]
    vmem |= {"q2": pool[8], "xh1": pool[9], "qt": vmem["q2t"], "ctx": vmem["c2"], "lse": vmem["lse2"]}
    wout = vmem["wout"]
    vmem |= {"cq": wout.at[0:width], "so": wout.at[width : 2 * width], "qkv": vmem["win"].at[:, : 3 * width]}
    y1b, dtok = y2b, dz_s
    cols = [slice(j, j + width) for j in range(0, inner, width)]
    blocks = [slice(t, t + TB) for t in range(0, size, TB)]
    seq, row, dp = lax.axis_size("seq"), lax.axis_index("seq"), lax.axis_index("dp")
    mover = Mover(sems)

    def load(*names):
        for name in names:
            mover.start(name, hbm[name], vmem[name])

    load(*HELD)
    split = [(keep * width, give * width, rows * width) for keep, give, rows in STREAMS]
    streams = [
        Stream(grads, sums_h, *where, slots[i], (sends.at[i], recvs.at[i])) for i, where in enumerate(split)
    ]
    vectors = VectorSum(held, (sends.at[len(STREAMS)], recvs.at[len(STREAMS)]))
    core, x, y = streams[0].core, lax.rem(dp // 2, 2), dp // 4
    pieces = []

    def send_piece(step):
        length = size // seq
        part = length // PIECES
        copies = []
        for d in range(1, seq):
            to = lax.rem(row + d, seq)
            rows = pl.ds(pl.multiple_of(to * length + step * part, 16), part)
            place = dtok_h.at[row, step * part : (step + 1) * part]
            copies.append(remote(dtok.at[rows], place, xsends, xrecvs, (3 + step) * seq + d, {"seq": to}))
        for copy in copies:
            copy.start()
        pieces.extend(copies)

    ticks = [s.tick for s in streams] + [vectors.tick, send_piece]

    def act(place):
        for stream, step in plan.get(place, ()):
            ticks[stream](step)

    meet(
        [{"dp": dp + 1 - 2 * core}, {"dp": dp + 2 - 4 * x}, {"dp": dp + 4 - 8 * y}]
        + [{"seq": lax.rem(row + d, seq)} for d in range(1, seq)]
    )

    def exchange(source, target, kind):
        length = source.shape[0] // seq
        copies = []
        for d in range(1, seq):
            to = lax.rem(row + d, seq)
            rows = pl.ds(pl.multiple_of(to * length, 16), length)
            copies.append(remote(source.at[rows], target.at[row], xsends, xrecvs, kind * seq + d, {"seq": to}))
        for copy in copies:
            copy.start()
        mover.start((kind, "own"), source.at[pl.ds(pl.multiple_of(row * length, 16), length)], target.at[row])
        return copies

    gives = {keep + i: give + i for keep, give, rows in STREAMS for i in range(rows)}

    def gather(i, values):
        half = width // 2
        keep, give = i * width, gives[i] * width
        left = pl.multiple_of(jnp.where(core == 0, keep, give), width)
        right = pl.multiple_of(jnp.where(core == 0, give, keep), width)
        grads[pl.ds(left, width), :] = values[:, :half].astype(BF16)
        grads[pl.ds(right, width), :] = values[:, half:].astype(BF16)

    def total(values):
        return jnp.sum(values.astype(F32), axis=0, keepdims=True)

    def count(i, values):
        dvec_ref[i : i + 1, :] += values

    gain0, shift0 = gains[0:1, :].astype(F32), shifts[0:1, :].astype(F32)
    gain1, gain2, shift2 = gains[1:2, :].astype(F32), gains[2:3, :].astype(F32), shifts[2:3, :].astype(F32)
    dvec_ref[...] = jnp.zeros_like(dvec_ref)
    mover.wait("y2", "win", "cot", "wout")
    y2_ref, win = vmem["y2"], vmem["win"]

    @pl.loop(0, size // TB)
    def _(tb):
        ts = pl.ds(pl.multiple_of(tb * TB, TB), TB)
        y2 = y2_ref[ts, :]
        low = y2.astype(BF16)
        y2b[ts, :] = low
        h3 = y2 + vec_of(bfo, 0, width)
        for j, cs in enumerate(cols):
            u = mm(low, win[:, cs]) + vec_of(bfi, j * width, width)
            sg = 0.5 * jnp.tanh(0.5 * u) + 0.5
            a = u * sg
            slopes[j][ts, :] = (sg + a * (1.0 - sg)).astype(BF16)
            a = a.astype(BF16)
            acts[j][ts, :] = a
            h3 = h3 + mm(a, wout[cs, :])
        xh, rstd = normalize(h3)
        out_row[ts, :] = (xh * gain2 + shift2).astype(BF16)
        dh3, dg, db = norm_back(vmem["cot"][ts, :].astype(F32), xh, rstd, gain2)
        y2_ref[ts, :] = dh3
        dz = dh3.astype(BF16)
        dz_s[ts, :] = dz
        count(V_G + 2, dg)
        count(V_B + 2, db)
        count(V_FO, total(dz))

    out_copies = exchange(out_row, out_h, 0)
    for j in range(len(cols)):
        gather(G_OUT + j, mm(acts[j][...], dz_s[...], 0, 0))
    act("ffn_out")
    load("k", "v", "q", "x")
    mover.wait("xh2", "rs2")
    for tb, ts in enumerate(blocks):
        dz = dz_s[ts, :]
        dy2 = y2_ref[ts, :]
        for j, cs in enumerate(cols):
            du = (mm(dz, wout[cs, :], 1, 1) * slopes[j][ts, :].astype(F32)).astype(BF16)
            dus[j][ts, :] = du
            count(V_FI + j, total(du))
            dy2 = dy2 + mm(du, win[:, cs], 1, 1)
            if j == 1:
                act(("ffn", tb, 0))
        dh2, dg, db = norm_back(dy2, vmem["xh2"][ts, :].astype(F32), vmem["rs2"][ts, :], gain1)
        y2_ref[ts, :] = dh2
        count(V_G + 1, dg)
        count(V_B + 1, db)
        act(("ffn", tb, 1))

    load("q2", "xh1", "cq", "so", "qkv")
    dh2_ref = y2_ref
    for j in range(len(cols)):
        gather(G_IN + j, mm(y2b[...], dus[j][...], 0, 0))
        act(("in", j))
    act("ffn_in")
    cross_mask(mask2, tl_ref[...], sl_ref[...], row, size, src)
    act("mask2")
    mover.wait("co", "c2")
    for tb, ts in enumerate(blocks):
        da2 = dh2_ref[ts, :].astype(BF16)
        dc[ts, :] = mm(da2, vmem["co"][...], 1, 1).astype(BF16)
        dct[:, ts] = mm(vmem["co"][...], da2, 1, 1).astype(BF16)
        count(V_CO, total(da2))
        act(("cin", tb))
    act("cross_in")
    gather(G_CO, mm(vmem["c2"][...], dh2_ref[...].astype(BF16)))
    act("cross_out")
    mover.wait("k2", "q2t", "v2", "k2t", "lse2", "q2")
    row_attend_back(
        vmem["k2"], vmem["k2t"], vmem["v2"], vmem["q2"], vmem["q2t"], dc, dct, vmem["c2"], vmem["lse2"], mask2,
        delta, dqt, dq, dk2, dv2, size, src, lambda kb: 0, lambda i, j: act(("cross", i, j)),
    )
    load("qt", "ctx", "lse")
    count(V_CV, total(dv2[...]))
    count(V_CQ, total(dq[...]))
    mover.wait("mem", "ckv", "cq", "xh1", "rs1", "so")
    gather(G_CK, mm(vmem["mem"][...], dk2[...], 0, 0))
    gather(G_CK + 1, mm(vmem["mem"][...], dv2[...], 0, 0))
    act("ck")
    w_ckv = vmem["ckv"]
    dmem[...] = (mm(dk2[...], w_ckv[:, :width], 1, 1) + mm(dv2[...], w_ckv[:, width:], 1, 1)).astype(BF16)
    act("memory")
    mem_copies = exchange(dmem, dmem_h, 2)
    for tb, ts in enumerate(blocks):
        dy1 = dh2_ref[ts, :] + mm(dq[ts, :], vmem["cq"][...], 1, 1)
        xh1 = vmem["xh1"][ts, :].astype(F32)
        y1b[ts, :] = (xh1 * gain0 + shift0).astype(BF16)
        dh, dg, db = norm_back(dy1, xh1, vmem["rs1"][ts, :], gain0)
        count(V_G, dg)
        count(V_B, db)
        dh1[ts, :] = dh
        count(V_SO, total(dh.astype(BF16)))
        act(("nrm", tb))
    act("norm")
    gather(G_CQ, mm(y1b[...], dq[...], 0, 0))
    act("query")
    self_mask(mask, tl_ref[...], row, size)
    act("mask")
    mover.wait("ctx")
    gather(G_SO, mm(vmem["ctx"][...], dh1[...].astype(BF16)))
    act("self_out")
    for tb, ts in enumerate(blocks):
        da1 = dh1[ts, :].astype(BF16)
        dc[ts, :] = mm(da1, vmem["so"][...], 1, 1).astype(BF16)
        dct[:, ts] = mm(vmem["so"][...], da1, 1, 1).astype(BF16)
        act(("sin", tb))
    act("self_in")
    mover.wait("k", "qt", "v", "q", "kt", "lse")
    row_attend_back(
        vmem["k"], vmem["kt"], vmem["v"], vmem["q"], vmem["qt"], dc, dct, vmem["ctx"], vmem["lse"], mask,
        delta, dqt, dq, dk, dv, size, size, lambda kb: kb * TB, lambda i, j: act(("self", i, j)),
    )
    mover.wait("x", "qkv")
    for i, part in enumerate((dq, dk, dv)):
        gather(G_QKV + i, mm(vmem["x"][...], part[...], 0, 0))
    act("qkv")
    count(V_Q, total(dq[...]))
    count(V_V, total(dv[...]))
    held[0] = dvec_ref[...]
    act("vectors")
    w_qkv = vmem["qkv"]
    for tb, ts in enumerate(blocks):
        dtok[ts, :] = (
            dh1[ts, :]
            + mm(dq[ts, :], w_qkv[:, :width], 1, 1)
            + mm(dk[ts, :], w_qkv[:, width : 2 * width], 1, 1)
            + mm(dv[ts, :], w_qkv[:, 2 * width :], 1, 1)
        ).astype(BF16)
        act(("tok", tb))
    own = pl.ds(pl.multiple_of(row * (size // seq), 16), size // seq)
    mover.start("own tokens", dtok.at[own], dtok_h.at[row])
    act("tokens")
    act("end")
    dvec_ref[...] = vectors.total()
    for copy in out_copies + pieces + mem_copies:
        copy.wait()
    mover.finish()


PLAN = {
    "ffn_out": [(0, 0)],
    ("ffn", 1, 0): [(0, 1)],
    "ffn_in": [(1, 0)],
    "mask2": [(0, 2)],
    "cross_in": [(1, 1)],
    ("cross", 2, 0): [(0, 3)],
    "ck": [(2, 0)],
    ("nrm", 2): [(1, 2), (2, 1)],
    "self_out": [(3, 0), (0, 4)],
    "self_in": [(3, 1)],
    ("self", 0, 0): [(1, 3)],
    ("self", 1, 0): [(2, 2)],
    ("self", 1, 2): [(0, 5)],
    ("self", 1, 3): [(3, 2)],
    ("self", 2, 2): [(2, 3)],
    ("self", 3, 0): [(1, 4)],
    ("self", 3, 1): [(0, 6)],
    ("self", 3, 2): [(3, 3)],
    "qkv": [(4, 0), (5, 0)],
    ("tok", 1): [(2, 4)],
    ("tok", 2): [(4, 1), (5, 1)],
    "end": [(0, 7), (1, 5), (0, 8), (4, 2), (3, 4), (5, 2), (1, 6), (6, 2), (2, 5), (7, 0), (4, 3), (5, 3), (3, 5), (1, 7), (7, 1), (6, 3), (4, 4), (2, 6), (5, 4), (1, 8), (3, 6), (4, 5), (7, 2), (6, 4), (2, 7), (5, 5), (2, 8), (7, 3), (3, 7), (4, 6), (3, 8), (7, 4), (5, 6), (4, 7), (7, 5), (5, 7), (4, 8), (5, 8), (7, 6), (7, 7)],
    "vectors": [(6, 0)],
    "tokens": [(6, 1)],
}


def unpack_kernel(grads_h, dvec_ref, dtok_h, dmem_h, *rest):
    outs, rest = rest[:18], rest[18:]
    mats, vecs = outs[:9], outs[9:]
    grads, dtok, dmem, rest = rest[0], rest[1], rest[2], rest[3:]
    wide, sems = rest[:9], rest[9]
    mover = Mover(sems)
    width = 2 * grads.shape[2]
    half = width // 2
    plan = ((0, G_QKV, 1, 3), (1, G_SO, 1, 1), (2, G_CQ, 1, 1), (3, G_CK, 1, 2), (4, G_CO, 1, 1), (5, G_IN, 1, 4), (6, G_OUT, 4, 1))
    for i, base, units, blocks in plan:
        rows = slice(base * width, (base + units * blocks) * width)
        mover.start(i, grads_h.at[:, rows], grads.at[:, rows])
    mover.start("tok", dtok_h, dtok)
    mover.start("mem", dmem_h, dmem)
    for i, base, units, blocks in plan:
        mover.wait(i)
        for b in range(blocks):
            for u in range(units):
                rows = slice((base + b + u) * width, (base + b + u + 1) * width)
                for c in range(2):
                    wide[i][u * width : (u + 1) * width, b * width + c * half : b * width + (c + 1) * half] = grads[c, rows, :].astype(F32)
        mover.start((i, "out"), wide[i], mats[i])
    for i, name, source in ((7, "tok", dtok), (8, "mem", dmem)):
        mover.wait(name)
        wide[i][...] = source[...].astype(F32)
        mover.start((i, "out"), wide[i], mats[i])
    place = 0
    for ref in vecs:
        if len(ref.shape) == 2:
            ref[...] = dvec_ref[place : place + ref.shape[0], :]
            place += ref.shape[0]
        else:
            for j in range(ref.shape[0] // width):
                ref[j * width : (j + 1) * width] = dvec_ref[place, :]
                place += 1
    mover.finish()


WHOLE = pl.BlockSpec(memory_space=pltpu.VMEM)


def call(kernel, ins, outs, scratch, name):
    return pl.pallas_call(
        kernel,
        out_shape=[jax.ShapeDtypeStruct(*o) for o in outs],
        in_specs=[WHOLE] * len(ins),
        out_specs=[WHOLE] * len(outs),
        scratch_shapes=[pltpu.VMEM(*s) for s in scratch],
        compiler_params=pltpu.CompilerParams(vmem_limit_bytes=60 * 2**20),
        name=name,
    )(*ins)


ANY = pl.BlockSpec(memory_space=pl.ANY)


def forward(tokens, memory, cot, tl, sl, small, wqkv, wso, wcq, wckv, wco):
    seq, block, d = tokens.shape
    t, s = seq * block, seq * memory.shape[1]
    tok, feat, row = ((t, d), BF16), ((d, t), BF16), ((HEADS, 1, t), F32)
    col, mem = ((t, 1), F32), ((s, d), BF16)
    kept = [tok, mem, tok, feat, tok, feat, tok, feat, row, tok, col,
            tok, feat, mem, ((d, s), BF16), mem, feat, row, ((t, d), F32), tok, col]
    weights = (wqkv, wso, wcq, wckv, wco)
    scratch = kept + [(w.shape, w.dtype) for w in weights]
    scratch += [((t, t), F32), ((s, t), F32), ((HEADS * AUG, t), BF16), ((HEADS * AUG, s), BF16), ((t, d), F32)]
    return pl.pallas_call(
        forward_kernel,
        out_shape=[jax.ShapeDtypeStruct(*o) for o in [tok] + kept],
        in_specs=[ANY] * 3 + [WHOLE] * (2 + len(small)) + [ANY] * 5,
        out_specs=[ANY] * FWD_OUTS,
        scratch_shapes=[pltpu.VMEM(*x) for x in scratch]
        + [pltpu.SemaphoreType.DMA((40,)), pltpu.SemaphoreType.DMA((3 * seq,)), pltpu.SemaphoreType.DMA((3 * seq,))],
        compiler_params=pltpu.CompilerParams(vmem_limit_bytes=60 * 2**20, collective_id=0, has_side_effects=True),
        name="forward",
    )(tokens, memory, cot, tl, sl, *small, *weights)


def main(tl, sl, small, ins):
    t, d = ins["y2"].shape
    s = ins["mem"].shape[0]
    seq = lax.axis_size("seq")
    tok, mem, wide = ((t, d), BF16), ((s, d), BF16), ((t, d), F32)
    scratch = [(ins[name].shape, ins[name].dtype) for name in HELD] + [tok] * POOL
    scratch += [tok, wide, ((t, t), F32), ((s, t), F32), ((2, 1, t), F32), ((2 * HEAD, t), F32), ((d, t), BF16),
                mem, mem, mem, ((ALL_UNITS * d, d // 2), BF16), ((6 + seq, VECS, d), F32)]
    for _, _, rows in STREAMS:
        r, c = rows * d, d // 2
        scratch += [((r, c), BF16), ((2, r // 4, c), BF16), ((2, r // 8, c), BF16), ((2, seq - 1, r // (8 * seq), c), BF16)]
    steps = pltpu.SemaphoreType.DMA((len(STREAMS) + 1, OWN + 2))
    return pl.pallas_call(
        functools.partial(main_kernel, PLAN),
        out_shape=[
            jax.ShapeDtypeStruct((seq, t // seq, d), BF16),
            jax.ShapeDtypeStruct((seq, t // seq, d), BF16),
            jax.ShapeDtypeStruct((seq, s // seq, d), BF16),
            jax.ShapeDtypeStruct((2, UNITS * d, d // 2), BF16),
            jax.ShapeDtypeStruct((VECS, d), F32),
        ],
        in_specs=[WHOLE] * 6 + [ANY] * len(INS),
        out_specs=[ANY] * 4 + [WHOLE],
        scratch_shapes=[pltpu.VMEM(*x) for x in scratch]
        + [pltpu.SemaphoreType.DMA((40,)), steps, steps] + [pltpu.SemaphoreType.DMA(((3 + PIECES) * seq,))] * 2,
        compiler_params=pltpu.CompilerParams(vmem_limit_bytes=62 * 2**20, collective_id=1, has_side_effects=True),
        name="main",
    )(tl, sl, *small, *[ins[name] for name in INS])


def unpack(grads, dvec, dtok, dmem, d, f):
    mats = [(d, 3 * d), (d, d), (d, d), (d, 2 * d), (d, d), (d, f), (f, d), dtok.shape, dmem.shape]
    vecs = [(2 * d,), (d,), (d,), (d,), (d,), (f,), (d,), (3, d), (3, d)]
    outs = pl.pallas_call(
        unpack_kernel,
        out_shape=[jax.ShapeDtypeStruct(o, F32) for o in mats + vecs],
        in_specs=[ANY, WHOLE, ANY, ANY],
        out_specs=[ANY] * 9 + [WHOLE] * 9,
        scratch_shapes=[pltpu.VMEM(x.shape, x.dtype) for x in (grads, dtok, dmem)]
        + [pltpu.VMEM(m, F32) for m in mats] + [pltpu.SemaphoreType.DMA((24,))],
        compiler_params=pltpu.CompilerParams(vmem_limit_bytes=60 * 2**20),
        name="unpack",
    )(grads, dvec, dtok, dmem)
    d_qkv, d_so, d_cq, d_ckv, d_co, d_fi, d_fo, d_tok, d_mem = outs[:9]
    v_qv, v_so, v_cq, v_cv, v_co, v_fi, v_fo, d_gains, d_shifts = outs[9:]
    return (d_tok, d_mem, d_qkv, v_qv, d_so, v_so, d_cq, v_cq, d_ckv, v_cv, d_co, v_co, d_fi, v_fi, d_fo, v_fo, d_gains, d_shifts)


def layer_norm(values, gain, shift):
    center = values - jnp.mean(values, axis=-1, keepdims=True)
    spread = jnp.mean(center * center, axis=-1, keepdims=True)
    return center * lax.rsqrt(spread + 1e-05) * gain + shift


def doc_ids(lengths, size):
    ends = jnp.cumsum(lengths, axis=1)
    places = jnp.arange(size, dtype=jnp.int32)
    return jnp.sum((ends[:, None, :] <= places[None, :, None]).astype(jnp.int32), axis=2)


def block_width(key_total):
    return 512 if key_total % 512 == 0 else key_total


def contract_rows(left, right):
    return lax.dot_general(
        left, right, (((0,), (0,)), ((), ())), preferred_element_type=jnp.float32
    )


def contract_cols(left, right):
    return lax.dot_general(
        left, right, (((1,), (1,)), ((), ())), preferred_element_type=jnp.float32
    )


def block_scores(queries, keys, allowed, start_at, width_of, score_scale):
    key_block = lax.dynamic_slice_in_dim(keys, start_at, width_of, 1)
    scores = (
        jnp.einsum("rqhd,rkhd->rhqk", queries, key_block, preferred_element_type=jnp.float32)
        * score_scale
    )
    return jnp.where(allowed(start_at, width_of)[:, None], scores, -1000000000.0)


def attend_forward(queries, keys, values, allowed, skip_after, score_scale):
    row_count, query_count, head_count, head_size = queries.shape
    key_total = keys.shape[1]
    width_of = block_width(key_total)
    block_count = key_total // width_of

    def statistics(carried, block_index):
        start_at = block_index * width_of

        def statistics_work(state):
            running_max, running_sum = state
            scores = block_scores(queries, keys, allowed, start_at, width_of, score_scale)
            new_max = jnp.maximum(running_max, jnp.max(scores, axis=3))
            new_sum = running_sum * jnp.exp(running_max - new_max) + jnp.sum(
                jnp.exp(scores - new_max[..., None]), axis=3
            )
            return (new_max, new_sum)

        return (
            lax.cond(start_at > skip_after, lambda state: state, statistics_work, carried),
            None,
        )

    stat_shape = (row_count, head_count, query_count)
    start_state = (
        jnp.full(stat_shape, -1000000000.0, jnp.float32),
        jnp.zeros(stat_shape, jnp.float32),
    )
    block_numbers = jnp.arange(block_count, dtype=jnp.int32)
    (running_max, running_sum), _ = lax.scan(statistics, start_state, block_numbers)
    log_total = running_max + jnp.log(running_sum)

    def mixing(carried, block_index):
        start_at = block_index * width_of

        def mixing_work(accum):
            scores = block_scores(queries, keys, allowed, start_at, width_of, score_scale)
            probs = jnp.exp(scores - log_total[..., None]).astype(jnp.bfloat16)
            value_block = lax.dynamic_slice_in_dim(values, start_at, width_of, 1)
            return accum + jnp.einsum(
                "rhqk,rkhd->rqhd", probs, value_block, preferred_element_type=jnp.float32
            )

        return (lax.cond(start_at > skip_after, lambda accum: accum, mixing_work, carried), None)

    start_accum = jnp.zeros((row_count, query_count, head_count, head_size), jnp.float32)
    accum, _ = lax.scan(mixing, start_accum, block_numbers)
    return (accum, log_total)


def attend_back(
    queries, keys, values, allowed, skip_after, score_scale, log_total, grad_out, delta
):
    row_count, query_count, head_count, head_size = queries.shape
    key_total = keys.shape[1]
    width_of = block_width(key_total)
    block_count = key_total // width_of

    def step(block_index, state):
        start_at = block_index * width_of

        def step_work(inner):
            scores = block_scores(queries, keys, allowed, start_at, width_of, score_scale)
            probs = jnp.exp(scores - log_total[..., None])
            key_block = lax.dynamic_slice_in_dim(keys, start_at, width_of, 1)
            value_block = lax.dynamic_slice_in_dim(values, start_at, width_of, 1)
            grad_probs = jnp.einsum(
                "rqhd,rkhd->rhqk", grad_out, value_block, preferred_element_type=jnp.float32
            )
            grad_scores = (probs * (grad_probs - delta[..., None])).astype(jnp.bfloat16)
            grad_query = (
                inner[0]
                + jnp.einsum(
                    "rhqk,rkhd->rqhd", grad_scores, key_block, preferred_element_type=jnp.float32
                )
                * score_scale
            )
            key_part = (
                jnp.einsum(
                    "rhqk,rqhd->rkhd", grad_scores, queries, preferred_element_type=jnp.float32
                )
                * score_scale
            )
            value_part = jnp.einsum(
                "rhqk,rqhd->rkhd",
                probs.astype(jnp.bfloat16),
                grad_out,
                preferred_element_type=jnp.float32,
            )
            grad_keys = lax.dynamic_update_slice_in_dim(inner[1], key_part, start_at, 1)
            grad_values = lax.dynamic_update_slice_in_dim(inner[2], value_part, start_at, 1)
            return (grad_query, grad_keys, grad_values)

        return lax.cond(start_at > skip_after, lambda inner: inner, step_work, state)

    start_state = (jnp.zeros((row_count, query_count, head_count, head_size), jnp.float32),)
    start_state = start_state + (
        jnp.zeros((row_count, key_total, head_count, head_size), jnp.float32),
        jnp.zeros((row_count, key_total, head_count, head_size), jnp.float32),
    )
    return lax.fori_loop(0, block_count, step, start_state)


def blocks_on_device(
    tokens,
    memory,
    doc_lengths,
    src_lengths,
    cotangent,
    w_qkv,
    qv_bias,
    self_out,
    self_out_bias,
    cross_query,
    cross_q_bias,
    cross_kv,
    cross_v_bias,
    cross_out,
    cross_out_bias,
    ffn_in,
    ffn_in_bias,
    ffn_out,
    ffn_out_bias,
    norm_gains,
    norm_biases,
):
    row_count, block_len, model_width = tokens.shape
    src_block = memory.shape[1]
    seq_count = lax.axis_size("seq")
    row_length = block_len * seq_count
    src_length = src_block * seq_count
    score_scale = HEAD ** (-0.5)
    first_place = lax.axis_index("seq") * block_len
    last_place = first_place + block_len - 1
    target_ids = doc_ids(doc_lengths, row_length)
    source_ids = doc_ids(src_lengths, src_length)
    own_ids = lax.dynamic_slice_in_dim(target_ids, first_place, block_len, 1)
    own_places = first_place + jnp.arange(block_len, dtype=jnp.int32)

    def self_allowed(start_at, width_of):
        key_ids = lax.dynamic_slice_in_dim(target_ids, start_at, width_of, 1)
        key_places = start_at + jnp.arange(width_of, dtype=jnp.int32)
        return (own_ids[:, :, None] == key_ids[:, None, :]) & (
            key_places[None, None, :] <= own_places[None, :, None]
        )

    def cross_allowed(start_at, width_of):
        return (own_ids[:, :, None] == source_ids[:, None, :]) | (own_ids[:, :, None] == NDOC)

    def split_heads(array_in):
        return array_in.reshape(array_in.shape[0], array_in.shape[1], HEADS, HEAD)

    token_rows = row_count * block_len
    flat_tokens = tokens.reshape(token_rows, model_width)
    flat_memory = memory.reshape(row_count * src_block, model_width)
    pair_bias = qv_bias.astype(jnp.float32)
    gains = norm_gains.astype(jnp.float32)
    shifts = norm_biases.astype(jnp.float32)
    packed = jnp.dot(flat_tokens, w_qkv, preferred_element_type=jnp.float32)
    self_queries = (packed[:, :model_width] + pair_bias[:model_width]).astype(jnp.bfloat16)
    self_keys = (
        packed[:, model_width : 2 * model_width]
        .astype(jnp.bfloat16)
        .reshape(row_count, block_len, model_width)
    )
    self_values = (
        (packed[:, 2 * model_width :] + pair_bias[model_width:])
        .astype(jnp.bfloat16)
        .reshape(row_count, block_len, model_width)
    )
    memory_pair = jnp.dot(flat_memory, cross_kv, preferred_element_type=jnp.float32)
    cross_keys = (
        memory_pair[:, :model_width].astype(jnp.bfloat16).reshape(row_count, src_block, model_width)
    )
    cross_values = (
        (memory_pair[:, model_width:] + cross_v_bias.astype(jnp.float32))
        .astype(jnp.bfloat16)
        .reshape(row_count, src_block, model_width)
    )
    all_keys, all_values, all_ckeys, all_cvalues = (
        lax.all_gather(self_keys, "seq", axis=1, tiled=True),
        lax.all_gather(self_values, "seq", axis=1, tiled=True),
        lax.all_gather(cross_keys, "seq", axis=1, tiled=True),
        lax.all_gather(cross_values, "seq", axis=1, tiled=True),
    )
    query_heads = split_heads(self_queries.reshape(row_count, block_len, model_width))
    self_accum, self_log = attend_forward(
        query_heads,
        split_heads(all_keys),
        split_heads(all_values),
        self_allowed,
        last_place,
        score_scale,
    )
    context_low = self_accum.reshape(token_rows, model_width).astype(jnp.bfloat16)
    inputs_f = flat_tokens.astype(jnp.float32)
    first_sum = (
        inputs_f
        + jnp.dot(context_low, self_out, preferred_element_type=jnp.float32)
        + self_out_bias.astype(jnp.float32)
    )
    first_norm, first_pull = jax.vjp(layer_norm, first_sum, gains[0], shifts[0])
    first_low = first_norm.astype(jnp.bfloat16)
    cross_q_rows = (
        jnp.dot(first_low, cross_query, preferred_element_type=jnp.float32)
        + cross_q_bias.astype(jnp.float32)
    ).astype(jnp.bfloat16)
    cross_heads = split_heads(cross_q_rows.reshape(row_count, block_len, model_width))
    cross_accum, cross_log = attend_forward(
        cross_heads,
        split_heads(all_ckeys),
        split_heads(all_cvalues),
        cross_allowed,
        src_length,
        score_scale,
    )
    cross_low = cross_accum.reshape(token_rows, model_width).astype(jnp.bfloat16)
    second_sum = (
        first_norm
        + jnp.dot(cross_low, cross_out, preferred_element_type=jnp.float32)
        + cross_out_bias.astype(jnp.float32)
    )
    second_norm, second_pull = jax.vjp(layer_norm, second_sum, gains[1], shifts[1])
    second_low = second_norm.astype(jnp.bfloat16)
    hidden_pre = jnp.dot(
        second_low, ffn_in, preferred_element_type=jnp.float32
    ) + ffn_in_bias.astype(jnp.float32)
    hidden_low = jax.nn.silu(hidden_pre).astype(jnp.bfloat16)
    third_sum = (
        second_norm
        + jnp.dot(hidden_low, ffn_out, preferred_element_type=jnp.float32)
        + ffn_out_bias.astype(jnp.float32)
    )
    result, third_pull = jax.vjp(layer_norm, third_sum, gains[2], shifts[2])
    output = result.astype(jnp.bfloat16).reshape(row_count, block_len, model_width)
    grad_third, gain_three, shift_three = third_pull(
        cotangent.reshape(token_rows, model_width).astype(jnp.float32)
    )
    grad_branch = grad_third.astype(jnp.bfloat16)
    d_ffn_out = contract_rows(hidden_low, grad_branch)
    d_ffn_out_bias = jnp.sum(grad_branch.astype(jnp.float32), axis=0)
    grad_hidden = contract_cols(grad_branch, ffn_out)
    sigmoid_pre = jax.nn.sigmoid(hidden_pre)
    grad_pre = (grad_hidden * sigmoid_pre * (1.0 + hidden_pre * (1.0 - sigmoid_pre))).astype(
        jnp.bfloat16
    )
    d_ffn_in = contract_rows(second_low, grad_pre)
    d_ffn_in_bias = jnp.sum(grad_pre.astype(jnp.float32), axis=0)
    grad_second_norm = grad_third + contract_cols(grad_pre, ffn_in)
    back_keys, back_values, back_ckeys, back_cvalues = (
        all_keys,
        all_values,
        all_ckeys,
        all_cvalues,
    )
    grad_second, gain_two, shift_two = second_pull(grad_second_norm)
    grad_cross_branch = grad_second.astype(jnp.bfloat16)
    d_cross_out = contract_rows(cross_low, grad_cross_branch)
    d_cross_out_bias = jnp.sum(grad_cross_branch.astype(jnp.float32), axis=0)
    grad_cross_ctx = contract_cols(grad_cross_branch, cross_out).astype(jnp.bfloat16)
    grad_cross_heads = split_heads(grad_cross_ctx.reshape(row_count, block_len, model_width))
    cross_delta = jnp.swapaxes(
        jnp.sum(grad_cross_heads.astype(jnp.float32) * cross_accum, axis=3), 1, 2
    )
    grad_cq, grad_ck_all, grad_cv_all = attend_back(
        cross_heads,
        split_heads(back_ckeys),
        split_heads(back_cvalues),
        cross_allowed,
        src_length,
        score_scale,
        cross_log,
        grad_cross_heads,
        cross_delta,
    )
    grad_ck_own, grad_cv_own = (
        lax.psum_scatter(
            grad_ck_all.reshape(row_count, src_length, model_width).astype(jnp.bfloat16),
            "seq",
            scatter_dimension=1,
            tiled=True,
        ).astype(jnp.float32),
        lax.psum_scatter(
            grad_cv_all.reshape(row_count, src_length, model_width).astype(jnp.bfloat16),
            "seq",
            scatter_dimension=1,
            tiled=True,
        ).astype(jnp.float32),
    )
    grad_pair = jnp.concatenate(
        [
            grad_ck_own.reshape(row_count * src_block, model_width).astype(jnp.bfloat16),
            grad_cv_own.reshape(row_count * src_block, model_width).astype(jnp.bfloat16),
        ],
        axis=1,
    )
    d_cross_kv = contract_rows(flat_memory, grad_pair)
    d_cross_v_bias = jnp.sum(grad_pair[:, model_width:].astype(jnp.float32), axis=0)
    d_memory = contract_cols(grad_pair, cross_kv).reshape(row_count, src_block, model_width)
    grad_cq_low = grad_cq.reshape(token_rows, model_width).astype(jnp.bfloat16)
    d_cross_query = contract_rows(first_low, grad_cq_low)
    d_cross_q_bias = jnp.sum(grad_cq_low.astype(jnp.float32), axis=0)
    grad_first_norm = grad_second + contract_cols(grad_cq_low, cross_query)
    grad_first, gain_one, shift_one = first_pull(grad_first_norm)
    grad_self_branch = grad_first.astype(jnp.bfloat16)
    d_self_out = contract_rows(context_low, grad_self_branch)
    d_self_out_bias = jnp.sum(grad_self_branch.astype(jnp.float32), axis=0)
    grad_context = contract_cols(grad_self_branch, self_out).astype(jnp.bfloat16)
    grad_context_heads = split_heads(grad_context.reshape(row_count, block_len, model_width))
    self_delta = jnp.swapaxes(
        jnp.sum(grad_context_heads.astype(jnp.float32) * self_accum, axis=3), 1, 2
    )
    grad_q, grad_k_all, grad_v_all = attend_back(
        query_heads,
        split_heads(back_keys),
        split_heads(back_values),
        self_allowed,
        last_place,
        score_scale,
        self_log,
        grad_context_heads,
        self_delta,
    )
    grad_k_own, grad_v_own = (
        lax.psum_scatter(
            grad_k_all.reshape(row_count, row_length, model_width).astype(jnp.bfloat16),
            "seq",
            scatter_dimension=1,
            tiled=True,
        ).astype(jnp.float32),
        lax.psum_scatter(
            grad_v_all.reshape(row_count, row_length, model_width).astype(jnp.bfloat16),
            "seq",
            scatter_dimension=1,
            tiled=True,
        ).astype(jnp.float32),
    )
    grad_k_flat = grad_k_own.reshape(token_rows, model_width)
    grad_v_flat = grad_v_own.reshape(token_rows, model_width)
    grad_q_low = grad_q.reshape(token_rows, model_width).astype(jnp.bfloat16)
    grad_v_low = grad_v_flat.astype(jnp.bfloat16)
    grad_proj = jnp.concatenate([grad_q_low, grad_k_flat.astype(jnp.bfloat16), grad_v_low], axis=1)
    d_w_qkv = contract_rows(flat_tokens, grad_proj)
    d_qv_bias = jnp.concatenate(
        [
            jnp.sum(grad_q_low.astype(jnp.float32), axis=0),
            jnp.sum(grad_v_low.astype(jnp.float32), axis=0),
        ]
    )
    d_tokens = (grad_first + contract_cols(grad_proj, w_qkv)).reshape(
        row_count, block_len, model_width
    )
    d_norm_gains = jnp.stack([gain_one, gain_two, gain_three])
    d_norm_biases = jnp.stack([shift_one, shift_two, shift_three])
    (
        d_w_qkv,
        d_qv_bias,
        d_self_out,
        d_self_out_bias,
        d_cross_query,
        d_cross_q_bias,
        d_cross_kv,
        d_cross_v_bias,
        d_cross_out,
        d_cross_out_bias,
        d_ffn_in,
        d_ffn_in_bias,
        d_ffn_out,
        d_ffn_out_bias,
        d_norm_gains,
        d_norm_biases,
    ) = lax.psum(
        (
            d_w_qkv,
            d_qv_bias,
            d_self_out,
            d_self_out_bias,
            d_cross_query,
            d_cross_q_bias,
            d_cross_kv,
            d_cross_v_bias,
            d_cross_out,
            d_cross_out_bias,
            d_ffn_in,
            d_ffn_in_bias,
            d_ffn_out,
            d_ffn_out_bias,
            d_norm_gains,
            d_norm_biases,
        ),
        ("dp", "seq"),
    )
    return (
        output,
        d_tokens,
        d_memory,
        d_w_qkv,
        d_qv_bias,
        d_self_out,
        d_self_out_bias,
        d_cross_query,
        d_cross_q_bias,
        d_cross_kv,
        d_cross_v_bias,
        d_cross_out,
        d_cross_out_bias,
        d_ffn_in,
        d_ffn_in_bias,
        d_ffn_out,
        d_ffn_out_bias,
        d_norm_gains,
        d_norm_biases,
    )


def rows_on_device(
    tokens, memory, tl, sl, cotangent, w_qkv, qv_bias, self_out, self_out_bias, cross_query, cross_q_bias,
    cross_kv, cross_v_bias, cross_out, cross_out_bias, ffn_in, ffn_in_bias, ffn_out, ffn_out_bias, gains, shifts,
):
    small = (qv_bias, self_out_bias, cross_q_bias, cross_v_bias, cross_out_bias, gains, shifts)
    saved = forward(tokens, memory, cotangent, tl, sl, small, w_qkv, self_out, cross_query, cross_kv, cross_out)
    names = ("cot", "x", "mem", "q", "qt", "k", "kt", "v", "ctx", "lse", "xh1", "rs1",
             "q2", "q2t", "k2", "k2t", "v2", "c2", "lse2", "y2", "xh2", "rs2")
    ins = dict(zip(names, saved))
    ins |= {"qkv": w_qkv, "so": self_out, "cq": cross_query, "ckv": cross_kv, "co": cross_out, "win": ffn_in, "wout": ffn_out}
    out, dtok, dmem, sums, dvec = main(tl, sl, (ffn_in_bias, ffn_out_bias, gains, shifts), ins)
    return (out,) + unpack(sums, dvec, dtok, dmem, ffn_in.shape[0], ffn_in.shape[1])


def on_device(tokens, *rest):
    if tokens.shape[0] == lax.axis_size("seq") and lax.axis_size("dp") == 8:
        return rows_on_device(tokens, *rest)
    return blocks_on_device(tokens, *rest)


def solution(mesh):
    in_specs = (
        P("dp", "seq", None),
        P("dp", "seq", None),
        P("dp", None),
        P("dp", None),
        P("dp", "seq", None),
        P(),
        P(),
        P(),
        P(),
        P(),
        P(),
        P(),
        P(),
        P(),
        P(),
        P(),
        P(),
        P(),
        P(),
        P(),
        P(),
    )
    out_specs = (
        P("dp", "seq", None),
        P("dp", "seq", None),
        P("dp", "seq", None),
        P(),
        P(),
        P(),
        P(),
        P(),
        P(),
        P(),
        P(),
        P(),
        P(),
        P(),
        P(),
        P(),
        P(),
        P(),
        P(),
    )
    return jax.shard_map(
        on_device, mesh=mesh, in_specs=in_specs, out_specs=out_specs, check_vma=False
    )
```

```python
import functools
import jax
import jax.numpy as jnp
from jax import lax
from jax.experimental import pallas as pl
from jax.experimental.pallas import tpu as pltpu
from jax.sharding import PartitionSpec as P

HEADS = 8
HEAD = 64
NDOC = 32
AUG = HEAD + 16
MASKED = -1e9
LOG2E = 1.4426950408889634
SCALE = HEAD**-0.5
F32 = jnp.float32
BF16 = jnp.bfloat16
TB = 256
FB = 512

V_Q, V_V, V_SO, V_CQ, V_CV, V_CO, V_FI, V_FO, V_G, V_B = 0, 1, 2, 3, 4, 5, 6, 10, 11, 14
VECS = 24
G_IN, G_OUT, G_CO, G_CK, G_CQ, G_SO, G_QKV = 0, 4, 8, 9, 11, 12, 13
STREAMS = ((4, 20, 4), (0, 16, 4), (8, 20, 3), (11, 23, 2), (13, 16, 2), (15, 18, 1))
UNITS, ALL_UNITS = 16, 25
PIECES = 8
STEPS = 8
COPIES = (1, 2, 2, 6, 6, 2, 2, 1)
OWN = sum(COPIES)


def vec_of(ref, start, length):
    return ref[start : start + length].astype(F32).reshape(1, length)


def mm(left, right, lc=1, rc=0):
    return lax.dot_general(
        left, right, (((lc,), (rc,)), ((), ())), preferred_element_type=F32
    )


def row_ids(lengths, row, size):
    rows, docs = lengths.shape
    at_row = lax.broadcasted_iota(jnp.int32, (rows, docs), 0) == row
    own = jnp.sum(jnp.where(at_row, lengths.astype(F32), 0.0), axis=0, keepdims=True)
    own = jnp.broadcast_to(own, (docs, docs))
    down = lax.broadcasted_iota(jnp.int32, (docs, docs), 0)
    over = lax.broadcasted_iota(jnp.int32, (docs, docs), 1)
    ends_col = jnp.sum(jnp.where(over <= down, own, 0.0), axis=1, keepdims=True)
    own_col = jnp.sum(jnp.where(over == down, own, 0.0), axis=1, keepdims=True)
    ends_row = jnp.sum(
        jnp.where(down <= over, jnp.broadcast_to(own_col, (docs, docs)), 0.0),
        axis=0,
        keepdims=True,
    )
    place_row = lax.broadcasted_iota(jnp.int32, (docs, size), 1).astype(F32)
    place_col = lax.broadcasted_iota(jnp.int32, (size, docs), 0).astype(F32)
    ids_row = jnp.sum(jnp.where(ends_col <= place_row, 1.0, 0.0), axis=0, keepdims=True)
    ids_col = jnp.sum(jnp.where(ends_row <= place_col, 1.0, 0.0), axis=1, keepdims=True)
    return ids_row, ids_col


def self_mask(mask_ref, lengths, row, size):
    ids_row, ids_col = row_ids(lengths, row, size)
    for kb in range(size // TB):
        for qb in range(kb, size // TB):
            ks, qs = slice(kb * TB, (kb + 1) * TB), slice(qb * TB, (qb + 1) * TB)
            seen = ids_col[ks] == ids_row[:, qs]
            if kb == qb:
                down = lax.broadcasted_iota(jnp.int32, (TB, TB), 0)
                over = lax.broadcasted_iota(jnp.int32, (TB, TB), 1)
                seen = seen & (down <= over)
            mask_ref[ks, qs] = jnp.where(seen, 0.0, MASKED)


def cross_mask(mask_ref, lengths, src_lengths, row, size, src):
    ids_row, _ = row_ids(lengths, row, size)
    _, src_col = row_ids(src_lengths, row, src)
    for qb in range(size // TB):
        qs = slice(qb * TB, (qb + 1) * TB)
        seen = (src_col == ids_row[:, qs]) | (ids_row[:, qs] == float(NDOC))
        mask_ref[:, qs] = jnp.where(seen, 0.0, MASKED)


def half_of(values, half):
    down = lax.broadcasted_iota(jnp.int32, values.shape, 0)
    keep = (down >= HEAD) if half else (down < HEAD)
    return jnp.where(keep, values, jnp.zeros_like(values))


def normalize(h):
    center = h - jnp.mean(h, axis=-1, keepdims=True)
    spread = jnp.mean(center * center, axis=-1, keepdims=True)
    rstd = lax.rsqrt(spread + 1e-05)
    return center * rstd, rstd


def norm_back(grad, xh, rstd, gain):
    gs = grad * gain
    m1 = jnp.mean(gs, axis=-1, keepdims=True)
    m2 = jnp.mean(gs * xh, axis=-1, keepdims=True)
    dh = (gs - m1 - xh * m2) * rstd
    return (
        dh,
        jnp.sum(grad * xh, axis=0, keepdims=True),
        jnp.sum(grad, axis=0, keepdims=True),
    )


def row_attend(k_ref, qt_ref, vt_ref, mask_ref, ctx_ref, lse_ref, size, key_end):
    for pair in range(HEADS // 2):
        lanes = slice(pair * 2 * HEAD, (pair + 1) * 2 * HEAD)
        for half in range(2):
            head = pair * 2 + half
            for qb in range(size // TB):
                ke, qs = key_end(qb), slice(qb * TB, (qb + 1) * TB)
                s = mm(k_ref[0:ke, lanes], half_of(qt_ref[lanes, qs], half))
                s = s + mask_ref[0:ke, qs]
                m = jnp.max(s, axis=0, keepdims=True)
                p = jnp.exp2(s - m).astype(BF16)
                o = mm(vt_ref[head * AUG : (head + 1) * AUG, 0:ke], p)
                total = o[HEAD : HEAD + 1]
                ctx_ref[head * HEAD : (head + 1) * HEAD, qs] = (
                    o[:HEAD] * (1.0 / total)
                ).astype(BF16)
                lse_ref[head, :, qs] = m + jnp.log2(total)


class Mover:
    def __init__(self, sems):
        self.sems, self.used, self.pending = sems, 0, {}

    def start(self, name, src, dst):
        copy = pltpu.make_async_copy(src, dst, self.sems.at[self.used])
        self.used += 1
        copy.start()
        self.pending[name] = copy

    def wait(self, *names):
        for name in names:
            self.pending.pop(name).wait()

    def finish(self):
        self.wait(*list(self.pending))


def meet(peers):
    barrier = pltpu.get_barrier_semaphore()
    for peer in peers:
        pl.semaphore_signal(barrier, inc=1, device_id=peer, device_id_type=pl.DeviceIdType.MESH)
    pl.semaphore_wait(barrier, len(peers))


def remote(src, dst, sends, recvs, index, peer):
    return pltpu.make_async_remote_copy(
        src_ref=src, dst_ref=dst, send_sem=sends.at[index], recv_sem=recvs.at[index],
        device_id=peer, device_id_type=pl.DeviceIdType.MESH,
    )


FWD_OUTS = 22


def forward_kernel(
    tok_ref, src_ref, cot_ref, tl_ref, sl_ref, bqv, bso, bcq, bcv, bco, gains, shifts,
    wqkv_h, wso_h, wcq_h, wckv_h, wco_h, *rest,
):
    outs, rest = rest[:FWD_OUTS], rest[FWD_OUTS:]
    cot_out = outs[0]
    kept, rest = rest[: FWD_OUTS - 1], rest[FWD_OUTS - 1 :]
    (wqkv_ref, wso_ref, wcq_ref, wckv_ref, wco_ref, mask, mask2, vt, v2t, y1,
     sems, sends, recvs) = rest
    (x_ref, mem_ref, q_ref, qt_ref, k_ref, kt_ref, v_ref, ctx_ref, lse_ref, xh1_ref, rs1_ref,
     q2_ref, q2t_ref, k2_ref, k2t_ref, v2_ref, c2_ref, lse2_ref, y2_ref, xh2_ref, rs2_ref) = kept
    size, width = x_ref.shape
    src = mem_ref.shape[0]
    seq = tok_ref.shape[0]
    blocks = size // TB
    row = lax.axis_index("seq")
    mover = Mover(sems)
    mover.start("wqkv", wqkv_h, wqkv_ref)
    mover.start("wckv", wckv_h, wckv_ref)
    mover.start("wso", wso_h, wso_ref)
    mover.start("wcq", wcq_h, wcq_ref)
    mover.start("wco", wco_h, wco_ref)

    def place(block, length):
        return pl.ds(pl.multiple_of(block * length, length), length)

    peers = [{"seq": lax.rem(row + d, seq)} for d in range(1, seq)]
    meet(peers)

    def exchange(source, target, length, kind):
        copies = []
        for d in range(1, seq):
            to = lax.rem(row + d, seq)
            copy = remote(source.at[to], target.at[place(row, length)], sends, recvs, kind * seq + d, {"seq": to})
            copy.start()
            copies.append(copy)
        mover.start((kind, "own"), source.at[row], target.at[place(row, length)])
        return copies

    tok_copies = exchange(tok_ref, x_ref, TB, 0)
    mem_copies = exchange(src_ref, mem_ref, src // seq, 1)

    for head in range(HEADS):
        vt[head * AUG + HEAD : (head + 1) * AUG, :] = jnp.ones((AUG - HEAD, size), BF16)
        v2t[head * AUG + HEAD : (head + 1) * AUG, :] = jnp.ones((AUG - HEAD, src), BF16)
    self_mask(mask, tl_ref[...], row, size)
    cross_mask(mask2, tl_ref[...], sl_ref[...], row, size, src)

    def put_vt(ref, values, place):
        for head in range(HEADS):
            ref[head * AUG : head * AUG + HEAD, place] = values[head * HEAD : (head + 1) * HEAD]

    mover.wait("wqkv", (0, "own"))
    for d in range(seq):
        if d:
            tok_copies[d - 1].wait_recv()
        ts = place(lax.rem(row + seq - d, seq), TB)
        xb = x_ref[ts, :]
        q = ((mm(xb, wqkv_ref[:, :width]) + vec_of(bqv, 0, width)) * (SCALE * LOG2E)).astype(BF16)
        q_ref[ts, :] = q
        qt_ref[:, ts] = q.T
        k = mm(xb, wqkv_ref[:, width : 2 * width]).astype(BF16)
        k_ref[ts, :] = k
        kt_ref[:, ts] = k.T
        v = (mm(xb, wqkv_ref[:, 2 * width :]) + vec_of(bqv, width, width)).astype(BF16)
        v_ref[ts, :] = v
        put_vt(vt, v.T, ts)
    mover.wait("wckv", (1, "own"))
    for copy in mem_copies:
        copy.wait_recv()
    cot_copies = exchange(cot_ref, cot_out, TB, 2)
    for i in (0, 1, 2, 3, 4, 5, 6):
        mover.start(i, kept[i], outs[1 + i])
    k2 = mm(mem_ref[...], wckv_ref[:, :width]).astype(BF16)
    k2_ref[...] = k2
    k2t_ref[...] = k2.T
    v2 = (mm(mem_ref[...], wckv_ref[:, width:]) + vec_of(bcv, 0, width)).astype(BF16)
    v2_ref[...] = v2
    put_vt(v2t, v2.T, slice(None))
    for i in (13, 14, 15):
        mover.start(i, kept[i], outs[1 + i])

    row_attend(k_ref, qt_ref, vt, mask, ctx_ref, lse_ref, size, lambda qb: (qb + 1) * TB)
    for i in (7, 8):
        mover.start(i, kept[i], outs[1 + i])
    mover.wait("wso", "wcq")
    for tb in range(size // FB):
        ts = slice(tb * FB, (tb + 1) * FB)
        h1 = x_ref[ts, :].astype(F32) + mm(ctx_ref[:, ts].T, wso_ref[...]) + vec_of(bso, 0, width)
        xh, rstd = normalize(h1)
        xh1_ref[ts, :] = xh.astype(BF16)
        rs1_ref[ts, :] = rstd
        yb = xh * gains[0:1, :].astype(F32) + shifts[0:1, :].astype(F32)
        y1[ts, :] = yb
        q2 = ((mm(yb.astype(BF16), wcq_ref[...]) + vec_of(bcq, 0, width)) * (SCALE * LOG2E)).astype(BF16)
        q2_ref[ts, :] = q2
        q2t_ref[:, ts] = q2.T
    for i in (9, 10, 11, 12):
        mover.start(i, kept[i], outs[1 + i])
    row_attend(k2_ref, q2t_ref, v2t, mask2, c2_ref, lse2_ref, size, lambda qb: src)
    for i in (16, 17):
        mover.start(i, kept[i], outs[1 + i])
    mover.wait("wco")
    for tb in range(size // FB):
        ts = slice(tb * FB, (tb + 1) * FB)
        h2 = y1[ts, :] + mm(c2_ref[:, ts].T, wco_ref[...]) + vec_of(bco, 0, width)
        xh, rstd = normalize(h2)
        xh2_ref[ts, :] = xh.astype(BF16)
        rs2_ref[ts, :] = rstd
        y2_ref[ts, :] = xh * gains[1:2, :].astype(F32) + shifts[1:2, :].astype(F32)
        for i in (18, 19, 20):
            mover.start((i, tb), kept[i].at[ts], outs[1 + i].at[ts])
    for copy in cot_copies:
        copy.wait_recv()
    for copy in tok_copies + mem_copies + cot_copies:
        copy.wait_send()
    mover.finish()


def row_attend_back(
    k_ref, kt_ref, v_ref, q_ref, qt_ref, dc_ref, dct_ref, ctx_ref, lse_ref, mask_ref,
    delta, dqt, dq_ref, dk_ref, dv_ref, size, keys, query_start, after,
):
    for pair in range(HEADS // 2):
        lanes = slice(pair * 2 * HEAD, (pair + 1) * 2 * HEAD)
        both = dct_ref[lanes, :].astype(F32) * ctx_ref[lanes, :].astype(F32)
        for half in range(2):
            delta[half] = jnp.sum(both[half * HEAD : (half + 1) * HEAD], axis=0, keepdims=True)
        dqt[...] = jnp.zeros_like(dqt)
        for kb in range(keys // TB):
            ks, qs = slice(kb * TB, (kb + 1) * TB), slice(query_start(kb), size)
            dks, dvs = [], []
            for half in range(2):
                head = pair * 2 + half
                rows = slice(head * HEAD, (head + 1) * HEAD)
                s = mm(k_ref[ks, lanes], half_of(qt_ref[lanes, qs], half))
                p = jnp.exp2(s + mask_ref[ks, qs] - lse_ref[head, :, qs])
                dp = mm(v_ref[ks, lanes], half_of(dct_ref[lanes, qs], half))
                ds = (p * (dp - delta[half, :, qs])).astype(BF16)
                dvs.append(mm(p.astype(BF16), dc_ref[qs, lanes]))
                dks.append(mm(ds, q_ref[qs, lanes]))
                dqt[half * HEAD : (half + 1) * HEAD, qs] += mm(kt_ref[rows, ks], ds)
            first = lax.broadcasted_iota(jnp.int32, (TB, 2 * HEAD), 1) < HEAD
            dv_ref[ks, lanes] = jnp.where(first, dvs[0], dvs[1]).astype(BF16)
            dk_ref[ks, lanes] = (jnp.where(first, dks[0], dks[1]) * (1.0 / LOG2E)).astype(BF16)
            after(pair, kb)
        dq_ref[:, lanes] = (dqt[...] * SCALE).astype(BF16).T


class Stream:
    def __init__(self, grads, sums, base, give, rows, slots, sems):
        dp, self.seq = lax.axis_index("dp"), lax.axis_size("seq")
        self.z = lax.axis_index("seq")
        self.core, x, y = lax.rem(dp, 2), lax.rem(dp // 2, 2), dp // 4
        self.near = {"dp": dp + 1 - 2 * self.core}
        by_x, by_y = {"dp": dp + 2 - 4 * x}, {"dp": dp + 4 - 8 * y}
        self.grads, self.sums, self.base, self.give, self.rows = grads, sums, base, give, rows
        self.slots, self.sems = slots, sems
        half, quarter, eighth = rows // 2, rows // 4, rows // 8
        self.unit = rows // (8 * self.seq)
        self.plan = []
        for part, (one, two, b1, b2) in enumerate(((x, y, by_x, by_y), (y, x, by_y, by_x))):
            start = part * half
            keep1, give1 = start + one * quarter, start + (1 - one) * quarter
            keep2, give2 = keep1 + two * eighth, keep1 + (1 - two) * eighth
            self.plan.append((b1, keep1, give1, b2, keep2, give2))

    def at(self, start, length):
        return pl.ds(pl.multiple_of(self.base + start, 16), length)

    def view(self, start, length):
        return self.grads.at[self.at(start, length)]

    def summed(self, start, length):
        return self.sums.at[self.core, self.at(start, length)]

    def own_copies(self):
        moves = [keep2 + self.z * self.unit for _, _, _, _, keep2, _ in self.plan]
        return [
            pltpu.make_async_copy(self.view(at, self.unit), self.summed(at, self.unit), self.sems[0].at[OWN + i])
            for i, at in enumerate(moves)
        ]

    def copies(self, step):
        rows, (s0, s1, s2, s3), seq = self.rows, self.slots, self.seq
        first = sum(COPIES[:step])
        sends, recvs = self.sems
        moves = []
        if step == 0:
            moves.append((self.grads.at[self.give : self.give + rows], s0, self.near))
        if step == 7:
            moves.append((self.summed(0, rows), self.summed(0, rows), self.near))
        for part, (b1, keep1, give1, b2, keep2, give2) in enumerate(self.plan):
            if step == 1:
                moves.append((self.view(give1, rows // 4), s1.at[part], b1))
            if step == 2:
                moves.append((self.view(give2, rows // 8), s2.at[part], b2))
            if step == 5:
                moves.append((self.summed(keep2, rows // 8), self.summed(keep2, rows // 8), b2))
            if step == 6:
                moves.append((self.summed(keep1, rows // 4), self.summed(keep1, rows // 4), b1))
            for d in range(1, seq):
                to = lax.rem(self.z + d, seq)
                if step == 3:
                    moves.append((self.view(keep2 + to * self.unit, self.unit), s3.at[part, d - 1], {"seq": to}))
                if step == 4:
                    own = keep2 + self.z * self.unit
                    moves.append((self.view(own, self.unit), self.summed(own, self.unit), {"seq": to}))
        return [remote(*move[:2], sends, recvs, first + i, move[2]) for i, move in enumerate(moves)]

    def add(self, start, slots, length):
        chunk = min(length, self.rows // 8)

        def at(i):
            place = pl.ds(pl.multiple_of(self.base + start + i * chunk, 16), chunk)
            total = self.grads[place, :].astype(F32)
            for slot in slots:
                total = total + slot[pl.ds(pl.multiple_of(i * chunk, 16), chunk), :].astype(F32)
            self.grads[place, :] = total.astype(BF16)

        if length == chunk:
            at(0)
        else:
            pl.loop(0, length // chunk)(at)

    def tick(self, step):
        if step:
            for copy in self.copies(step - 1):
                copy.wait()
        if step == 5:
            for copy in self.own_copies():
                copy.wait()
        s0, s1, s2, s3 = self.slots
        if step == 1:
            self.add(0, [s0], self.rows)
        for part, (_, keep1, _, _, keep2, _) in enumerate(self.plan):
            if step == 2:
                self.add(keep1, [s1.at[part]], self.rows // 4)
            if step == 3:
                self.add(keep2, [s2.at[part]], self.rows // 8)
            if step == 4:
                self.add(keep2 + self.z * self.unit, [s3.at[part, d] for d in range(self.seq - 1)], self.unit)
        if step < STEPS:
            for copy in self.copies(step):
                copy.start()
        if step == 4 and step < STEPS:
            for copy in self.own_copies():
                copy.start()


class VectorSum:
    def __init__(self, held, sems):
        dp, self.seq, self.z = lax.axis_index("dp"), lax.axis_size("seq"), lax.axis_index("seq")
        core, x, y = lax.rem(dp, 2), lax.rem(dp // 2, 2), dp // 4
        self.partners = [{"dp": dp + 1 - 2 * core}, {"dp": dp + 2 - 4 * x}, {"dp": dp + 4 - 8 * y}]
        self.held, self.sems = held, sems

    def copies(self, step):
        sends, recvs = self.sems
        if step < 3:
            return [remote(self.held.at[2 * step], self.held.at[2 * step + 1], sends, recvs, step, self.partners[step])]
        own = self.held.at[6 + self.z]
        return [remote(own, own, sends, recvs, 2 + d, {"seq": lax.rem(self.z + d, self.seq)}) for d in range(1, self.seq)]

    def tick(self, step):
        if step:
            for copy in self.copies(step - 1):
                copy.wait()
            if step < 4:
                to = 2 * step if step < 3 else 6 + self.z
                self.held[to] = self.held[2 * step - 2] + self.held[2 * step - 1]
        if step < 4:
            for copy in self.copies(step):
                copy.start()

    def total(self):
        values = self.held[6]
        for i in range(1, self.seq):
            values = values + self.held[6 + i]
        return values


INS = ("y2", "win", "cot", "wout", "xh2", "rs2", "co", "c2", "k2", "q2t", "v2", "k2t", "lse2", "mem", "ckv",
       "rs1", "kt", "k", "v", "q", "x", "q2", "xh1", "cq", "so", "qkv", "qt", "ctx", "lse")
HELD = INS[:17]
POOL = 14


def main_kernel(plan, tl_ref, sl_ref, bfi, bfo, gains, shifts, *rest):
    n = len(INS)
    hbm, rest = dict(zip(INS, rest[:n])), rest[n:]
    (out_h, dtok_h, dmem_h, sums_h, dvec_ref), rest = rest[:5], rest[5:]
    vmem, rest = dict(zip(HELD, rest[: len(HELD)])), rest[len(HELD) :]
    pool, rest = rest[:POOL], rest[POOL:]
    (out_row, dh1, mask, mask2, delta, dqt, dct, dk2, dv2, dmem, grads, held), rest = rest[:12], rest[12:]
    slots, rest = [rest[4 * i : 4 * i + 4] for i in range(len(STREAMS))], rest[4 * len(STREAMS) :]
    sems, sends, recvs, xsends, xrecvs = rest
    size, width = vmem["y2"].shape
    inner = vmem["win"].shape[1]
    src = vmem["mem"].shape[0]
    acts, dus, slopes, (y2b, dz_s) = pool[0:4], pool[4:8], pool[8:12], pool[12:14]
    vmem |= dict(zip(("k", "v", "q", "x"), pool[0:4]))
    dq, dk, dv, dc = pool[4:8]
    vmem |= {"q2": pool[8], "xh1": pool[9], "qt": vmem["q2t"], "ctx": vmem["c2"], "lse": vmem["lse2"]}
    wout = vmem["wout"]
    vmem |= {"cq": wout.at[0:width], "so": wout.at[width : 2 * width], "qkv": vmem["win"].at[:, : 3 * width]}
    y1b, dtok = y2b, dz_s
    cols = [slice(j, j + width) for j in range(0, inner, width)]
    blocks = [slice(t, t + TB) for t in range(0, size, TB)]
    seq, row, dp = lax.axis_size("seq"), lax.axis_index("seq"), lax.axis_index("dp")
    mover = Mover(sems)

    def load(*names):
        for name in names:
            mover.start(name, hbm[name], vmem[name])

    load(*HELD)
    split = [(keep * width, give * width, rows * width) for keep, give, rows in STREAMS]
    streams = [
        Stream(grads, sums_h, *where, slots[i], (sends.at[i], recvs.at[i])) for i, where in enumerate(split)
    ]
    vectors = VectorSum(held, (sends.at[len(STREAMS)], recvs.at[len(STREAMS)]))
    core, x, y = streams[0].core, lax.rem(dp // 2, 2), dp // 4
    pieces = []

    def piece_sender(source, target, kind):
        def send_piece(step):
            length = size // seq
            part = length // PIECES
            copies = []
            for d in range(1, seq):
                to = lax.rem(row + d, seq)
                rows = pl.ds(pl.multiple_of(to * length + step * part, 16), part)
                place = target.at[row, step * part : (step + 1) * part]
                copies.append(remote(source.at[rows], place, xsends, xrecvs, (kind + step) * seq + d, {"seq": to}))
            for copy in copies:
                copy.start()
            pieces.extend(copies)

        return send_piece

    ticks = [s.tick for s in streams] + [vectors.tick, piece_sender(dtok, dtok_h, 1), piece_sender(out_row, out_h, 1 + PIECES)]

    def act(place):
        for stream, step in plan.get(place, ()):
            ticks[stream](step)

    meet(
        [{"dp": dp + 1 - 2 * core}, {"dp": dp + 2 - 4 * x}, {"dp": dp + 4 - 8 * y}]
        + [{"seq": lax.rem(row + d, seq)} for d in range(1, seq)]
    )

    def exchange(source, target, kind):
        length = source.shape[0] // seq
        copies = []
        for d in range(1, seq):
            to = lax.rem(row + d, seq)
            rows = pl.ds(pl.multiple_of(to * length, 16), length)
            copies.append(remote(source.at[rows], target.at[row], xsends, xrecvs, kind * seq + d, {"seq": to}))
        for copy in copies:
            copy.start()
        mover.start((kind, "own"), source.at[pl.ds(pl.multiple_of(row * length, 16), length)], target.at[row])
        return copies

    gives = {keep + i: give + i for keep, give, rows in STREAMS for i in range(rows)}

    def gather(i, values):
        half = width // 2
        keep, give = i * width, gives[i] * width
        left = pl.multiple_of(jnp.where(core == 0, keep, give), width)
        right = pl.multiple_of(jnp.where(core == 0, give, keep), width)
        grads[pl.ds(left, width), :] = values[:, :half].astype(BF16)
        grads[pl.ds(right, width), :] = values[:, half:].astype(BF16)

    def total(values):
        return jnp.sum(values.astype(F32), axis=0, keepdims=True)

    def count(i, values):
        dvec_ref[i : i + 1, :] += values

    gain0, shift0 = gains[0:1, :].astype(F32), shifts[0:1, :].astype(F32)
    gain1, gain2, shift2 = gains[1:2, :].astype(F32), gains[2:3, :].astype(F32), shifts[2:3, :].astype(F32)
    dvec_ref[...] = jnp.zeros_like(dvec_ref)
    mover.wait("y2", "win", "cot", "wout")
    y2_ref, win = vmem["y2"], vmem["win"]

    for tb in range(size // FB):
        ts = slice(tb * FB, (tb + 1) * FB)
        y2 = y2_ref[ts, :]
        low = y2.astype(BF16)
        y2b[ts, :] = low
        h3 = y2 + vec_of(bfo, 0, width)
        for j, cs in enumerate(cols):
            u = mm(low, win[:, cs]) + vec_of(bfi, j * width, width)
            sg = 0.5 * jnp.tanh(0.5 * u) + 0.5
            a = u * sg
            slopes[j][ts, :] = (sg + a * (1.0 - sg)).astype(BF16)
            a = a.astype(BF16)
            acts[j][ts, :] = a
            h3 = h3 + mm(a, wout[cs, :])
        xh, rstd = normalize(h3)
        out_row[ts, :] = (xh * gain2 + shift2).astype(BF16)
        dh3, dg, db = norm_back(vmem["cot"][ts, :].astype(F32), xh, rstd, gain2)
        y2_ref[ts, :] = dh3
        dz = dh3.astype(BF16)
        dz_s[ts, :] = dz
        count(V_G + 2, dg)
        count(V_B + 2, db)
        count(V_FO, total(dz))

    own = pl.ds(pl.multiple_of(row * (size // seq), 16), size // seq)
    mover.start("own output", out_row.at[own], out_h.at[row])
    for j in range(len(cols)):
        gather(G_OUT + j, mm(acts[j][...], dz_s[...], 0, 0))
        act(("out", j))
    act("ffn_out")
    load("k", "v", "q", "x")
    mover.wait("xh2", "rs2")
    for tb, ts in enumerate([slice(t, t + FB) for t in range(0, size, FB)]):
        dz = dz_s[ts, :]
        dy2 = y2_ref[ts, :]
        for j, cs in enumerate(cols):
            du = (mm(dz, wout[cs, :], 1, 1) * slopes[j][ts, :].astype(F32)).astype(BF16)
            dus[j][ts, :] = du
            count(V_FI + j, total(du))
            dy2 = dy2 + mm(du, win[:, cs], 1, 1)
            if j < 3:
                act(("ffn", tb, j))
        dh2, dg, db = norm_back(dy2, vmem["xh2"][ts, :].astype(F32), vmem["rs2"][ts, :], gain1)
        y2_ref[ts, :] = dh2
        count(V_G + 1, dg)
        count(V_B + 1, db)
        act(("ffn", tb, 3))

    load("q2", "xh1", "cq", "so", "qkv")
    dh2_ref = y2_ref
    for j in range(len(cols)):
        gather(G_IN + j, mm(y2b[...], dus[j][...], 0, 0))
        act(("in", j))
    act("ffn_in")
    cross_mask(mask2, tl_ref[...], sl_ref[...], row, size, src)
    act("mask2")
    mover.wait("co", "c2")
    for tb, ts in enumerate(blocks):
        da2 = dh2_ref[ts, :].astype(BF16)
        dc[ts, :] = mm(da2, vmem["co"][...], 1, 1).astype(BF16)
        dct[:, ts] = mm(vmem["co"][...], da2, 1, 1).astype(BF16)
        count(V_CO, total(da2))
        act(("cin", tb))
    act("cross_in")
    gather(G_CO, mm(vmem["c2"][...], dh2_ref[...].astype(BF16)))
    act("cross_out")
    mover.wait("k2", "q2t", "v2", "k2t", "lse2", "q2")
    row_attend_back(
        vmem["k2"], vmem["k2t"], vmem["v2"], vmem["q2"], vmem["q2t"], dc, dct, vmem["c2"], vmem["lse2"], mask2,
        delta, dqt, dq, dk2, dv2, size, src, lambda kb: 0, lambda i, j: act(("cross", i, j)),
    )
    load("qt", "ctx", "lse")
    count(V_CV, total(dv2[...]))
    count(V_CQ, total(dq[...]))
    mover.wait("mem", "ckv", "cq", "xh1", "rs1", "so")
    gather(G_CK, mm(vmem["mem"][...], dk2[...], 0, 0))
    gather(G_CK + 1, mm(vmem["mem"][...], dv2[...], 0, 0))
    act("ck")
    w_ckv = vmem["ckv"]
    dmem[...] = (mm(dk2[...], w_ckv[:, :width], 1, 1) + mm(dv2[...], w_ckv[:, width:], 1, 1)).astype(BF16)
    act("memory")
    mem_copies = exchange(dmem, dmem_h, 0)
    for tb, ts in enumerate(blocks):
        dy1 = dh2_ref[ts, :] + mm(dq[ts, :], vmem["cq"][...], 1, 1)
        xh1 = vmem["xh1"][ts, :].astype(F32)
        y1b[ts, :] = (xh1 * gain0 + shift0).astype(BF16)
        dh, dg, db = norm_back(dy1, xh1, vmem["rs1"][ts, :], gain0)
        count(V_G, dg)
        count(V_B, db)
        dh1[ts, :] = dh
        count(V_SO, total(dh.astype(BF16)))
        act(("nrm", tb))
    act("norm")
    gather(G_CQ, mm(y1b[...], dq[...], 0, 0))
    act("query")
    self_mask(mask, tl_ref[...], row, size)
    act("mask")
    mover.wait("ctx")
    gather(G_SO, mm(vmem["ctx"][...], dh1[...].astype(BF16)))
    act("self_out")
    for tb, ts in enumerate(blocks):
        da1 = dh1[ts, :].astype(BF16)
        dc[ts, :] = mm(da1, vmem["so"][...], 1, 1).astype(BF16)
        dct[:, ts] = mm(vmem["so"][...], da1, 1, 1).astype(BF16)
        act(("sin", tb))
    act("self_in")
    mover.wait("k", "qt", "v", "q", "kt", "lse")
    row_attend_back(
        vmem["k"], vmem["kt"], vmem["v"], vmem["q"], vmem["qt"], dc, dct, vmem["ctx"], vmem["lse"], mask,
        delta, dqt, dq, dk, dv, size, size, lambda kb: kb * TB, lambda i, j: act(("self", i, j)),
    )
    mover.wait("x", "qkv")
    for i, part in enumerate((dq, dk, dv)):
        gather(G_QKV + i, mm(vmem["x"][...], part[...], 0, 0))
        act(("qkv", i))
    act("qkv")
    count(V_Q, total(dq[...]))
    count(V_V, total(dv[...]))
    held[0] = dvec_ref[...]
    act("vectors")
    w_qkv = vmem["qkv"]
    for tb, ts in enumerate(blocks):
        dtok[ts, :] = (
            dh1[ts, :]
            + mm(dq[ts, :], w_qkv[:, :width], 1, 1)
            + mm(dk[ts, :], w_qkv[:, width : 2 * width], 1, 1)
            + mm(dv[ts, :], w_qkv[:, 2 * width :], 1, 1)
        ).astype(BF16)
        act(("tok", tb))
    mover.start("own tokens", dtok.at[own], dtok_h.at[row])
    act("tokens")
    act("end")
    dvec_ref[...] = vectors.total()
    for copy in pieces + mem_copies:
        copy.wait()
    mover.finish()


PLAN = {
    ("out", 0): [(8, 0)],
    "ffn_out": [(0, 0), (8, 1)],
    ("ffn", 0, 2): [(0, 1), (8, 2)],
    ("ffn", 1, 0): [(8, 3)],
    ("ffn", 1, 2): [(8, 4)],
    ("in", 2): [(8, 5)],
    "ffn_in": [(1, 0), (0, 2)],
    ("cin", 0): [(8, 6)],
    "cross_in": [(1, 1)],
    ("cross", 0, 0): [(8, 7)],
    ("cross", 1, 0): [(0, 3)],
    "ck": [(2, 0)],
    ("nrm", 0): [(1, 2)],
    "norm": [(2, 1)],
    "self_out": [(3, 0), (0, 4)],
    ("sin", 1): [(1, 3)],
    "self_in": [(3, 1)],
    ("self", 0, 2): [(2, 2)],
    ("self", 1, 2): [(0, 5)],
    ("self", 2, 0): [(2, 3)],
    ("self", 3, 0): [(1, 4), (0, 6)],
    ("self", 3, 2): [(3, 2)],
    ("qkv", 1): [(4, 0), (2, 4)],
    "qkv": [(5, 0)],
    ("tok", 1): [(4, 1)],
    "tokens": [(5, 1), (6, 1)],
    "end": [(0, 7), (7, 0), (3, 3), (0, 8), (4, 2), (2, 5), (5, 2), (6, 2), (7, 1), (4, 3), (1, 5), (5, 3), (7, 2), (2, 6), (3, 4), (6, 3), (1, 6), (4, 4), (5, 4), (2, 7), (2, 8), (7, 3), (3, 5), (6, 4), (1, 7), (7, 4), (4, 5), (5, 5), (3, 6), (7, 5), (5, 6), (7, 6), (4, 6), (3, 7), (7, 7), (5, 7), (3, 8), (1, 8), (4, 7), (5, 8), (4, 8)],
    "vectors": [(6, 0)],
}


def unpack_kernel(grads_h, dvec_ref, dtok_h, dmem_h, *rest):
    outs, rest = rest[:18], rest[18:]
    mats, vecs = outs[:9], outs[9:]
    grads, dtok, dmem, rest = rest[0], rest[1], rest[2], rest[3:]
    wide, sems = rest[:9], rest[9]
    mover = Mover(sems)
    width = 2 * grads.shape[2]
    half = width // 2
    plan = ((0, G_QKV, 1, 3), (1, G_SO, 1, 1), (2, G_CQ, 1, 1), (3, G_CK, 1, 2), (4, G_CO, 1, 1), (5, G_IN, 1, 4), (6, G_OUT, 4, 1))
    for i, base, units, blocks in plan:
        rows = slice(base * width, (base + units * blocks) * width)
        mover.start(i, grads_h.at[:, rows], grads.at[:, rows])
    mover.start("tok", dtok_h, dtok)
    mover.start("mem", dmem_h, dmem)
    for i, base, units, blocks in plan:
        mover.wait(i)
        for b in range(blocks):
            for u in range(units):
                rows = slice((base + b + u) * width, (base + b + u + 1) * width)
                for c in range(2):
                    wide[i][u * width : (u + 1) * width, b * width + c * half : b * width + (c + 1) * half] = grads[c, rows, :].astype(F32)
        mover.start((i, "out"), wide[i], mats[i])
    for i, name, source in ((7, "tok", dtok), (8, "mem", dmem)):
        mover.wait(name)
        wide[i][...] = source[...].astype(F32)
        mover.start((i, "out"), wide[i], mats[i])
    place = 0
    for ref in vecs:
        if len(ref.shape) == 2:
            ref[...] = dvec_ref[place : place + ref.shape[0], :]
            place += ref.shape[0]
        else:
            for j in range(ref.shape[0] // width):
                ref[j * width : (j + 1) * width] = dvec_ref[place, :]
                place += 1
    mover.finish()


WHOLE = pl.BlockSpec(memory_space=pltpu.VMEM)


def call(kernel, ins, outs, scratch, name):
    return pl.pallas_call(
        kernel,
        out_shape=[jax.ShapeDtypeStruct(*o) for o in outs],
        in_specs=[WHOLE] * len(ins),
        out_specs=[WHOLE] * len(outs),
        scratch_shapes=[pltpu.VMEM(*s) for s in scratch],
        compiler_params=pltpu.CompilerParams(vmem_limit_bytes=60 * 2**20),
        name=name,
    )(*ins)


ANY = pl.BlockSpec(memory_space=pl.ANY)


def forward(tokens, memory, cot, tl, sl, small, wqkv, wso, wcq, wckv, wco):
    seq, block, d = tokens.shape
    t, s = seq * block, seq * memory.shape[1]
    tok, feat, row = ((t, d), BF16), ((d, t), BF16), ((HEADS, 1, t), F32)
    col, mem = ((t, 1), F32), ((s, d), BF16)
    kept = [tok, mem, tok, feat, tok, feat, tok, feat, row, tok, col,
            tok, feat, mem, ((d, s), BF16), mem, feat, row, ((t, d), F32), tok, col]
    weights = (wqkv, wso, wcq, wckv, wco)
    scratch = kept + [(w.shape, w.dtype) for w in weights]
    scratch += [((t, t), F32), ((s, t), F32), ((HEADS * AUG, t), BF16), ((HEADS * AUG, s), BF16), ((t, d), F32)]
    return pl.pallas_call(
        forward_kernel,
        out_shape=[jax.ShapeDtypeStruct(*o) for o in [tok] + kept],
        in_specs=[ANY] * 3 + [WHOLE] * (2 + len(small)) + [ANY] * 5,
        out_specs=[ANY] * FWD_OUTS,
        scratch_shapes=[pltpu.VMEM(*x) for x in scratch]
        + [pltpu.SemaphoreType.DMA((40,)), pltpu.SemaphoreType.DMA((3 * seq,)), pltpu.SemaphoreType.DMA((3 * seq,))],
        compiler_params=pltpu.CompilerParams(vmem_limit_bytes=60 * 2**20, collective_id=0, has_side_effects=True),
        name="forward",
    )(tokens, memory, cot, tl, sl, *small, *weights)


def main(tl, sl, small, ins):
    t, d = ins["y2"].shape
    s = ins["mem"].shape[0]
    seq = lax.axis_size("seq")
    tok, mem, wide = ((t, d), BF16), ((s, d), BF16), ((t, d), F32)
    scratch = [(ins[name].shape, ins[name].dtype) for name in HELD] + [tok] * POOL
    scratch += [tok, wide, ((t, t), F32), ((s, t), F32), ((2, 1, t), F32), ((2 * HEAD, t), F32), ((d, t), BF16),
                mem, mem, mem, ((ALL_UNITS * d, d // 2), BF16), ((6 + seq, VECS, d), F32)]
    for _, _, rows in STREAMS:
        r, c = rows * d, d // 2
        scratch += [((r, c), BF16), ((2, r // 4, c), BF16), ((2, r // 8, c), BF16), ((2, seq - 1, r // (8 * seq), c), BF16)]
    steps = pltpu.SemaphoreType.DMA((len(STREAMS) + 1, OWN + 2))
    return pl.pallas_call(
        functools.partial(main_kernel, PLAN),
        out_shape=[
            jax.ShapeDtypeStruct((seq, t // seq, d), BF16),
            jax.ShapeDtypeStruct((seq, t // seq, d), BF16),
            jax.ShapeDtypeStruct((seq, s // seq, d), BF16),
            jax.ShapeDtypeStruct((2, UNITS * d, d // 2), BF16),
            jax.ShapeDtypeStruct((VECS, d), F32),
        ],
        in_specs=[WHOLE] * 6 + [ANY] * len(INS),
        out_specs=[ANY] * 4 + [WHOLE],
        scratch_shapes=[pltpu.VMEM(*x) for x in scratch]
        + [pltpu.SemaphoreType.DMA((40,)), steps, steps] + [pltpu.SemaphoreType.DMA(((1 + 2 * PIECES) * seq,))] * 2,
        compiler_params=pltpu.CompilerParams(vmem_limit_bytes=62 * 2**20, collective_id=1, has_side_effects=True),
        name="main",
    )(tl, sl, *small, *[ins[name] for name in INS])


def unpack(grads, dvec, dtok, dmem, d, f):
    mats = [(d, 3 * d), (d, d), (d, d), (d, 2 * d), (d, d), (d, f), (f, d), dtok.shape, dmem.shape]
    vecs = [(2 * d,), (d,), (d,), (d,), (d,), (f,), (d,), (3, d), (3, d)]
    outs = pl.pallas_call(
        unpack_kernel,
        out_shape=[jax.ShapeDtypeStruct(o, F32) for o in mats + vecs],
        in_specs=[ANY, WHOLE, ANY, ANY],
        out_specs=[ANY] * 9 + [WHOLE] * 9,
        scratch_shapes=[pltpu.VMEM(x.shape, x.dtype) for x in (grads, dtok, dmem)]
        + [pltpu.VMEM(m, F32) for m in mats] + [pltpu.SemaphoreType.DMA((24,))],
        compiler_params=pltpu.CompilerParams(vmem_limit_bytes=60 * 2**20),
        name="unpack",
    )(grads, dvec, dtok, dmem)
    d_qkv, d_so, d_cq, d_ckv, d_co, d_fi, d_fo, d_tok, d_mem = outs[:9]
    v_qv, v_so, v_cq, v_cv, v_co, v_fi, v_fo, d_gains, d_shifts = outs[9:]
    return (d_tok, d_mem, d_qkv, v_qv, d_so, v_so, d_cq, v_cq, d_ckv, v_cv, d_co, v_co, d_fi, v_fi, d_fo, v_fo, d_gains, d_shifts)


def layer_norm(values, gain, shift):
    center = values - jnp.mean(values, axis=-1, keepdims=True)
    spread = jnp.mean(center * center, axis=-1, keepdims=True)
    return center * lax.rsqrt(spread + 1e-05) * gain + shift


def doc_ids(lengths, size):
    ends = jnp.cumsum(lengths, axis=1)
    places = jnp.arange(size, dtype=jnp.int32)
    return jnp.sum((ends[:, None, :] <= places[None, :, None]).astype(jnp.int32), axis=2)


def block_width(key_total):
    return 512 if key_total % 512 == 0 else key_total


def contract_rows(left, right):
    return lax.dot_general(
        left, right, (((0,), (0,)), ((), ())), preferred_element_type=jnp.float32
    )


def contract_cols(left, right):
    return lax.dot_general(
        left, right, (((1,), (1,)), ((), ())), preferred_element_type=jnp.float32
    )


def block_scores(queries, keys, allowed, start_at, width_of, score_scale):
    key_block = lax.dynamic_slice_in_dim(keys, start_at, width_of, 1)
    scores = (
        jnp.einsum("rqhd,rkhd->rhqk", queries, key_block, preferred_element_type=jnp.float32)
        * score_scale
    )
    return jnp.where(allowed(start_at, width_of)[:, None], scores, -1000000000.0)


def attend_forward(queries, keys, values, allowed, skip_after, score_scale):
    row_count, query_count, head_count, head_size = queries.shape
    key_total = keys.shape[1]
    width_of = block_width(key_total)
    block_count = key_total // width_of

    def statistics(carried, block_index):
        start_at = block_index * width_of

        def statistics_work(state):
            running_max, running_sum = state
            scores = block_scores(queries, keys, allowed, start_at, width_of, score_scale)
            new_max = jnp.maximum(running_max, jnp.max(scores, axis=3))
            new_sum = running_sum * jnp.exp(running_max - new_max) + jnp.sum(
                jnp.exp(scores - new_max[..., None]), axis=3
            )
            return (new_max, new_sum)

        return (
            lax.cond(start_at > skip_after, lambda state: state, statistics_work, carried),
            None,
        )

    stat_shape = (row_count, head_count, query_count)
    start_state = (
        jnp.full(stat_shape, -1000000000.0, jnp.float32),
        jnp.zeros(stat_shape, jnp.float32),
    )
    block_numbers = jnp.arange(block_count, dtype=jnp.int32)
    (running_max, running_sum), _ = lax.scan(statistics, start_state, block_numbers)
    log_total = running_max + jnp.log(running_sum)

    def mixing(carried, block_index):
        start_at = block_index * width_of

        def mixing_work(accum):
            scores = block_scores(queries, keys, allowed, start_at, width_of, score_scale)
            probs = jnp.exp(scores - log_total[..., None]).astype(jnp.bfloat16)
            value_block = lax.dynamic_slice_in_dim(values, start_at, width_of, 1)
            return accum + jnp.einsum(
                "rhqk,rkhd->rqhd", probs, value_block, preferred_element_type=jnp.float32
            )

        return (lax.cond(start_at > skip_after, lambda accum: accum, mixing_work, carried), None)

    start_accum = jnp.zeros((row_count, query_count, head_count, head_size), jnp.float32)
    accum, _ = lax.scan(mixing, start_accum, block_numbers)
    return (accum, log_total)


def attend_back(
    queries, keys, values, allowed, skip_after, score_scale, log_total, grad_out, delta
):
    row_count, query_count, head_count, head_size = queries.shape
    key_total = keys.shape[1]
    width_of = block_width(key_total)
    block_count = key_total // width_of

    def step(block_index, state):
        start_at = block_index * width_of

        def step_work(inner):
            scores = block_scores(queries, keys, allowed, start_at, width_of, score_scale)
            probs = jnp.exp(scores - log_total[..., None])
            key_block = lax.dynamic_slice_in_dim(keys, start_at, width_of, 1)
            value_block = lax.dynamic_slice_in_dim(values, start_at, width_of, 1)
            grad_probs = jnp.einsum(
                "rqhd,rkhd->rhqk", grad_out, value_block, preferred_element_type=jnp.float32
            )
            grad_scores = (probs * (grad_probs - delta[..., None])).astype(jnp.bfloat16)
            grad_query = (
                inner[0]
                + jnp.einsum(
                    "rhqk,rkhd->rqhd", grad_scores, key_block, preferred_element_type=jnp.float32
                )
                * score_scale
            )
            key_part = (
                jnp.einsum(
                    "rhqk,rqhd->rkhd", grad_scores, queries, preferred_element_type=jnp.float32
                )
                * score_scale
            )
            value_part = jnp.einsum(
                "rhqk,rqhd->rkhd",
                probs.astype(jnp.bfloat16),
                grad_out,
                preferred_element_type=jnp.float32,
            )
            grad_keys = lax.dynamic_update_slice_in_dim(inner[1], key_part, start_at, 1)
            grad_values = lax.dynamic_update_slice_in_dim(inner[2], value_part, start_at, 1)
            return (grad_query, grad_keys, grad_values)

        return lax.cond(start_at > skip_after, lambda inner: inner, step_work, state)

    start_state = (jnp.zeros((row_count, query_count, head_count, head_size), jnp.float32),)
    start_state = start_state + (
        jnp.zeros((row_count, key_total, head_count, head_size), jnp.float32),
        jnp.zeros((row_count, key_total, head_count, head_size), jnp.float32),
    )
    return lax.fori_loop(0, block_count, step, start_state)


def blocks_on_device(
    tokens,
    memory,
    doc_lengths,
    src_lengths,
    cotangent,
    w_qkv,
    qv_bias,
    self_out,
    self_out_bias,
    cross_query,
    cross_q_bias,
    cross_kv,
    cross_v_bias,
    cross_out,
    cross_out_bias,
    ffn_in,
    ffn_in_bias,
    ffn_out,
    ffn_out_bias,
    norm_gains,
    norm_biases,
):
    row_count, block_len, model_width = tokens.shape
    src_block = memory.shape[1]
    seq_count = lax.axis_size("seq")
    row_length = block_len * seq_count
    src_length = src_block * seq_count
    score_scale = HEAD ** (-0.5)
    first_place = lax.axis_index("seq") * block_len
    last_place = first_place + block_len - 1
    target_ids = doc_ids(doc_lengths, row_length)
    source_ids = doc_ids(src_lengths, src_length)
    own_ids = lax.dynamic_slice_in_dim(target_ids, first_place, block_len, 1)
    own_places = first_place + jnp.arange(block_len, dtype=jnp.int32)

    def self_allowed(start_at, width_of):
        key_ids = lax.dynamic_slice_in_dim(target_ids, start_at, width_of, 1)
        key_places = start_at + jnp.arange(width_of, dtype=jnp.int32)
        return (own_ids[:, :, None] == key_ids[:, None, :]) & (
            key_places[None, None, :] <= own_places[None, :, None]
        )

    def cross_allowed(start_at, width_of):
        return (own_ids[:, :, None] == source_ids[:, None, :]) | (own_ids[:, :, None] == NDOC)

    def split_heads(array_in):
        return array_in.reshape(array_in.shape[0], array_in.shape[1], HEADS, HEAD)

    token_rows = row_count * block_len
    flat_tokens = tokens.reshape(token_rows, model_width)
    flat_memory = memory.reshape(row_count * src_block, model_width)
    pair_bias = qv_bias.astype(jnp.float32)
    gains = norm_gains.astype(jnp.float32)
    shifts = norm_biases.astype(jnp.float32)
    packed = jnp.dot(flat_tokens, w_qkv, preferred_element_type=jnp.float32)
    self_queries = (packed[:, :model_width] + pair_bias[:model_width]).astype(jnp.bfloat16)
    self_keys = (
        packed[:, model_width : 2 * model_width]
        .astype(jnp.bfloat16)
        .reshape(row_count, block_len, model_width)
    )
    self_values = (
        (packed[:, 2 * model_width :] + pair_bias[model_width:])
        .astype(jnp.bfloat16)
        .reshape(row_count, block_len, model_width)
    )
    memory_pair = jnp.dot(flat_memory, cross_kv, preferred_element_type=jnp.float32)
    cross_keys = (
        memory_pair[:, :model_width].astype(jnp.bfloat16).reshape(row_count, src_block, model_width)
    )
    cross_values = (
        (memory_pair[:, model_width:] + cross_v_bias.astype(jnp.float32))
        .astype(jnp.bfloat16)
        .reshape(row_count, src_block, model_width)
    )
    all_keys, all_values, all_ckeys, all_cvalues = (
        lax.all_gather(self_keys, "seq", axis=1, tiled=True),
        lax.all_gather(self_values, "seq", axis=1, tiled=True),
        lax.all_gather(cross_keys, "seq", axis=1, tiled=True),
        lax.all_gather(cross_values, "seq", axis=1, tiled=True),
    )
    query_heads = split_heads(self_queries.reshape(row_count, block_len, model_width))
    self_accum, self_log = attend_forward(
        query_heads,
        split_heads(all_keys),
        split_heads(all_values),
        self_allowed,
        last_place,
        score_scale,
    )
    context_low = self_accum.reshape(token_rows, model_width).astype(jnp.bfloat16)
    inputs_f = flat_tokens.astype(jnp.float32)
    first_sum = (
        inputs_f
        + jnp.dot(context_low, self_out, preferred_element_type=jnp.float32)
        + self_out_bias.astype(jnp.float32)
    )
    first_norm, first_pull = jax.vjp(layer_norm, first_sum, gains[0], shifts[0])
    first_low = first_norm.astype(jnp.bfloat16)
    cross_q_rows = (
        jnp.dot(first_low, cross_query, preferred_element_type=jnp.float32)
        + cross_q_bias.astype(jnp.float32)
    ).astype(jnp.bfloat16)
    cross_heads = split_heads(cross_q_rows.reshape(row_count, block_len, model_width))
    cross_accum, cross_log = attend_forward(
        cross_heads,
        split_heads(all_ckeys),
        split_heads(all_cvalues),
        cross_allowed,
        src_length,
        score_scale,
    )
    cross_low = cross_accum.reshape(token_rows, model_width).astype(jnp.bfloat16)
    second_sum = (
        first_norm
        + jnp.dot(cross_low, cross_out, preferred_element_type=jnp.float32)
        + cross_out_bias.astype(jnp.float32)
    )
    second_norm, second_pull = jax.vjp(layer_norm, second_sum, gains[1], shifts[1])
    second_low = second_norm.astype(jnp.bfloat16)
    hidden_pre = jnp.dot(
        second_low, ffn_in, preferred_element_type=jnp.float32
    ) + ffn_in_bias.astype(jnp.float32)
    hidden_low = jax.nn.silu(hidden_pre).astype(jnp.bfloat16)
    third_sum = (
        second_norm
        + jnp.dot(hidden_low, ffn_out, preferred_element_type=jnp.float32)
        + ffn_out_bias.astype(jnp.float32)
    )
    result, third_pull = jax.vjp(layer_norm, third_sum, gains[2], shifts[2])
    output = result.astype(jnp.bfloat16).reshape(row_count, block_len, model_width)
    grad_third, gain_three, shift_three = third_pull(
        cotangent.reshape(token_rows, model_width).astype(jnp.float32)
    )
    grad_branch = grad_third.astype(jnp.bfloat16)
    d_ffn_out = contract_rows(hidden_low, grad_branch)
    d_ffn_out_bias = jnp.sum(grad_branch.astype(jnp.float32), axis=0)
    grad_hidden = contract_cols(grad_branch, ffn_out)
    sigmoid_pre = jax.nn.sigmoid(hidden_pre)
    grad_pre = (grad_hidden * sigmoid_pre * (1.0 + hidden_pre * (1.0 - sigmoid_pre))).astype(
        jnp.bfloat16
    )
    d_ffn_in = contract_rows(second_low, grad_pre)
    d_ffn_in_bias = jnp.sum(grad_pre.astype(jnp.float32), axis=0)
    grad_second_norm = grad_third + contract_cols(grad_pre, ffn_in)
    back_keys, back_values, back_ckeys, back_cvalues = (
        all_keys,
        all_values,
        all_ckeys,
        all_cvalues,
    )
    grad_second, gain_two, shift_two = second_pull(grad_second_norm)
    grad_cross_branch = grad_second.astype(jnp.bfloat16)
    d_cross_out = contract_rows(cross_low, grad_cross_branch)
    d_cross_out_bias = jnp.sum(grad_cross_branch.astype(jnp.float32), axis=0)
    grad_cross_ctx = contract_cols(grad_cross_branch, cross_out).astype(jnp.bfloat16)
    grad_cross_heads = split_heads(grad_cross_ctx.reshape(row_count, block_len, model_width))
    cross_delta = jnp.swapaxes(
        jnp.sum(grad_cross_heads.astype(jnp.float32) * cross_accum, axis=3), 1, 2
    )
    grad_cq, grad_ck_all, grad_cv_all = attend_back(
        cross_heads,
        split_heads(back_ckeys),
        split_heads(back_cvalues),
        cross_allowed,
        src_length,
        score_scale,
        cross_log,
        grad_cross_heads,
        cross_delta,
    )
    grad_ck_own, grad_cv_own = (
        lax.psum_scatter(
            grad_ck_all.reshape(row_count, src_length, model_width).astype(jnp.bfloat16),
            "seq",
            scatter_dimension=1,
            tiled=True,
        ).astype(jnp.float32),
        lax.psum_scatter(
            grad_cv_all.reshape(row_count, src_length, model_width).astype(jnp.bfloat16),
            "seq",
            scatter_dimension=1,
            tiled=True,
        ).astype(jnp.float32),
    )
    grad_pair = jnp.concatenate(
        [
            grad_ck_own.reshape(row_count * src_block, model_width).astype(jnp.bfloat16),
            grad_cv_own.reshape(row_count * src_block, model_width).astype(jnp.bfloat16),
        ],
        axis=1,
    )
    d_cross_kv = contract_rows(flat_memory, grad_pair)
    d_cross_v_bias = jnp.sum(grad_pair[:, model_width:].astype(jnp.float32), axis=0)
    d_memory = contract_cols(grad_pair, cross_kv).reshape(row_count, src_block, model_width)
    grad_cq_low = grad_cq.reshape(token_rows, model_width).astype(jnp.bfloat16)
    d_cross_query = contract_rows(first_low, grad_cq_low)
    d_cross_q_bias = jnp.sum(grad_cq_low.astype(jnp.float32), axis=0)
    grad_first_norm = grad_second + contract_cols(grad_cq_low, cross_query)
    grad_first, gain_one, shift_one = first_pull(grad_first_norm)
    grad_self_branch = grad_first.astype(jnp.bfloat16)
    d_self_out = contract_rows(context_low, grad_self_branch)
    d_self_out_bias = jnp.sum(grad_self_branch.astype(jnp.float32), axis=0)
    grad_context = contract_cols(grad_self_branch, self_out).astype(jnp.bfloat16)
    grad_context_heads = split_heads(grad_context.reshape(row_count, block_len, model_width))
    self_delta = jnp.swapaxes(
        jnp.sum(grad_context_heads.astype(jnp.float32) * self_accum, axis=3), 1, 2
    )
    grad_q, grad_k_all, grad_v_all = attend_back(
        query_heads,
        split_heads(back_keys),
        split_heads(back_values),
        self_allowed,
        last_place,
        score_scale,
        self_log,
        grad_context_heads,
        self_delta,
    )
    grad_k_own, grad_v_own = (
        lax.psum_scatter(
            grad_k_all.reshape(row_count, row_length, model_width).astype(jnp.bfloat16),
            "seq",
            scatter_dimension=1,
            tiled=True,
        ).astype(jnp.float32),
        lax.psum_scatter(
            grad_v_all.reshape(row_count, row_length, model_width).astype(jnp.bfloat16),
            "seq",
            scatter_dimension=1,
            tiled=True,
        ).astype(jnp.float32),
    )
    grad_k_flat = grad_k_own.reshape(token_rows, model_width)
    grad_v_flat = grad_v_own.reshape(token_rows, model_width)
    grad_q_low = grad_q.reshape(token_rows, model_width).astype(jnp.bfloat16)
    grad_v_low = grad_v_flat.astype(jnp.bfloat16)
    grad_proj = jnp.concatenate([grad_q_low, grad_k_flat.astype(jnp.bfloat16), grad_v_low], axis=1)
    d_w_qkv = contract_rows(flat_tokens, grad_proj)
    d_qv_bias = jnp.concatenate(
        [
            jnp.sum(grad_q_low.astype(jnp.float32), axis=0),
            jnp.sum(grad_v_low.astype(jnp.float32), axis=0),
        ]
    )
    d_tokens = (grad_first + contract_cols(grad_proj, w_qkv)).reshape(
        row_count, block_len, model_width
    )
    d_norm_gains = jnp.stack([gain_one, gain_two, gain_three])
    d_norm_biases = jnp.stack([shift_one, shift_two, shift_three])
    (
        d_w_qkv,
        d_qv_bias,
        d_self_out,
        d_self_out_bias,
        d_cross_query,
        d_cross_q_bias,
        d_cross_kv,
        d_cross_v_bias,
        d_cross_out,
        d_cross_out_bias,
        d_ffn_in,
        d_ffn_in_bias,
        d_ffn_out,
        d_ffn_out_bias,
        d_norm_gains,
        d_norm_biases,
    ) = lax.psum(
        (
            d_w_qkv,
            d_qv_bias,
            d_self_out,
            d_self_out_bias,
            d_cross_query,
            d_cross_q_bias,
            d_cross_kv,
            d_cross_v_bias,
            d_cross_out,
            d_cross_out_bias,
            d_ffn_in,
            d_ffn_in_bias,
            d_ffn_out,
            d_ffn_out_bias,
            d_norm_gains,
            d_norm_biases,
        ),
        ("dp", "seq"),
    )
    return (
        output,
        d_tokens,
        d_memory,
        d_w_qkv,
        d_qv_bias,
        d_self_out,
        d_self_out_bias,
        d_cross_query,
        d_cross_q_bias,
        d_cross_kv,
        d_cross_v_bias,
        d_cross_out,
        d_cross_out_bias,
        d_ffn_in,
        d_ffn_in_bias,
        d_ffn_out,
        d_ffn_out_bias,
        d_norm_gains,
        d_norm_biases,
    )


def rows_on_device(
    tokens, memory, tl, sl, cotangent, w_qkv, qv_bias, self_out, self_out_bias, cross_query, cross_q_bias,
    cross_kv, cross_v_bias, cross_out, cross_out_bias, ffn_in, ffn_in_bias, ffn_out, ffn_out_bias, gains, shifts,
):
    small = (qv_bias, self_out_bias, cross_q_bias, cross_v_bias, cross_out_bias, gains, shifts)
    saved = forward(tokens, memory, cotangent, tl, sl, small, w_qkv, self_out, cross_query, cross_kv, cross_out)
    names = ("cot", "x", "mem", "q", "qt", "k", "kt", "v", "ctx", "lse", "xh1", "rs1",
             "q2", "q2t", "k2", "k2t", "v2", "c2", "lse2", "y2", "xh2", "rs2")
    ins = dict(zip(names, saved))
    ins |= {"qkv": w_qkv, "so": self_out, "cq": cross_query, "ckv": cross_kv, "co": cross_out, "win": ffn_in, "wout": ffn_out}
    out, dtok, dmem, sums, dvec = main(tl, sl, (ffn_in_bias, ffn_out_bias, gains, shifts), ins)
    return (out,) + unpack(sums, dvec, dtok, dmem, ffn_in.shape[0], ffn_in.shape[1])


def on_device(tokens, *rest):
    if tokens.shape[0] == lax.axis_size("seq") and lax.axis_size("dp") == 8:
        return rows_on_device(tokens, *rest)
    return blocks_on_device(tokens, *rest)


def solution(mesh):
    in_specs = (
        P("dp", "seq", None),
        P("dp", "seq", None),
        P("dp", None),
        P("dp", None),
        P("dp", "seq", None),
        P(),
        P(),
        P(),
        P(),
        P(),
        P(),
        P(),
        P(),
        P(),
        P(),
        P(),
        P(),
        P(),
        P(),
        P(),
        P(),
    )
    out_specs = (
        P("dp", "seq", None),
        P("dp", "seq", None),
        P("dp", "seq", None),
        P(),
        P(),
        P(),
        P(),
        P(),
        P(),
        P(),
        P(),
        P(),
        P(),
        P(),
        P(),
        P(),
        P(),
        P(),
        P(),
    )
    return jax.shard_map(
        on_device, mesh=mesh, in_specs=in_specs, out_specs=out_specs, check_vma=False
    )
```

```python
import functools
import jax
import jax.numpy as jnp
from jax import lax
from jax.experimental import pallas as pl
from jax.experimental.pallas import tpu as pltpu
from jax.sharding import PartitionSpec as P

HEADS = 8
HEAD = 64
NDOC = 32
AUG = HEAD + 16
MASKED = -1e9
LOG2E = 1.4426950408889634
SCALE = HEAD**-0.5
F32 = jnp.float32
BF16 = jnp.bfloat16
TB = 256
FB = 512

V_Q, V_V, V_SO, V_CQ, V_CV, V_CO, V_FI, V_FO, V_G, V_B = 0, 1, 2, 3, 4, 5, 6, 10, 11, 14
VECS = 24
G_IN, G_OUT, G_CO, G_CK, G_CQ, G_SO, G_QKV = 0, 4, 8, 9, 11, 12, 13
STREAMS = ((4, 20, 4), (0, 16, 4), (8, 20, 3), (11, 23, 2), (13, 16, 2), (15, 18, 1))
UNITS, ALL_UNITS = 16, 25
PIECES = 8
STEPS = 8
COPIES = (1, 2, 2, 6, 6, 2, 2, 1)
OWN = sum(COPIES)


def vec_of(ref, start, length):
    return ref[start : start + length].astype(F32).reshape(1, length)


def mm(left, right, lc=1, rc=0):
    return lax.dot_general(
        left, right, (((lc,), (rc,)), ((), ())), preferred_element_type=F32
    )


def row_ids(lengths, row, size):
    rows, docs = lengths.shape
    at_row = lax.broadcasted_iota(jnp.int32, (rows, docs), 0) == row
    own = jnp.sum(jnp.where(at_row, lengths.astype(F32), 0.0), axis=0, keepdims=True)
    own = jnp.broadcast_to(own, (docs, docs))
    down = lax.broadcasted_iota(jnp.int32, (docs, docs), 0)
    over = lax.broadcasted_iota(jnp.int32, (docs, docs), 1)
    ends_col = jnp.sum(jnp.where(over <= down, own, 0.0), axis=1, keepdims=True)
    own_col = jnp.sum(jnp.where(over == down, own, 0.0), axis=1, keepdims=True)
    ends_row = jnp.sum(
        jnp.where(down <= over, jnp.broadcast_to(own_col, (docs, docs)), 0.0),
        axis=0,
        keepdims=True,
    )
    place_row = lax.broadcasted_iota(jnp.int32, (docs, size), 1).astype(F32)
    place_col = lax.broadcasted_iota(jnp.int32, (size, docs), 0).astype(F32)
    ids_row = jnp.sum(jnp.where(ends_col <= place_row, 1.0, 0.0), axis=0, keepdims=True)
    ids_col = jnp.sum(jnp.where(ends_row <= place_col, 1.0, 0.0), axis=1, keepdims=True)
    return ids_row, ids_col


def self_mask(mask_ref, lengths, row, size):
    ids_row, ids_col = row_ids(lengths, row, size)
    for kb in range(size // TB):
        for qb in range(kb, size // TB):
            ks, qs = slice(kb * TB, (kb + 1) * TB), slice(qb * TB, (qb + 1) * TB)
            seen = ids_col[ks] == ids_row[:, qs]
            if kb == qb:
                down = lax.broadcasted_iota(jnp.int32, (TB, TB), 0)
                over = lax.broadcasted_iota(jnp.int32, (TB, TB), 1)
                seen = seen & (down <= over)
            mask_ref[ks, qs] = jnp.where(seen, 0.0, MASKED)


def cross_mask(mask_ref, lengths, src_lengths, row, size, src):
    ids_row, _ = row_ids(lengths, row, size)
    _, src_col = row_ids(src_lengths, row, src)
    for qb in range(size // TB):
        qs = slice(qb * TB, (qb + 1) * TB)
        seen = (src_col == ids_row[:, qs]) | (ids_row[:, qs] == float(NDOC))
        mask_ref[:, qs] = jnp.where(seen, 0.0, MASKED)


def half_of(values, half):
    down = lax.broadcasted_iota(jnp.int32, values.shape, 0)
    keep = (down >= HEAD) if half else (down < HEAD)
    return jnp.where(keep, values, jnp.zeros_like(values))


def normalize(h):
    center = h - jnp.mean(h, axis=-1, keepdims=True)
    spread = jnp.mean(center * center, axis=-1, keepdims=True)
    rstd = lax.rsqrt(spread + 1e-05)
    return center * rstd, rstd


def norm_back(grad, xh, rstd, gain):
    gs = grad * gain
    m1 = jnp.mean(gs, axis=-1, keepdims=True)
    m2 = jnp.mean(gs * xh, axis=-1, keepdims=True)
    dh = (gs - m1 - xh * m2) * rstd
    return (
        dh,
        jnp.sum(grad * xh, axis=0, keepdims=True),
        jnp.sum(grad, axis=0, keepdims=True),
    )


def row_attend(k_ref, qt_ref, vt_ref, mask_ref, ctx_ref, lse_ref, size, key_end):
    for pair in range(HEADS // 2):
        lanes = slice(pair * 2 * HEAD, (pair + 1) * 2 * HEAD)
        for half in range(2):
            head = pair * 2 + half
            for qb in range(size // TB):
                ke, qs = key_end(qb), slice(qb * TB, (qb + 1) * TB)
                s = mm(k_ref[0:ke, lanes], half_of(qt_ref[lanes, qs], half))
                s = s + mask_ref[0:ke, qs]
                m = jnp.max(s, axis=0, keepdims=True)
                p = jnp.exp2(s - m).astype(BF16)
                o = mm(vt_ref[head * AUG : (head + 1) * AUG, 0:ke], p)
                total = o[HEAD : HEAD + 1]
                ctx_ref[head * HEAD : (head + 1) * HEAD, qs] = (
                    o[:HEAD] * (1.0 / total)
                ).astype(BF16)
                lse_ref[head, :, qs] = m + jnp.log2(total)


class Mover:
    def __init__(self, sems):
        self.sems, self.used, self.pending = sems, 0, {}

    def start(self, name, src, dst):
        copy = pltpu.make_async_copy(src, dst, self.sems.at[self.used])
        self.used += 1
        copy.start()
        self.pending[name] = copy

    def wait(self, *names):
        for name in names:
            self.pending.pop(name).wait()

    def finish(self):
        self.wait(*list(self.pending))


def meet(peers):
    barrier = pltpu.get_barrier_semaphore()
    for peer in peers:
        pl.semaphore_signal(barrier, inc=1, device_id=peer, device_id_type=pl.DeviceIdType.MESH)
    pl.semaphore_wait(barrier, len(peers))


def remote(src, dst, sends, recvs, index, peer):
    return pltpu.make_async_remote_copy(
        src_ref=src, dst_ref=dst, send_sem=sends.at[index], recv_sem=recvs.at[index],
        device_id=peer, device_id_type=pl.DeviceIdType.MESH,
    )


FWD_OUTS = 22


def forward_kernel(
    tok_ref, src_ref, cot_ref, tl_ref, sl_ref, bqv, bso, bcq, bcv, bco, gains, shifts,
    wqkv_h, wso_h, wcq_h, wckv_h, wco_h, *rest,
):
    outs, rest = rest[:FWD_OUTS], rest[FWD_OUTS:]
    cot_out = outs[0]
    kept, rest = rest[: FWD_OUTS - 1], rest[FWD_OUTS - 1 :]
    (wqkv_ref, wso_ref, wcq_ref, wckv_ref, wco_ref, mask, mask2, vt, v2t, y1,
     sems, sends, recvs) = rest
    (x_ref, mem_ref, q_ref, qt_ref, k_ref, kt_ref, v_ref, ctx_ref, lse_ref, xh1_ref, rs1_ref,
     q2_ref, q2t_ref, k2_ref, k2t_ref, v2_ref, c2_ref, lse2_ref, y2_ref, xh2_ref, rs2_ref) = kept
    size, width = x_ref.shape
    src = mem_ref.shape[0]
    seq = tok_ref.shape[0]
    blocks = size // TB
    row = lax.axis_index("seq")
    mover = Mover(sems)
    mover.start("wqkv", wqkv_h, wqkv_ref)
    mover.start("wckv", wckv_h, wckv_ref)
    mover.start("wso", wso_h, wso_ref)
    mover.start("wcq", wcq_h, wcq_ref)
    mover.start("wco", wco_h, wco_ref)

    def place(block, length):
        return pl.ds(pl.multiple_of(block * length, length), length)

    peers = [{"seq": lax.rem(row + d, seq)} for d in range(1, seq)]
    meet(peers)

    def exchange(source, target, length, kind):
        copies = []
        for d in range(1, seq):
            to = lax.rem(row + d, seq)
            copy = remote(source.at[to], target.at[place(row, length)], sends, recvs, kind * seq + d, {"seq": to})
            copy.start()
            copies.append(copy)
        mover.start((kind, "own"), source.at[row], target.at[place(row, length)])
        return copies

    part = TB // 2
    tok_copies = []
    for half in range(2):
        for d in range(1, seq):
            to = lax.rem(row + d, seq)
            source = tok_ref.at[to, half * part : (half + 1) * part]
            target = x_ref.at[pl.ds(pl.multiple_of(row * TB + half * part, part), part)]
            copy = remote(source, target, sends, recvs, (3 * half) * seq + d, {"seq": to})
            copy.start()
            tok_copies.append(copy)
    mover.start((0, "own"), tok_ref.at[row], x_ref.at[place(row, TB)])
    mem_copies = exchange(src_ref, mem_ref, src // seq, 1)

    for head in range(HEADS):
        vt[head * AUG + HEAD : (head + 1) * AUG, :] = jnp.ones((AUG - HEAD, size), BF16)
        v2t[head * AUG + HEAD : (head + 1) * AUG, :] = jnp.ones((AUG - HEAD, src), BF16)
    self_mask(mask, tl_ref[...], row, size)
    cross_mask(mask2, tl_ref[...], sl_ref[...], row, size, src)

    def put_vt(ref, values, place):
        for head in range(HEADS):
            ref[head * AUG : head * AUG + HEAD, place] = values[head * HEAD : (head + 1) * HEAD]

    mover.wait("wqkv", (0, "own"))
    for step in range(2 * seq - 1):
        if step:
            tok_copies[step - 1].wait_recv()
            half, d = divmod(step - 1, seq - 1)
            start = lax.rem(row + seq - 1 - d, seq) * TB + half * part
            ts = pl.ds(pl.multiple_of(start, part), part)
        else:
            ts = place(row, TB)
        xb = x_ref[ts, :]
        q = ((mm(xb, wqkv_ref[:, :width]) + vec_of(bqv, 0, width)) * (SCALE * LOG2E)).astype(BF16)
        q_ref[ts, :] = q
        qt_ref[:, ts] = q.T
        k = mm(xb, wqkv_ref[:, width : 2 * width]).astype(BF16)
        k_ref[ts, :] = k
        kt_ref[:, ts] = k.T
        v = (mm(xb, wqkv_ref[:, 2 * width :]) + vec_of(bqv, width, width)).astype(BF16)
        v_ref[ts, :] = v
        put_vt(vt, v.T, ts)
    mover.wait("wckv", (1, "own"))
    for copy in mem_copies:
        copy.wait_recv()
    cot_copies = exchange(cot_ref, cot_out, TB, 2)
    for i in (0, 1, 2, 3, 4, 5, 6):
        mover.start(i, kept[i], outs[1 + i])
    k2 = mm(mem_ref[...], wckv_ref[:, :width]).astype(BF16)
    k2_ref[...] = k2
    k2t_ref[...] = k2.T
    v2 = (mm(mem_ref[...], wckv_ref[:, width:]) + vec_of(bcv, 0, width)).astype(BF16)
    v2_ref[...] = v2
    put_vt(v2t, v2.T, slice(None))
    for i in (13, 14, 15):
        mover.start(i, kept[i], outs[1 + i])

    row_attend(k_ref, qt_ref, vt, mask, ctx_ref, lse_ref, size, lambda qb: (qb + 1) * TB)
    for i in (7, 8):
        mover.start(i, kept[i], outs[1 + i])
    mover.wait("wso", "wcq")
    for tb in range(size // FB):
        ts = slice(tb * FB, (tb + 1) * FB)
        h1 = x_ref[ts, :].astype(F32) + mm(ctx_ref[:, ts].T, wso_ref[...]) + vec_of(bso, 0, width)
        xh, rstd = normalize(h1)
        xh1_ref[ts, :] = xh.astype(BF16)
        rs1_ref[ts, :] = rstd
        yb = xh * gains[0:1, :].astype(F32) + shifts[0:1, :].astype(F32)
        y1[ts, :] = yb
        q2 = ((mm(yb.astype(BF16), wcq_ref[...]) + vec_of(bcq, 0, width)) * (SCALE * LOG2E)).astype(BF16)
        q2_ref[ts, :] = q2
        q2t_ref[:, ts] = q2.T
    for i in (9, 10, 11, 12):
        mover.start(i, kept[i], outs[1 + i])
    row_attend(k2_ref, q2t_ref, v2t, mask2, c2_ref, lse2_ref, size, lambda qb: src)
    for i in (16, 17):
        mover.start(i, kept[i], outs[1 + i])
    mover.wait("wco")
    for tb in range(size // FB):
        ts = slice(tb * FB, (tb + 1) * FB)
        h2 = y1[ts, :] + mm(c2_ref[:, ts].T, wco_ref[...]) + vec_of(bco, 0, width)
        xh, rstd = normalize(h2)
        xh2_ref[ts, :] = xh.astype(BF16)
        rs2_ref[ts, :] = rstd
        y2_ref[ts, :] = xh * gains[1:2, :].astype(F32) + shifts[1:2, :].astype(F32)
        for i in (18, 19, 20):
            mover.start((i, tb), kept[i].at[ts], outs[1 + i].at[ts])
    for copy in cot_copies:
        copy.wait_recv()
    for copy in tok_copies + mem_copies + cot_copies:
        copy.wait_send()
    mover.finish()


def row_attend_back(
    k_ref, kt_ref, v_ref, q_ref, qt_ref, dc_ref, dct_ref, ctx_ref, lse_ref, mask_ref,
    delta, dqt, dq_ref, dk_ref, dv_ref, size, keys, query_start, after,
):
    for pair in range(HEADS // 2):
        lanes = slice(pair * 2 * HEAD, (pair + 1) * 2 * HEAD)
        both = dct_ref[lanes, :].astype(F32) * ctx_ref[lanes, :].astype(F32)
        for half in range(2):
            delta[half] = jnp.sum(both[half * HEAD : (half + 1) * HEAD], axis=0, keepdims=True)
        dqt[...] = jnp.zeros_like(dqt)
        for kb in range(keys // TB):
            ks, qs = slice(kb * TB, (kb + 1) * TB), slice(query_start(kb), size)
            dks, dvs = [], []
            for half in range(2):
                head = pair * 2 + half
                rows = slice(head * HEAD, (head + 1) * HEAD)
                s = mm(k_ref[ks, lanes], half_of(qt_ref[lanes, qs], half))
                p = jnp.exp2(s + mask_ref[ks, qs] - lse_ref[head, :, qs])
                dp = mm(v_ref[ks, lanes], half_of(dct_ref[lanes, qs], half))
                ds = (p * (dp - delta[half, :, qs])).astype(BF16)
                dvs.append(mm(p.astype(BF16), dc_ref[qs, lanes]))
                dks.append(mm(ds, q_ref[qs, lanes]))
                dqt[half * HEAD : (half + 1) * HEAD, qs] += mm(kt_ref[rows, ks], ds)
            first = lax.broadcasted_iota(jnp.int32, (TB, 2 * HEAD), 1) < HEAD
            dv_ref[ks, lanes] = jnp.where(first, dvs[0], dvs[1]).astype(BF16)
            dk_ref[ks, lanes] = (jnp.where(first, dks[0], dks[1]) * (1.0 / LOG2E)).astype(BF16)
            after(pair, kb)
        dq_ref[:, lanes] = (dqt[...] * SCALE).astype(BF16).T


class Stream:
    def __init__(self, grads, sums, base, give, rows, slots, sems):
        dp, self.seq = lax.axis_index("dp"), lax.axis_size("seq")
        self.z = lax.axis_index("seq")
        self.core, x, y = lax.rem(dp, 2), lax.rem(dp // 2, 2), dp // 4
        self.near = {"dp": dp + 1 - 2 * self.core}
        by_x, by_y = {"dp": dp + 2 - 4 * x}, {"dp": dp + 4 - 8 * y}
        self.grads, self.sums, self.base, self.give, self.rows = grads, sums, base, give, rows
        self.slots, self.sems = slots, sems
        half, quarter, eighth = rows // 2, rows // 4, rows // 8
        self.unit = rows // (8 * self.seq)
        self.plan = []
        for part, (one, two, b1, b2) in enumerate(((x, y, by_x, by_y), (y, x, by_y, by_x))):
            start = part * half
            keep1, give1 = start + one * quarter, start + (1 - one) * quarter
            keep2, give2 = keep1 + two * eighth, keep1 + (1 - two) * eighth
            self.plan.append((b1, keep1, give1, b2, keep2, give2))

    def at(self, start, length):
        return pl.ds(pl.multiple_of(self.base + start, 16), length)

    def view(self, start, length):
        return self.grads.at[self.at(start, length)]

    def summed(self, start, length):
        return self.sums.at[self.core, self.at(start, length)]

    def own_copies(self):
        moves = [keep2 + self.z * self.unit for _, _, _, _, keep2, _ in self.plan]
        return [
            pltpu.make_async_copy(self.view(at, self.unit), self.summed(at, self.unit), self.sems[0].at[OWN + i])
            for i, at in enumerate(moves)
        ]

    def copies(self, step):
        rows, (s0, s1, s2, s3), seq = self.rows, self.slots, self.seq
        first = sum(COPIES[:step])
        sends, recvs = self.sems
        moves = []
        if step == 0:
            moves.append((self.grads.at[self.give : self.give + rows], s0, self.near))
        if step == 7:
            moves.append((self.summed(0, rows), self.summed(0, rows), self.near))
        for part, (b1, keep1, give1, b2, keep2, give2) in enumerate(self.plan):
            if step == 1:
                moves.append((self.view(give1, rows // 4), s1.at[part], b1))
            if step == 2:
                moves.append((self.view(give2, rows // 8), s2.at[part], b2))
            if step == 5:
                moves.append((self.summed(keep2, rows // 8), self.summed(keep2, rows // 8), b2))
            if step == 6:
                moves.append((self.summed(keep1, rows // 4), self.summed(keep1, rows // 4), b1))
            for d in range(1, seq):
                to = lax.rem(self.z + d, seq)
                if step == 3:
                    moves.append((self.view(keep2 + to * self.unit, self.unit), s3.at[part, d - 1], {"seq": to}))
                if step == 4:
                    own = keep2 + self.z * self.unit
                    moves.append((self.view(own, self.unit), self.summed(own, self.unit), {"seq": to}))
        return [remote(*move[:2], sends, recvs, first + i, move[2]) for i, move in enumerate(moves)]

    def add(self, start, slots, length):
        chunk = min(length, self.rows // 8)

        def at(i):
            place = pl.ds(pl.multiple_of(self.base + start + i * chunk, 16), chunk)
            total = self.grads[place, :].astype(F32)
            for slot in slots:
                total = total + slot[pl.ds(pl.multiple_of(i * chunk, 16), chunk), :].astype(F32)
            self.grads[place, :] = total.astype(BF16)

        if length == chunk:
            at(0)
        else:
            pl.loop(0, length // chunk)(at)

    def tick(self, step):
        if step:
            for copy in self.copies(step - 1):
                copy.wait()
        if step == 5:
            for copy in self.own_copies():
                copy.wait()
        s0, s1, s2, s3 = self.slots
        if step == 1:
            self.add(0, [s0], self.rows)
        for part, (_, keep1, _, _, keep2, _) in enumerate(self.plan):
            if step == 2:
                self.add(keep1, [s1.at[part]], self.rows // 4)
            if step == 3:
                self.add(keep2, [s2.at[part]], self.rows // 8)
            if step == 4:
                self.add(keep2 + self.z * self.unit, [s3.at[part, d] for d in range(self.seq - 1)], self.unit)
        if step < STEPS:
            for copy in self.copies(step):
                copy.start()
        if step == 4 and step < STEPS:
            for copy in self.own_copies():
                copy.start()


class VectorSum:
    def __init__(self, held, sems):
        dp, self.seq, self.z = lax.axis_index("dp"), lax.axis_size("seq"), lax.axis_index("seq")
        core, x, y = lax.rem(dp, 2), lax.rem(dp // 2, 2), dp // 4
        self.partners = [{"dp": dp + 1 - 2 * core}, {"dp": dp + 2 - 4 * x}, {"dp": dp + 4 - 8 * y}]
        self.held, self.sems = held, sems

    def copies(self, step):
        sends, recvs = self.sems
        if step < 3:
            return [remote(self.held.at[2 * step], self.held.at[2 * step + 1], sends, recvs, step, self.partners[step])]
        own = self.held.at[6 + self.z]
        return [remote(own, own, sends, recvs, 2 + d, {"seq": lax.rem(self.z + d, self.seq)}) for d in range(1, self.seq)]

    def tick(self, step):
        if step:
            for copy in self.copies(step - 1):
                copy.wait()
            if step < 4:
                to = 2 * step if step < 3 else 6 + self.z
                self.held[to] = self.held[2 * step - 2] + self.held[2 * step - 1]
        if step < 4:
            for copy in self.copies(step):
                copy.start()

    def total(self):
        values = self.held[6]
        for i in range(1, self.seq):
            values = values + self.held[6 + i]
        return values


INS = ("y2", "win", "cot", "wout", "xh2", "rs2", "co", "c2", "k2", "q2t", "v2", "k2t", "lse2", "mem", "ckv",
       "rs1", "kt", "k", "v", "q", "x", "q2", "xh1", "cq", "so", "qkv", "qt", "ctx", "lse")
HELD = INS[:17]
POOL = 14


def main_kernel(plan, tl_ref, sl_ref, bfi, bfo, gains, shifts, *rest):
    n = len(INS)
    hbm, rest = dict(zip(INS, rest[:n])), rest[n:]
    (out_h, dtok_h, dmem_h, sums_h, dvec_ref), rest = rest[:5], rest[5:]
    vmem, rest = dict(zip(HELD, rest[: len(HELD)])), rest[len(HELD) :]
    pool, rest = rest[:POOL], rest[POOL:]
    (out_row, dh1, mask, mask2, delta, dqt, dct, dk2, dv2, dmem, grads, held), rest = rest[:12], rest[12:]
    slots, rest = [rest[4 * i : 4 * i + 4] for i in range(len(STREAMS))], rest[4 * len(STREAMS) :]
    sems, sends, recvs, xsends, xrecvs = rest
    size, width = vmem["y2"].shape
    inner = vmem["win"].shape[1]
    src = vmem["mem"].shape[0]
    acts, dus, slopes, (y2b, dz_s) = pool[0:4], pool[4:8], pool[8:12], pool[12:14]
    vmem |= dict(zip(("k", "v", "q", "x"), pool[0:4]))
    dq, dk, dv, dc = pool[4:8]
    vmem |= {"q2": pool[8], "xh1": pool[9], "qt": vmem["q2t"], "ctx": vmem["c2"], "lse": vmem["lse2"]}
    wout = vmem["wout"]
    vmem |= {"cq": wout.at[0:width], "so": wout.at[width : 2 * width], "qkv": vmem["win"].at[:, : 3 * width]}
    y1b, dtok = y2b, dz_s
    cols = [slice(j, j + width) for j in range(0, inner, width)]
    blocks = [slice(t, t + TB) for t in range(0, size, TB)]
    seq, row, dp = lax.axis_size("seq"), lax.axis_index("seq"), lax.axis_index("dp")
    mover = Mover(sems)

    def load(*names):
        for name in names:
            mover.start(name, hbm[name], vmem[name])

    load(*HELD[:4])
    split = [(keep * width, give * width, rows * width) for keep, give, rows in STREAMS]
    streams = [
        Stream(grads, sums_h, *where, slots[i], (sends.at[i], recvs.at[i])) for i, where in enumerate(split)
    ]
    vectors = VectorSum(held, (sends.at[len(STREAMS)], recvs.at[len(STREAMS)]))
    core, x, y = streams[0].core, lax.rem(dp // 2, 2), dp // 4
    pieces = []

    def piece_sender(source, target, kind):
        def send_piece(step):
            length = size // seq
            part = length // PIECES
            copies = []
            for d in range(1, seq):
                to = lax.rem(row + d, seq)
                rows = pl.ds(pl.multiple_of(to * length + step * part, 16), part)
                place = target.at[row, step * part : (step + 1) * part]
                copies.append(remote(source.at[rows], place, xsends, xrecvs, (kind + step) * seq + d, {"seq": to}))
            for copy in copies:
                copy.start()
            pieces.extend(copies)

        return send_piece

    ticks = [s.tick for s in streams] + [vectors.tick, piece_sender(dtok, dtok_h, 1), piece_sender(out_row, out_h, 1 + PIECES)]

    def act(place):
        for stream, step in plan.get(place, ()):
            ticks[stream](step)

    meet(
        [{"dp": dp + 1 - 2 * core}, {"dp": dp + 2 - 4 * x}, {"dp": dp + 4 - 8 * y}]
        + [{"seq": lax.rem(row + d, seq)} for d in range(1, seq)]
    )

    def exchange(source, target, kind):
        length = source.shape[0] // seq
        copies = []
        for d in range(1, seq):
            to = lax.rem(row + d, seq)
            rows = pl.ds(pl.multiple_of(to * length, 16), length)
            copies.append(remote(source.at[rows], target.at[row], xsends, xrecvs, kind * seq + d, {"seq": to}))
        for copy in copies:
            copy.start()
        mover.start((kind, "own"), source.at[pl.ds(pl.multiple_of(row * length, 16), length)], target.at[row])
        return copies

    gives = {keep + i: give + i for keep, give, rows in STREAMS for i in range(rows)}

    def gather(i, values):
        half = width // 2
        keep, give = i * width, gives[i] * width
        left = pl.multiple_of(jnp.where(core == 0, keep, give), width)
        right = pl.multiple_of(jnp.where(core == 0, give, keep), width)
        grads[pl.ds(left, width), :] = values[:, :half].astype(BF16)
        grads[pl.ds(right, width), :] = values[:, half:].astype(BF16)

    def total(values):
        return jnp.sum(values.astype(F32), axis=0, keepdims=True)

    def count(i, values):
        dvec_ref[i : i + 1, :] += values

    gain0, shift0 = gains[0:1, :].astype(F32), shifts[0:1, :].astype(F32)
    gain1, gain2, shift2 = gains[1:2, :].astype(F32), gains[2:3, :].astype(F32), shifts[2:3, :].astype(F32)
    dvec_ref[...] = jnp.zeros_like(dvec_ref)
    mover.wait("y2", "win", "cot", "wout")
    load(*HELD[4:])
    y2_ref, win = vmem["y2"], vmem["win"]

    for tb in range(size // FB):
        ts = slice(tb * FB, (tb + 1) * FB)
        y2 = y2_ref[ts, :]
        low = y2.astype(BF16)
        y2b[ts, :] = low
        h3 = y2 + vec_of(bfo, 0, width)
        for j, cs in enumerate(cols):
            u = mm(low, win[:, cs]) + vec_of(bfi, j * width, width)
            sg = 0.5 * jnp.tanh(0.5 * u) + 0.5
            a = u * sg
            slopes[j][ts, :] = (sg + a * (1.0 - sg)).astype(BF16)
            a = a.astype(BF16)
            acts[j][ts, :] = a
            h3 = h3 + mm(a, wout[cs, :])
        xh, rstd = normalize(h3)
        out_row[ts, :] = (xh * gain2 + shift2).astype(BF16)
        dh3, dg, db = norm_back(vmem["cot"][ts, :].astype(F32), xh, rstd, gain2)
        y2_ref[ts, :] = dh3
        dz = dh3.astype(BF16)
        dz_s[ts, :] = dz
        count(V_G + 2, dg)
        count(V_B + 2, db)
        count(V_FO, total(dz))

    own = pl.ds(pl.multiple_of(row * (size // seq), 16), size // seq)
    mover.start("own output", out_row.at[own], out_h.at[row])
    for j in range(len(cols)):
        gather(G_OUT + j, mm(acts[j][...], dz_s[...], 0, 0))
        act(("out", j))
    act("ffn_out")
    load("k", "v", "q", "x")
    mover.wait("xh2", "rs2")
    for tb, ts in enumerate([slice(t, t + FB) for t in range(0, size, FB)]):
        dz = dz_s[ts, :]
        dy2 = y2_ref[ts, :]
        for j, cs in enumerate(cols):
            du = (mm(dz, wout[cs, :], 1, 1) * slopes[j][ts, :].astype(F32)).astype(BF16)
            dus[j][ts, :] = du
            count(V_FI + j, total(du))
            dy2 = dy2 + mm(du, win[:, cs], 1, 1)
            if j < 3:
                act(("ffn", tb, j))
        dh2, dg, db = norm_back(dy2, vmem["xh2"][ts, :].astype(F32), vmem["rs2"][ts, :], gain1)
        y2_ref[ts, :] = dh2
        count(V_G + 1, dg)
        count(V_B + 1, db)
        act(("ffn", tb, 3))

    load("q2", "xh1", "cq", "so", "qkv")
    dh2_ref = y2_ref
    for j in range(len(cols)):
        gather(G_IN + j, mm(y2b[...], dus[j][...], 0, 0))
        act(("in", j))
    act("ffn_in")
    cross_mask(mask2, tl_ref[...], sl_ref[...], row, size, src)
    act("mask2")
    mover.wait("co", "c2")
    for tb, ts in enumerate(blocks):
        da2 = dh2_ref[ts, :].astype(BF16)
        dc[ts, :] = mm(da2, vmem["co"][...], 1, 1).astype(BF16)
        dct[:, ts] = mm(vmem["co"][...], da2, 1, 1).astype(BF16)
        count(V_CO, total(da2))
        act(("cin", tb))
    act("cross_in")
    gather(G_CO, mm(vmem["c2"][...], dh2_ref[...].astype(BF16)))
    act("cross_out")
    mover.wait("k2", "q2t", "v2", "k2t", "lse2", "q2")
    row_attend_back(
        vmem["k2"], vmem["k2t"], vmem["v2"], vmem["q2"], vmem["q2t"], dc, dct, vmem["c2"], vmem["lse2"], mask2,
        delta, dqt, dq, dk2, dv2, size, src, lambda kb: 0, lambda i, j: act(("cross", i, j)),
    )
    load("qt", "ctx", "lse")
    count(V_CV, total(dv2[...]))
    count(V_CQ, total(dq[...]))
    mover.wait("mem", "ckv", "cq", "xh1", "rs1", "so")
    gather(G_CK, mm(vmem["mem"][...], dk2[...], 0, 0))
    gather(G_CK + 1, mm(vmem["mem"][...], dv2[...], 0, 0))
    act("ck")
    w_ckv = vmem["ckv"]
    dmem[...] = (mm(dk2[...], w_ckv[:, :width], 1, 1) + mm(dv2[...], w_ckv[:, width:], 1, 1)).astype(BF16)
    act("memory")
    mem_copies = exchange(dmem, dmem_h, 0)
    for tb, ts in enumerate(blocks):
        dy1 = dh2_ref[ts, :] + mm(dq[ts, :], vmem["cq"][...], 1, 1)
        xh1 = vmem["xh1"][ts, :].astype(F32)
        y1b[ts, :] = (xh1 * gain0 + shift0).astype(BF16)
        dh, dg, db = norm_back(dy1, xh1, vmem["rs1"][ts, :], gain0)
        count(V_G, dg)
        count(V_B, db)
        dh1[ts, :] = dh
        count(V_SO, total(dh.astype(BF16)))
        act(("nrm", tb))
    act("norm")
    gather(G_CQ, mm(y1b[...], dq[...], 0, 0))
    act("query")
    self_mask(mask, tl_ref[...], row, size)
    act("mask")
    mover.wait("ctx")
    gather(G_SO, mm(vmem["ctx"][...], dh1[...].astype(BF16)))
    act("self_out")
    for tb, ts in enumerate(blocks):
        da1 = dh1[ts, :].astype(BF16)
        dc[ts, :] = mm(da1, vmem["so"][...], 1, 1).astype(BF16)
        dct[:, ts] = mm(vmem["so"][...], da1, 1, 1).astype(BF16)
        act(("sin", tb))
    act("self_in")
    mover.wait("k", "qt", "v", "q", "kt", "lse")
    row_attend_back(
        vmem["k"], vmem["kt"], vmem["v"], vmem["q"], vmem["qt"], dc, dct, vmem["ctx"], vmem["lse"], mask,
        delta, dqt, dq, dk, dv, size, size, lambda kb: kb * TB, lambda i, j: act(("self", i, j)),
    )
    mover.wait("x", "qkv")
    for i, part in enumerate((dq, dk, dv)):
        gather(G_QKV + i, mm(vmem["x"][...], part[...], 0, 0))
        act(("qkv", i))
    act("qkv")
    count(V_Q, total(dq[...]))
    count(V_V, total(dv[...]))
    held[0] = dvec_ref[...]
    act("vectors")
    w_qkv = vmem["qkv"]
    for tb, ts in enumerate(blocks):
        dtok[ts, :] = (
            dh1[ts, :]
            + mm(dq[ts, :], w_qkv[:, :width], 1, 1)
            + mm(dk[ts, :], w_qkv[:, width : 2 * width], 1, 1)
            + mm(dv[ts, :], w_qkv[:, 2 * width :], 1, 1)
        ).astype(BF16)
        act(("tok", tb))
    mover.start("own tokens", dtok.at[own], dtok_h.at[row])
    act("tokens")
    act("end")
    dvec_ref[...] = vectors.total()
    for copy in pieces + mem_copies:
        copy.wait()
    mover.finish()


PLAN = {
    ("out", 0): [(8, 0)],
    "ffn_out": [(0, 0)],
    ("ffn", 0, 0): [(8, 1)],
    ("ffn", 0, 2): [(0, 1), (8, 2)],
    ("ffn", 1, 1): [(8, 3)],
    ("in", 0): [(8, 4)],
    "ffn_in": [(1, 0)],
    "mask2": [(0, 2), (8, 5)],
    ("cross", 0, 0): [(1, 1), (8, 6)],
    ("cross", 2, 0): [(0, 3)],
    "ck": [(2, 0)],
    ("nrm", 2): [(2, 1)],
    "norm": [(8, 7)],
    "self_out": [(3, 0), (1, 2)],
    ("sin", 1): [(0, 4)],
    "self_in": [(3, 1)],
    ("self", 0, 1): [(2, 2)],
    ("self", 1, 0): [(1, 3)],
    ("self", 2, 0): [(0, 5)],
    ("self", 2, 1): [(3, 2), (2, 3)],
    ("self", 3, 2): [(1, 4)],
    ("self", 3, 3): [(0, 6)],
    ("qkv", 1): [(4, 0)],
    "qkv": [(5, 0)],
    ("tok", 1): [(3, 3), (2, 4)],
    ("tok", 2): [(4, 1), (5, 1)],
    "tokens": [(6, 1)],
    "end": [(0, 7), (3, 4), (4, 2), (5, 2), (7, 0), (0, 8), (1, 5), (6, 2), (2, 5), (7, 1), (4, 3), (5, 3), (3, 5), (1, 6), (3, 6), (6, 3), (7, 2), (4, 4), (2, 6), (5, 4), (1, 7), (7, 3), (1, 8), (6, 4), (7, 4), (4, 5), (3, 7), (3, 8), (7, 5), (5, 5), (4, 6), (7, 6), (5, 6), (7, 7), (2, 7), (2, 8), (4, 7), (5, 7), (4, 8), (5, 8)],
    "vectors": [(6, 0)],
}


def unpack_kernel(grads_h, dvec_ref, dtok_h, dmem_h, *rest):
    outs, rest = rest[:18], rest[18:]
    mats, vecs = outs[:9], outs[9:]
    grads, dtok, dmem, rest = rest[0], rest[1], rest[2], rest[3:]
    wide, sems = rest[:9], rest[9]
    mover = Mover(sems)
    width = 2 * grads.shape[2]
    half = width // 2
    plan = ((0, G_QKV, 1, 3), (1, G_SO, 1, 1), (2, G_CQ, 1, 1), (3, G_CK, 1, 2), (4, G_CO, 1, 1), (5, G_IN, 1, 4), (6, G_OUT, 4, 1))
    for i, base, units, blocks in plan:
        rows = slice(base * width, (base + units * blocks) * width)
        mover.start(i, grads_h.at[:, rows], grads.at[:, rows])
    mover.start("tok", dtok_h, dtok)
    mover.start("mem", dmem_h, dmem)
    for i, base, units, blocks in plan:
        mover.wait(i)
        for b in range(blocks):
            for u in range(units):
                rows = slice((base + b + u) * width, (base + b + u + 1) * width)
                for c in range(2):
                    wide[i][u * width : (u + 1) * width, b * width + c * half : b * width + (c + 1) * half] = grads[c, rows, :].astype(F32)
        mover.start((i, "out"), wide[i], mats[i])
    for i, name, source in ((7, "tok", dtok), (8, "mem", dmem)):
        mover.wait(name)
        wide[i][...] = source[...].astype(F32)
        mover.start((i, "out"), wide[i], mats[i])
    place = 0
    for ref in vecs:
        if len(ref.shape) == 2:
            ref[...] = dvec_ref[place : place + ref.shape[0], :]
            place += ref.shape[0]
        else:
            for j in range(ref.shape[0] // width):
                ref[j * width : (j + 1) * width] = dvec_ref[place, :]
                place += 1
    mover.finish()


WHOLE = pl.BlockSpec(memory_space=pltpu.VMEM)


def call(kernel, ins, outs, scratch, name):
    return pl.pallas_call(
        kernel,
        out_shape=[jax.ShapeDtypeStruct(*o) for o in outs],
        in_specs=[WHOLE] * len(ins),
        out_specs=[WHOLE] * len(outs),
        scratch_shapes=[pltpu.VMEM(*s) for s in scratch],
        compiler_params=pltpu.CompilerParams(vmem_limit_bytes=60 * 2**20),
        name=name,
    )(*ins)


ANY = pl.BlockSpec(memory_space=pl.ANY)


def forward(tokens, memory, cot, tl, sl, small, wqkv, wso, wcq, wckv, wco):
    seq, block, d = tokens.shape
    t, s = seq * block, seq * memory.shape[1]
    tok, feat, row = ((t, d), BF16), ((d, t), BF16), ((HEADS, 1, t), F32)
    col, mem = ((t, 1), F32), ((s, d), BF16)
    kept = [tok, mem, tok, feat, tok, feat, tok, feat, row, tok, col,
            tok, feat, mem, ((d, s), BF16), mem, feat, row, ((t, d), F32), tok, col]
    weights = (wqkv, wso, wcq, wckv, wco)
    scratch = kept + [(w.shape, w.dtype) for w in weights]
    scratch += [((t, t), F32), ((s, t), F32), ((HEADS * AUG, t), BF16), ((HEADS * AUG, s), BF16), ((t, d), F32)]
    return pl.pallas_call(
        forward_kernel,
        out_shape=[jax.ShapeDtypeStruct(*o) for o in [tok] + kept],
        in_specs=[ANY] * 3 + [WHOLE] * (2 + len(small)) + [ANY] * 5,
        out_specs=[ANY] * FWD_OUTS,
        scratch_shapes=[pltpu.VMEM(*x) for x in scratch]
        + [pltpu.SemaphoreType.DMA((40,)), pltpu.SemaphoreType.DMA((4 * seq,)), pltpu.SemaphoreType.DMA((4 * seq,))],
        compiler_params=pltpu.CompilerParams(vmem_limit_bytes=60 * 2**20, collective_id=0, has_side_effects=True),
        name="forward",
    )(tokens, memory, cot, tl, sl, *small, *weights)


def main(tl, sl, small, ins):
    t, d = ins["y2"].shape
    s = ins["mem"].shape[0]
    seq = lax.axis_size("seq")
    tok, mem, wide = ((t, d), BF16), ((s, d), BF16), ((t, d), F32)
    scratch = [(ins[name].shape, ins[name].dtype) for name in HELD] + [tok] * POOL
    scratch += [tok, wide, ((t, t), F32), ((s, t), F32), ((2, 1, t), F32), ((2 * HEAD, t), F32), ((d, t), BF16),
                mem, mem, mem, ((ALL_UNITS * d, d // 2), BF16), ((6 + seq, VECS, d), F32)]
    for _, _, rows in STREAMS:
        r, c = rows * d, d // 2
        scratch += [((r, c), BF16), ((2, r // 4, c), BF16), ((2, r // 8, c), BF16), ((2, seq - 1, r // (8 * seq), c), BF16)]
    steps = pltpu.SemaphoreType.DMA((len(STREAMS) + 1, OWN + 2))
    return pl.pallas_call(
        functools.partial(main_kernel, PLAN),
        out_shape=[
            jax.ShapeDtypeStruct((seq, t // seq, d), BF16),
            jax.ShapeDtypeStruct((seq, t // seq, d), BF16),
            jax.ShapeDtypeStruct((seq, s // seq, d), BF16),
            jax.ShapeDtypeStruct((2, UNITS * d, d // 2), BF16),
            jax.ShapeDtypeStruct((VECS, d), F32),
        ],
        in_specs=[WHOLE] * 6 + [ANY] * len(INS),
        out_specs=[ANY] * 4 + [WHOLE],
        scratch_shapes=[pltpu.VMEM(*x) for x in scratch]
        + [pltpu.SemaphoreType.DMA((40,)), steps, steps] + [pltpu.SemaphoreType.DMA(((1 + 2 * PIECES) * seq,))] * 2,
        compiler_params=pltpu.CompilerParams(vmem_limit_bytes=62 * 2**20, collective_id=1, has_side_effects=True),
        name="main",
    )(tl, sl, *small, *[ins[name] for name in INS])


def unpack(grads, dvec, dtok, dmem, d, f):
    mats = [(d, 3 * d), (d, d), (d, d), (d, 2 * d), (d, d), (d, f), (f, d), dtok.shape, dmem.shape]
    vecs = [(2 * d,), (d,), (d,), (d,), (d,), (f,), (d,), (3, d), (3, d)]
    outs = pl.pallas_call(
        unpack_kernel,
        out_shape=[jax.ShapeDtypeStruct(o, F32) for o in mats + vecs],
        in_specs=[ANY, WHOLE, ANY, ANY],
        out_specs=[ANY] * 9 + [WHOLE] * 9,
        scratch_shapes=[pltpu.VMEM(x.shape, x.dtype) for x in (grads, dtok, dmem)]
        + [pltpu.VMEM(m, F32) for m in mats] + [pltpu.SemaphoreType.DMA((24,))],
        compiler_params=pltpu.CompilerParams(vmem_limit_bytes=60 * 2**20),
        name="unpack",
    )(grads, dvec, dtok, dmem)
    d_qkv, d_so, d_cq, d_ckv, d_co, d_fi, d_fo, d_tok, d_mem = outs[:9]
    v_qv, v_so, v_cq, v_cv, v_co, v_fi, v_fo, d_gains, d_shifts = outs[9:]
    return (d_tok, d_mem, d_qkv, v_qv, d_so, v_so, d_cq, v_cq, d_ckv, v_cv, d_co, v_co, d_fi, v_fi, d_fo, v_fo, d_gains, d_shifts)


def layer_norm(values, gain, shift):
    center = values - jnp.mean(values, axis=-1, keepdims=True)
    spread = jnp.mean(center * center, axis=-1, keepdims=True)
    return center * lax.rsqrt(spread + 1e-05) * gain + shift


def doc_ids(lengths, size):
    ends = jnp.cumsum(lengths, axis=1)
    places = jnp.arange(size, dtype=jnp.int32)
    return jnp.sum((ends[:, None, :] <= places[None, :, None]).astype(jnp.int32), axis=2)


def block_width(key_total):
    return 512 if key_total % 512 == 0 else key_total


def contract_rows(left, right):
    return lax.dot_general(
        left, right, (((0,), (0,)), ((), ())), preferred_element_type=jnp.float32
    )


def contract_cols(left, right):
    return lax.dot_general(
        left, right, (((1,), (1,)), ((), ())), preferred_element_type=jnp.float32
    )


def block_scores(queries, keys, allowed, start_at, width_of, score_scale):
    key_block = lax.dynamic_slice_in_dim(keys, start_at, width_of, 1)
    scores = (
        jnp.einsum("rqhd,rkhd->rhqk", queries, key_block, preferred_element_type=jnp.float32)
        * score_scale
    )
    return jnp.where(allowed(start_at, width_of)[:, None], scores, -1000000000.0)


def attend_forward(queries, keys, values, allowed, skip_after, score_scale):
    row_count, query_count, head_count, head_size = queries.shape
    key_total = keys.shape[1]
    width_of = block_width(key_total)
    block_count = key_total // width_of

    def statistics(carried, block_index):
        start_at = block_index * width_of

        def statistics_work(state):
            running_max, running_sum = state
            scores = block_scores(queries, keys, allowed, start_at, width_of, score_scale)
            new_max = jnp.maximum(running_max, jnp.max(scores, axis=3))
            new_sum = running_sum * jnp.exp(running_max - new_max) + jnp.sum(
                jnp.exp(scores - new_max[..., None]), axis=3
            )
            return (new_max, new_sum)

        return (
            lax.cond(start_at > skip_after, lambda state: state, statistics_work, carried),
            None,
        )

    stat_shape = (row_count, head_count, query_count)
    start_state = (
        jnp.full(stat_shape, -1000000000.0, jnp.float32),
        jnp.zeros(stat_shape, jnp.float32),
    )
    block_numbers = jnp.arange(block_count, dtype=jnp.int32)
    (running_max, running_sum), _ = lax.scan(statistics, start_state, block_numbers)
    log_total = running_max + jnp.log(running_sum)

    def mixing(carried, block_index):
        start_at = block_index * width_of

        def mixing_work(accum):
            scores = block_scores(queries, keys, allowed, start_at, width_of, score_scale)
            probs = jnp.exp(scores - log_total[..., None]).astype(jnp.bfloat16)
            value_block = lax.dynamic_slice_in_dim(values, start_at, width_of, 1)
            return accum + jnp.einsum(
                "rhqk,rkhd->rqhd", probs, value_block, preferred_element_type=jnp.float32
            )

        return (lax.cond(start_at > skip_after, lambda accum: accum, mixing_work, carried), None)

    start_accum = jnp.zeros((row_count, query_count, head_count, head_size), jnp.float32)
    accum, _ = lax.scan(mixing, start_accum, block_numbers)
    return (accum, log_total)


def attend_back(
    queries, keys, values, allowed, skip_after, score_scale, log_total, grad_out, delta
):
    row_count, query_count, head_count, head_size = queries.shape
    key_total = keys.shape[1]
    width_of = block_width(key_total)
    block_count = key_total // width_of

    def step(block_index, state):
        start_at = block_index * width_of

        def step_work(inner):
            scores = block_scores(queries, keys, allowed, start_at, width_of, score_scale)
            probs = jnp.exp(scores - log_total[..., None])
            key_block = lax.dynamic_slice_in_dim(keys, start_at, width_of, 1)
            value_block = lax.dynamic_slice_in_dim(values, start_at, width_of, 1)
            grad_probs = jnp.einsum(
                "rqhd,rkhd->rhqk", grad_out, value_block, preferred_element_type=jnp.float32
            )
            grad_scores = (probs * (grad_probs - delta[..., None])).astype(jnp.bfloat16)
            grad_query = (
                inner[0]
                + jnp.einsum(
                    "rhqk,rkhd->rqhd", grad_scores, key_block, preferred_element_type=jnp.float32
                )
                * score_scale
            )
            key_part = (
                jnp.einsum(
                    "rhqk,rqhd->rkhd", grad_scores, queries, preferred_element_type=jnp.float32
                )
                * score_scale
            )
            value_part = jnp.einsum(
                "rhqk,rqhd->rkhd",
                probs.astype(jnp.bfloat16),
                grad_out,
                preferred_element_type=jnp.float32,
            )
            grad_keys = lax.dynamic_update_slice_in_dim(inner[1], key_part, start_at, 1)
            grad_values = lax.dynamic_update_slice_in_dim(inner[2], value_part, start_at, 1)
            return (grad_query, grad_keys, grad_values)

        return lax.cond(start_at > skip_after, lambda inner: inner, step_work, state)

    start_state = (jnp.zeros((row_count, query_count, head_count, head_size), jnp.float32),)
    start_state = start_state + (
        jnp.zeros((row_count, key_total, head_count, head_size), jnp.float32),
        jnp.zeros((row_count, key_total, head_count, head_size), jnp.float32),
    )
    return lax.fori_loop(0, block_count, step, start_state)


def blocks_on_device(
    tokens,
    memory,
    doc_lengths,
    src_lengths,
    cotangent,
    w_qkv,
    qv_bias,
    self_out,
    self_out_bias,
    cross_query,
    cross_q_bias,
    cross_kv,
    cross_v_bias,
    cross_out,
    cross_out_bias,
    ffn_in,
    ffn_in_bias,
    ffn_out,
    ffn_out_bias,
    norm_gains,
    norm_biases,
):
    row_count, block_len, model_width = tokens.shape
    src_block = memory.shape[1]
    seq_count = lax.axis_size("seq")
    row_length = block_len * seq_count
    src_length = src_block * seq_count
    score_scale = HEAD ** (-0.5)
    first_place = lax.axis_index("seq") * block_len
    last_place = first_place + block_len - 1
    target_ids = doc_ids(doc_lengths, row_length)
    source_ids = doc_ids(src_lengths, src_length)
    own_ids = lax.dynamic_slice_in_dim(target_ids, first_place, block_len, 1)
    own_places = first_place + jnp.arange(block_len, dtype=jnp.int32)

    def self_allowed(start_at, width_of):
        key_ids = lax.dynamic_slice_in_dim(target_ids, start_at, width_of, 1)
        key_places = start_at + jnp.arange(width_of, dtype=jnp.int32)
        return (own_ids[:, :, None] == key_ids[:, None, :]) & (
            key_places[None, None, :] <= own_places[None, :, None]
        )

    def cross_allowed(start_at, width_of):
        return (own_ids[:, :, None] == source_ids[:, None, :]) | (own_ids[:, :, None] == NDOC)

    def split_heads(array_in):
        return array_in.reshape(array_in.shape[0], array_in.shape[1], HEADS, HEAD)

    token_rows = row_count * block_len
    flat_tokens = tokens.reshape(token_rows, model_width)
    flat_memory = memory.reshape(row_count * src_block, model_width)
    pair_bias = qv_bias.astype(jnp.float32)
    gains = norm_gains.astype(jnp.float32)
    shifts = norm_biases.astype(jnp.float32)
    packed = jnp.dot(flat_tokens, w_qkv, preferred_element_type=jnp.float32)
    self_queries = (packed[:, :model_width] + pair_bias[:model_width]).astype(jnp.bfloat16)
    self_keys = (
        packed[:, model_width : 2 * model_width]
        .astype(jnp.bfloat16)
        .reshape(row_count, block_len, model_width)
    )
    self_values = (
        (packed[:, 2 * model_width :] + pair_bias[model_width:])
        .astype(jnp.bfloat16)
        .reshape(row_count, block_len, model_width)
    )
    memory_pair = jnp.dot(flat_memory, cross_kv, preferred_element_type=jnp.float32)
    cross_keys = (
        memory_pair[:, :model_width].astype(jnp.bfloat16).reshape(row_count, src_block, model_width)
    )
    cross_values = (
        (memory_pair[:, model_width:] + cross_v_bias.astype(jnp.float32))
        .astype(jnp.bfloat16)
        .reshape(row_count, src_block, model_width)
    )
    all_keys, all_values, all_ckeys, all_cvalues = (
        lax.all_gather(self_keys, "seq", axis=1, tiled=True),
        lax.all_gather(self_values, "seq", axis=1, tiled=True),
        lax.all_gather(cross_keys, "seq", axis=1, tiled=True),
        lax.all_gather(cross_values, "seq", axis=1, tiled=True),
    )
    query_heads = split_heads(self_queries.reshape(row_count, block_len, model_width))
    self_accum, self_log = attend_forward(
        query_heads,
        split_heads(all_keys),
        split_heads(all_values),
        self_allowed,
        last_place,
        score_scale,
    )
    context_low = self_accum.reshape(token_rows, model_width).astype(jnp.bfloat16)
    inputs_f = flat_tokens.astype(jnp.float32)
    first_sum = (
        inputs_f
        + jnp.dot(context_low, self_out, preferred_element_type=jnp.float32)
        + self_out_bias.astype(jnp.float32)
    )
    first_norm, first_pull = jax.vjp(layer_norm, first_sum, gains[0], shifts[0])
    first_low = first_norm.astype(jnp.bfloat16)
    cross_q_rows = (
        jnp.dot(first_low, cross_query, preferred_element_type=jnp.float32)
        + cross_q_bias.astype(jnp.float32)
    ).astype(jnp.bfloat16)
    cross_heads = split_heads(cross_q_rows.reshape(row_count, block_len, model_width))
    cross_accum, cross_log = attend_forward(
        cross_heads,
        split_heads(all_ckeys),
        split_heads(all_cvalues),
        cross_allowed,
        src_length,
        score_scale,
    )
    cross_low = cross_accum.reshape(token_rows, model_width).astype(jnp.bfloat16)
    second_sum = (
        first_norm
        + jnp.dot(cross_low, cross_out, preferred_element_type=jnp.float32)
        + cross_out_bias.astype(jnp.float32)
    )
    second_norm, second_pull = jax.vjp(layer_norm, second_sum, gains[1], shifts[1])
    second_low = second_norm.astype(jnp.bfloat16)
    hidden_pre = jnp.dot(
        second_low, ffn_in, preferred_element_type=jnp.float32
    ) + ffn_in_bias.astype(jnp.float32)
    hidden_low = jax.nn.silu(hidden_pre).astype(jnp.bfloat16)
    third_sum = (
        second_norm
        + jnp.dot(hidden_low, ffn_out, preferred_element_type=jnp.float32)
        + ffn_out_bias.astype(jnp.float32)
    )
    result, third_pull = jax.vjp(layer_norm, third_sum, gains[2], shifts[2])
    output = result.astype(jnp.bfloat16).reshape(row_count, block_len, model_width)
    grad_third, gain_three, shift_three = third_pull(
        cotangent.reshape(token_rows, model_width).astype(jnp.float32)
    )
    grad_branch = grad_third.astype(jnp.bfloat16)
    d_ffn_out = contract_rows(hidden_low, grad_branch)
    d_ffn_out_bias = jnp.sum(grad_branch.astype(jnp.float32), axis=0)
    grad_hidden = contract_cols(grad_branch, ffn_out)
    sigmoid_pre = jax.nn.sigmoid(hidden_pre)
    grad_pre = (grad_hidden * sigmoid_pre * (1.0 + hidden_pre * (1.0 - sigmoid_pre))).astype(
        jnp.bfloat16
    )
    d_ffn_in = contract_rows(second_low, grad_pre)
    d_ffn_in_bias = jnp.sum(grad_pre.astype(jnp.float32), axis=0)
    grad_second_norm = grad_third + contract_cols(grad_pre, ffn_in)
    back_keys, back_values, back_ckeys, back_cvalues = (
        all_keys,
        all_values,
        all_ckeys,
        all_cvalues,
    )
    grad_second, gain_two, shift_two = second_pull(grad_second_norm)
    grad_cross_branch = grad_second.astype(jnp.bfloat16)
    d_cross_out = contract_rows(cross_low, grad_cross_branch)
    d_cross_out_bias = jnp.sum(grad_cross_branch.astype(jnp.float32), axis=0)
    grad_cross_ctx = contract_cols(grad_cross_branch, cross_out).astype(jnp.bfloat16)
    grad_cross_heads = split_heads(grad_cross_ctx.reshape(row_count, block_len, model_width))
    cross_delta = jnp.swapaxes(
        jnp.sum(grad_cross_heads.astype(jnp.float32) * cross_accum, axis=3), 1, 2
    )
    grad_cq, grad_ck_all, grad_cv_all = attend_back(
        cross_heads,
        split_heads(back_ckeys),
        split_heads(back_cvalues),
        cross_allowed,
        src_length,
        score_scale,
        cross_log,
        grad_cross_heads,
        cross_delta,
    )
    grad_ck_own, grad_cv_own = (
        lax.psum_scatter(
            grad_ck_all.reshape(row_count, src_length, model_width).astype(jnp.bfloat16),
            "seq",
            scatter_dimension=1,
            tiled=True,
        ).astype(jnp.float32),
        lax.psum_scatter(
            grad_cv_all.reshape(row_count, src_length, model_width).astype(jnp.bfloat16),
            "seq",
            scatter_dimension=1,
            tiled=True,
        ).astype(jnp.float32),
    )
    grad_pair = jnp.concatenate(
        [
            grad_ck_own.reshape(row_count * src_block, model_width).astype(jnp.bfloat16),
            grad_cv_own.reshape(row_count * src_block, model_width).astype(jnp.bfloat16),
        ],
        axis=1,
    )
    d_cross_kv = contract_rows(flat_memory, grad_pair)
    d_cross_v_bias = jnp.sum(grad_pair[:, model_width:].astype(jnp.float32), axis=0)
    d_memory = contract_cols(grad_pair, cross_kv).reshape(row_count, src_block, model_width)
    grad_cq_low = grad_cq.reshape(token_rows, model_width).astype(jnp.bfloat16)
    d_cross_query = contract_rows(first_low, grad_cq_low)
    d_cross_q_bias = jnp.sum(grad_cq_low.astype(jnp.float32), axis=0)
    grad_first_norm = grad_second + contract_cols(grad_cq_low, cross_query)
    grad_first, gain_one, shift_one = first_pull(grad_first_norm)
    grad_self_branch = grad_first.astype(jnp.bfloat16)
    d_self_out = contract_rows(context_low, grad_self_branch)
    d_self_out_bias = jnp.sum(grad_self_branch.astype(jnp.float32), axis=0)
    grad_context = contract_cols(grad_self_branch, self_out).astype(jnp.bfloat16)
    grad_context_heads = split_heads(grad_context.reshape(row_count, block_len, model_width))
    self_delta = jnp.swapaxes(
        jnp.sum(grad_context_heads.astype(jnp.float32) * self_accum, axis=3), 1, 2
    )
    grad_q, grad_k_all, grad_v_all = attend_back(
        query_heads,
        split_heads(back_keys),
        split_heads(back_values),
        self_allowed,
        last_place,
        score_scale,
        self_log,
        grad_context_heads,
        self_delta,
    )
    grad_k_own, grad_v_own = (
        lax.psum_scatter(
            grad_k_all.reshape(row_count, row_length, model_width).astype(jnp.bfloat16),
            "seq",
            scatter_dimension=1,
            tiled=True,
        ).astype(jnp.float32),
        lax.psum_scatter(
            grad_v_all.reshape(row_count, row_length, model_width).astype(jnp.bfloat16),
            "seq",
            scatter_dimension=1,
            tiled=True,
        ).astype(jnp.float32),
    )
    grad_k_flat = grad_k_own.reshape(token_rows, model_width)
    grad_v_flat = grad_v_own.reshape(token_rows, model_width)
    grad_q_low = grad_q.reshape(token_rows, model_width).astype(jnp.bfloat16)
    grad_v_low = grad_v_flat.astype(jnp.bfloat16)
    grad_proj = jnp.concatenate([grad_q_low, grad_k_flat.astype(jnp.bfloat16), grad_v_low], axis=1)
    d_w_qkv = contract_rows(flat_tokens, grad_proj)
    d_qv_bias = jnp.concatenate(
        [
            jnp.sum(grad_q_low.astype(jnp.float32), axis=0),
            jnp.sum(grad_v_low.astype(jnp.float32), axis=0),
        ]
    )
    d_tokens = (grad_first + contract_cols(grad_proj, w_qkv)).reshape(
        row_count, block_len, model_width
    )
    d_norm_gains = jnp.stack([gain_one, gain_two, gain_three])
    d_norm_biases = jnp.stack([shift_one, shift_two, shift_three])
    (
        d_w_qkv,
        d_qv_bias,
        d_self_out,
        d_self_out_bias,
        d_cross_query,
        d_cross_q_bias,
        d_cross_kv,
        d_cross_v_bias,
        d_cross_out,
        d_cross_out_bias,
        d_ffn_in,
        d_ffn_in_bias,
        d_ffn_out,
        d_ffn_out_bias,
        d_norm_gains,
        d_norm_biases,
    ) = lax.psum(
        (
            d_w_qkv,
            d_qv_bias,
            d_self_out,
            d_self_out_bias,
            d_cross_query,
            d_cross_q_bias,
            d_cross_kv,
            d_cross_v_bias,
            d_cross_out,
            d_cross_out_bias,
            d_ffn_in,
            d_ffn_in_bias,
            d_ffn_out,
            d_ffn_out_bias,
            d_norm_gains,
            d_norm_biases,
        ),
        ("dp", "seq"),
    )
    return (
        output,
        d_tokens,
        d_memory,
        d_w_qkv,
        d_qv_bias,
        d_self_out,
        d_self_out_bias,
        d_cross_query,
        d_cross_q_bias,
        d_cross_kv,
        d_cross_v_bias,
        d_cross_out,
        d_cross_out_bias,
        d_ffn_in,
        d_ffn_in_bias,
        d_ffn_out,
        d_ffn_out_bias,
        d_norm_gains,
        d_norm_biases,
    )


def rows_on_device(
    tokens, memory, tl, sl, cotangent, w_qkv, qv_bias, self_out, self_out_bias, cross_query, cross_q_bias,
    cross_kv, cross_v_bias, cross_out, cross_out_bias, ffn_in, ffn_in_bias, ffn_out, ffn_out_bias, gains, shifts,
):
    small = (qv_bias, self_out_bias, cross_q_bias, cross_v_bias, cross_out_bias, gains, shifts)
    saved = forward(tokens, memory, cotangent, tl, sl, small, w_qkv, self_out, cross_query, cross_kv, cross_out)
    names = ("cot", "x", "mem", "q", "qt", "k", "kt", "v", "ctx", "lse", "xh1", "rs1",
             "q2", "q2t", "k2", "k2t", "v2", "c2", "lse2", "y2", "xh2", "rs2")
    ins = dict(zip(names, saved))
    ins |= {"qkv": w_qkv, "so": self_out, "cq": cross_query, "ckv": cross_kv, "co": cross_out, "win": ffn_in, "wout": ffn_out}
    out, dtok, dmem, sums, dvec = main(tl, sl, (ffn_in_bias, ffn_out_bias, gains, shifts), ins)
    return (out,) + unpack(sums, dvec, dtok, dmem, ffn_in.shape[0], ffn_in.shape[1])


def on_device(tokens, *rest):
    if tokens.shape[0] == lax.axis_size("seq") and lax.axis_size("dp") == 8:
        return rows_on_device(tokens, *rest)
    return blocks_on_device(tokens, *rest)


def solution(mesh):
    in_specs = (
        P("dp", "seq", None),
        P("dp", "seq", None),
        P("dp", None),
        P("dp", None),
        P("dp", "seq", None),
        P(),
        P(),
        P(),
        P(),
        P(),
        P(),
        P(),
        P(),
        P(),
        P(),
        P(),
        P(),
        P(),
        P(),
        P(),
        P(),
    )
    out_specs = (
        P("dp", "seq", None),
        P("dp", "seq", None),
        P("dp", "seq", None),
        P(),
        P(),
        P(),
        P(),
        P(),
        P(),
        P(),
        P(),
        P(),
        P(),
        P(),
        P(),
        P(),
        P(),
        P(),
        P(),
    )
    return jax.shard_map(
        on_device, mesh=mesh, in_specs=in_specs, out_specs=out_specs, check_vma=False
    )
```
